32 devices in a mesh: groups: 2 (over y), ctx: 16 (over z, x, core).
Axes of the slice: x: 2, y: 2, z: 4, core: 2. Of those that a mesh axis runs over, the one named last changes fastest.
Arguments:
- queries: bfloat16 [8192, 4096], P(('groups', 'ctx')), parts along dimension 0, may hold values from -13 to 13
- all_key_states: bfloat16 [8192, 512], P(('groups', 'ctx')), parts along dimension 0, may hold values from -9.5 to 9.5
- all_value_states: bfloat16 [8192, 512], P(('groups', 'ctx')), parts along dimension 0, may hold values from -6 to 6
- selected: int32 [32, 2], P(('groups', 'ctx')), parts along dimension 0, may hold values from 0 to 14, as said below
Outputs:
- attended: bfloat16 [8192, 4096], P(('groups', 'ctx')), parts along dimension 0
The draws below stay inside these ranges and needn't reach their ends.
There are 2 independent parts, one for each index of `groups`. The reference program is written for one: setup_inputs(seed, part) draws one part's arguments, and reference() takes and returns one part's arrays. A program takes and returns all parts, laid end to end along the dimension named above; each array names one. Nothing has to cross between parts.
Inputs may be any that keep to these rules, and one draw needn't show every extreme that they name: `selected`: for block i >= 2 the two entries of row i are different blocks below i; rows 0 and 1 hold 0 and 0; the last block's first entry is 14.
All inputs are finite; a program needn't handle non-finite values.
Results may differ from the reference program's by a relative error of at most 0.004.
Values may be sent and summed in bfloat16 or wider, within the bound.
No kernel may reach another device: no remote copies, remote signals or barrier semaphores. Data moves between devices by JAX's collectives and lax.ppermute only.
A program may use at most 64 MiB of HBM per device.

```python
import math
import jax
import jax.numpy as jnp
from jax import lax

QUERY_HEADS = 32
KEY_VALUE_HEADS = 4
HEAD_SIZE = 128
BLOCK_TOKENS = 256
NBLK = 16
CONTEXT_TOKENS = 4096


def draw_queries(key, part):
    random_component = jnp.clip(jax.random.normal(jax.random.fold_in(key, 1), (CONTEXT_TOKENS, QUERY_HEADS, HEAD_SIZE), jnp.float32), -4.0, 4.0) * 1.5
    return random_component.reshape(CONTEXT_TOKENS, QUERY_HEADS * HEAD_SIZE).astype(jnp.bfloat16)


def draw_all_key_states(key, part):
    random_component = jnp.clip(jax.random.normal(jax.random.fold_in(key, 4), (CONTEXT_TOKENS, KEY_VALUE_HEADS, HEAD_SIZE), jnp.float32), -6.0, 6.0)
    return random_component.reshape(CONTEXT_TOKENS, KEY_VALUE_HEADS * HEAD_SIZE).astype(jnp.bfloat16)


def draw_selected(key, part):
    block_position = jnp.arange(NBLK, dtype=jnp.int32)
    first_pick = jax.random.randint(jax.random.fold_in(key, 11), (NBLK,), 0, jnp.maximum(block_position, 1))
    first_pick = jnp.where(block_position == NBLK - 1, block_position - 1, first_pick)
    second_pick = jax.random.randint(jax.random.fold_in(key, 12), (NBLK,), 0, jnp.maximum(block_position - 1, 1))
    second_pick = second_pick + (second_pick >= first_pick).astype(jnp.int32)
    second_pick = jnp.where(block_position >= 2, second_pick, 0)
    return jnp.stack([first_pick, second_pick], axis=1).astype(jnp.int32)


def shard_levels(key, extent, split, low, high):
    def one(dim, shards_of):
        draws = jax.random.uniform(jax.random.fold_in(jax.random.fold_in(key, 6), dim), (shards_of,), jnp.float32, low / len(split), high / len(split))
        return jnp.repeat(jnp.exp(draws), extent[dim] // shards_of).reshape((-1,) + (1,) * (len(extent) - dim - 1))

    factor_of = one(*split[0])
    for cut in split[1:]:
        factor_of = factor_of * one(*cut)
    return factor_of


def scatter_about(key, dims, width, bound, shards=(), kind=jnp.bfloat16):
    drawn = jax.random.normal(key, dims, jnp.float32) * width
    if len(shards) > 0:
        drawn = shard_levels(key, dims, shards, -0.22, 0.18) * drawn
    return jnp.clip(drawn, min=-bound, max=bound).astype(kind)


def setup_inputs(seed: int = 0, part: int = 0) -> dict:
    keys = jax.random.split(jax.random.key(seed), 5)
    part_splits = jax.random.split(jax.random.fold_in(keys[4], part), 5)
    queries = draw_queries(jax.random.fold_in(jax.random.fold_in(keys[4], part), 71), part)
    all_key_states = draw_all_key_states(jax.random.fold_in(jax.random.fold_in(keys[4], part), 71), part)
    all_value_states = scatter_about(part_splits[2], (CONTEXT_TOKENS, KEY_VALUE_HEADS * HEAD_SIZE), 1.0, 6.0, ((0, 16),))
    selected = draw_selected(jax.random.fold_in(jax.random.fold_in(keys[4], part), 71), part)
    return dict(queries=queries, all_key_states=all_key_states, all_value_states=all_value_states, selected=selected)


def reference(queries, all_key_states, all_value_states, selected):
    group_width = QUERY_HEADS // KEY_VALUE_HEADS
    score_scale = 1.0 / math.sqrt(HEAD_SIZE)
    row_ids = jnp.arange(BLOCK_TOKENS, dtype=jnp.int32)
    causal = row_ids[None, :] <= row_ids[:, None]

    def rows_for_block(source, block_number):
        return lax.dynamic_slice_in_dim(source, (block_number * BLOCK_TOKENS).astype(jnp.int32), BLOCK_TOKENS, 0)

    def one_block(block_position):
        first_block = selected[block_position, 0]
        second_block = selected[block_position, 1]
        first_valid = first_block < block_position
        second_valid = jnp.logical_and(second_block < block_position, second_block != first_block)
        query_row_block = rows_for_block(queries, block_position).astype(jnp.float32).reshape(BLOCK_TOKENS, KEY_VALUE_HEADS, group_width, HEAD_SIZE)
        key_row_block = jnp.concatenate([rows_for_block(all_key_states, block_position), rows_for_block(all_key_states, first_block), rows_for_block(all_key_states, second_block)], axis=0)
        value_row_block = jnp.concatenate([rows_for_block(all_value_states, block_position), rows_for_block(all_value_states, first_block), rows_for_block(all_value_states, second_block)], axis=0)
        key_row_block = key_row_block.astype(jnp.float32).reshape(3 * BLOCK_TOKENS, KEY_VALUE_HEADS, HEAD_SIZE)
        value_row_block = value_row_block.astype(jnp.float32).reshape(3 * BLOCK_TOKENS, KEY_VALUE_HEADS, HEAD_SIZE)
        allowed = jnp.concatenate([causal, jnp.broadcast_to(first_valid, (BLOCK_TOKENS, BLOCK_TOKENS)), jnp.broadcast_to(second_valid, (BLOCK_TOKENS, BLOCK_TOKENS))], axis=1)
        scores = jnp.einsum('tgrd,ugd->tgru', query_row_block, key_row_block) * score_scale
        scores = jnp.where(allowed[:, None, None, :], scores, jnp.float32(-1e+30))
        row_max = lax.optimization_barrier(jnp.max(scores, axis=3, keepdims=True))
        weights = jnp.exp(scores - row_max)
        row_sum = lax.optimization_barrier(jnp.sum(weights, axis=3, keepdims=True))
        rounded = lax.optimization_barrier(weights.astype(jnp.bfloat16)).astype(jnp.float32)
        mixture = jnp.einsum('tgru,ugd->tgrd', rounded, value_row_block)
        return (mixture / row_sum).astype(jnp.bfloat16).reshape(BLOCK_TOKENS, QUERY_HEADS * HEAD_SIZE)
    result = lax.map(one_block, jnp.arange(NBLK, dtype=jnp.int32))
    return result.reshape(CONTEXT_TOKENS, QUERY_HEADS * HEAD_SIZE)
```

```python
import functools
import math

import jax
import jax.numpy as jnp
from jax import lax
from jax.experimental import pallas as pl
from jax.experimental.pallas import tpu as pltpu
from jax.sharding import PartitionSpec as P

QUERY_HEADS = 32
KEY_VALUE_HEADS = 4
HEAD_SIZE = 128
GROUP = QUERY_HEADS // KEY_VALUE_HEADS
SLOTS = 2 * KEY_VALUE_HEADS
REQUEST_ROWS = 16
MIB = 1024 * 1024


def pack_kernel(selected_ref, key_ref, value_ref, out_ref):
    devices, piece_rows = out_ref.shape[0], key_ref.shape[0] // out_ref.shape[0]
    for slot in range(SLOTS):
        ref = key_ref if slot < KEY_VALUE_HEADS else value_ref
        head = slot % KEY_VALUE_HEADS
        part = ref[:, head * HEAD_SIZE : (head + 1) * HEAD_SIZE]
        out_ref[:, slot * piece_rows : (slot + 1) * piece_rows, :] = part.reshape(
            devices, piece_rows, HEAD_SIZE
        )
    lane = lax.broadcasted_iota(jnp.int32, (devices, REQUEST_ROWS, HEAD_SIZE), 2)
    request = jnp.where(lane == 0, selected_ref[0, 0], selected_ref[0, 1])
    out_ref[:, SLOTS * piece_rows :, :] = request.astype(jnp.float32).astype(jnp.bfloat16)


def pack(keys, values, selected, devices):
    rows = keys.shape[0]
    piece_rows = rows // devices
    shape = (devices, SLOTS * piece_rows + REQUEST_ROWS, HEAD_SIZE)
    if piece_rows % 16 == 0:
        return pl.pallas_call(
            pack_kernel,
            out_shape=jax.ShapeDtypeStruct(shape, jnp.bfloat16),
            in_specs=[
                pl.BlockSpec(memory_space=pltpu.SMEM),
                pl.BlockSpec(memory_space=pltpu.VMEM),
                pl.BlockSpec(memory_space=pltpu.VMEM),
            ],
            out_specs=pl.BlockSpec(memory_space=pltpu.VMEM),
            name="pack",
        )(selected, keys, values)
    both = jnp.concatenate([keys, values], axis=1)
    both = both.reshape(devices, piece_rows, SLOTS, HEAD_SIZE).transpose(0, 2, 1, 3)
    both = both.reshape(devices, SLOTS * piece_rows, HEAD_SIZE)
    lane = jnp.arange(HEAD_SIZE) == 0
    request = jnp.where(lane, selected[0, 0], selected[0, 1]).astype(jnp.bfloat16)
    request = jnp.broadcast_to(request, (devices, REQUEST_ROWS, HEAD_SIZE))
    return jnp.concatenate([both, request], axis=1)


def pick_kernel(wanted_ref, held_ref, out_ref):
    rows = out_ref.shape[2]

    @pl.loop(0, out_ref.shape[0])
    def _(device):
        for pick in range(2):
            out_ref[device, pick] = held_ref[wanted_ref[device, pick], :rows, :]


def pick_pieces(wanted, held):
    devices, rows = held.shape[0], held.shape[1] - REQUEST_ROWS
    return pl.pallas_call(
        pick_kernel,
        out_shape=jax.ShapeDtypeStruct((devices, 2, rows, HEAD_SIZE), jnp.bfloat16),
        in_specs=[
            pl.BlockSpec(memory_space=pltpu.SMEM),
            pl.BlockSpec(memory_space=pltpu.VMEM),
        ],
        out_specs=pl.BlockSpec(memory_space=pltpu.VMEM),
        compiler_params=pltpu.CompilerParams(vmem_limit_bytes=16 * MIB),
        name="pick_pieces",
    )(wanted, held)


NT = (((1,), (1,)), ((), ()))
NN = (((1,), (0,)), ((), ()))


def attention_kernel(
    flags_ref, query_ref, key_ref, value_ref, far_key_ref, far_value_ref, out_ref
):
    rows = query_ref.shape[0]
    half = rows // 2
    factor = math.log2(math.e) / math.sqrt(HEAD_SIZE)
    row = lax.broadcasted_iota(jnp.int32, (half, half), 0)
    column = lax.broadcasted_iota(jnp.int32, (half, half), 1)
    causal = column <= row

    def attend(picks):
        own_key, own_value = key_ref[...], value_ref[...]
        far = [
            (
                far_key_ref[:, pick, 0].reshape(rows, HEAD_SIZE),
                far_value_ref[:, pick, 0].reshape(rows, HEAD_SIZE),
            )
            for pick in picks
        ]
        for head in range(GROUP):
            lanes = slice(head * HEAD_SIZE, (head + 1) * HEAD_SIZE)
            for part in range(2):
                query = query_ref[part * half : (part + 1) * half, lanes]
                pieces = []
                for block in range(part + 1):
                    span = slice(block * half, (block + 1) * half)
                    scores = lax.dot_general(
                        query, own_key[span], NT, preferred_element_type=jnp.float32
                    )
                    if block == part:
                        scores = jnp.where(causal, scores, -1e30)
                    pieces.append((scores, own_value[span]))
                for far_key, far_value in far:
                    scores = lax.dot_general(
                        query, far_key, NT, preferred_element_type=jnp.float32
                    )
                    pieces.append((scores, far_value))
                row_max = functools.reduce(
                    jnp.maximum, [jnp.max(s, axis=1, keepdims=True) for s, _ in pieces]
                )
                shift = row_max * factor
                row_sum, mixture = 0.0, 0.0
                for scores, value in pieces:
                    weights = jnp.exp2(scores * factor - shift)
                    row_sum = row_sum + jnp.sum(weights, axis=1, keepdims=True)
                    mixture = mixture + lax.dot_general(
                        weights.astype(jnp.bfloat16), value, NN, preferred_element_type=jnp.float32
                    )
                out_ref[part * half : (part + 1) * half, lanes] = (
                    mixture / row_sum
                ).astype(out_ref.dtype)

    first, second = flags_ref[0], flags_ref[1]

    @pl.when(first + second == 2)
    def _():
        attend((0, 1))

    @pl.when(first + second == 1)
    def _():
        attend((second,))

    @pl.when(first + second == 0)
    def _():
        attend(())


def attention(flags, queries, keys, values, far):
    rows = queries.shape[0]
    holders, _, _, piece_rows, _ = far.shape
    width = GROUP * HEAD_SIZE
    far_shape = (holders, 2, 1, piece_rows, HEAD_SIZE)
    scores = QUERY_HEADS * rows * 3 * rows
    return pl.pallas_call(
        attention_kernel,
        out_shape=jax.ShapeDtypeStruct(queries.shape, jnp.bfloat16),
        grid=(KEY_VALUE_HEADS,),
        in_specs=[
            pl.BlockSpec(memory_space=pltpu.SMEM),
            pl.BlockSpec((rows, width), lambda g: (0, g)),
            pl.BlockSpec((rows, HEAD_SIZE), lambda g: (0, g)),
            pl.BlockSpec((rows, HEAD_SIZE), lambda g: (0, g)),
            pl.BlockSpec(far_shape, lambda g: (0, 0, g, 0, 0)),
            pl.BlockSpec(far_shape, lambda g: (0, 0, g + KEY_VALUE_HEADS, 0, 0)),
        ],
        out_specs=pl.BlockSpec((rows, width), lambda g: (0, g)),
        compiler_params=pltpu.CompilerParams(vmem_limit_bytes=40 * MIB),
        cost_estimate=pl.CostEstimate(
            flops=4 * scores * HEAD_SIZE, bytes_accessed=6 * MIB, transcendentals=scores
        ),
        name="attention",
    )(flags, queries, keys, values, far, far)


def local(queries, all_key_states, all_value_states, selected):
    devices = lax.axis_size("ctx")
    my_block = lax.axis_index("ctx")
    rows = all_key_states.shape[0]
    piece_rows = rows // devices
    packed = pack(all_key_states, all_value_states, selected, devices)
    held = lax.all_to_all(packed, "ctx", split_axis=0, concat_axis=0, tiled=True)
    wanted = held[:, SLOTS * piece_rows, :2].astype(jnp.int32)
    wanted = jnp.clip(wanted, 0, devices - 1)
    chosen = pick_pieces(wanted, held)
    far = lax.all_to_all(chosen, "ctx", split_axis=0, concat_axis=0, tiled=True)
    far = far.reshape(devices, 2, SLOTS, piece_rows, HEAD_SIZE)
    if piece_rows % 16 != 0:
        far = far.transpose(1, 2, 0, 3, 4).reshape(1, 2, SLOTS, rows, HEAD_SIZE)
    first, second = selected[0, 0], selected[0, 1]
    first_valid = first < my_block
    second_valid = jnp.logical_and(second < my_block, second != first)
    flags = jnp.stack([first_valid, second_valid]).astype(jnp.int32)
    return attention(flags, queries, all_key_states, all_value_states, far)


def solution(mesh):
    placed = P(("groups", "ctx"), None)
    return jax.shard_map(
        local, mesh=mesh, in_specs=(placed,) * 4, out_specs=placed, check_vma=False
    )
```

```python
import math

import jax
import jax.numpy as jnp
from jax import lax
from jax.experimental import pallas as pl
from jax.experimental.pallas import tpu as pltpu
from jax.sharding import PartitionSpec as P

QUERY_HEADS = 32
KEY_VALUE_HEADS = 4
HEAD_SIZE = 128
GROUP = QUERY_HEADS // KEY_VALUE_HEADS
SLOTS = 2 * KEY_VALUE_HEADS
REQUEST_ROWS = 16
MIB = 1024 * 1024


def pack_kernel(selected_ref, key_ref, value_ref, out_ref):
    devices, piece_rows = out_ref.shape[0], key_ref.shape[0] // out_ref.shape[0]
    for slot in range(SLOTS):
        ref = key_ref if slot < KEY_VALUE_HEADS else value_ref
        head = slot % KEY_VALUE_HEADS
        part = ref[:, head * HEAD_SIZE : (head + 1) * HEAD_SIZE]
        out_ref[:, slot * piece_rows : (slot + 1) * piece_rows, :] = part.reshape(
            devices, piece_rows, HEAD_SIZE
        )
    lane = lax.broadcasted_iota(jnp.int32, (devices, REQUEST_ROWS, HEAD_SIZE), 2)
    request = jnp.where(lane == 0, selected_ref[0, 0], selected_ref[0, 1])
    out_ref[:, SLOTS * piece_rows :, :] = request.astype(jnp.float32).astype(jnp.bfloat16)


def pack(keys, values, selected, devices):
    rows = keys.shape[0]
    piece_rows = rows // devices
    shape = (devices, SLOTS * piece_rows + REQUEST_ROWS, HEAD_SIZE)
    if piece_rows % 16 == 0:
        return pl.pallas_call(
            pack_kernel,
            out_shape=jax.ShapeDtypeStruct(shape, jnp.bfloat16),
            in_specs=[
                pl.BlockSpec(memory_space=pltpu.SMEM),
                pl.BlockSpec(memory_space=pltpu.VMEM),
                pl.BlockSpec(memory_space=pltpu.VMEM),
            ],
            out_specs=pl.BlockSpec(memory_space=pltpu.VMEM),
            name="pack",
        )(selected, keys, values)
    both = jnp.concatenate([keys, values], axis=1)
    both = both.reshape(devices, piece_rows, SLOTS, HEAD_SIZE).transpose(0, 2, 1, 3)
    both = both.reshape(devices, SLOTS * piece_rows, HEAD_SIZE)
    lane = jnp.arange(HEAD_SIZE) == 0
    request = jnp.where(lane, selected[0, 0], selected[0, 1]).astype(jnp.bfloat16)
    request = jnp.broadcast_to(request, (devices, REQUEST_ROWS, HEAD_SIZE))
    return jnp.concatenate([both, request], axis=1)


def pick_kernel(wanted_ref, held_ref, out_ref):
    rows = out_ref.shape[2]

    @pl.loop(0, out_ref.shape[0])
    def _(device):
        for pick in range(2):
            out_ref[device, pick] = held_ref[wanted_ref[device, pick], :rows, :]


def pick_pieces(wanted, held):
    devices, rows = held.shape[0], held.shape[1] - REQUEST_ROWS
    return pl.pallas_call(
        pick_kernel,
        out_shape=jax.ShapeDtypeStruct((devices, 2, rows, HEAD_SIZE), jnp.bfloat16),
        in_specs=[
            pl.BlockSpec(memory_space=pltpu.SMEM),
            pl.BlockSpec(memory_space=pltpu.VMEM),
        ],
        out_specs=pl.BlockSpec(memory_space=pltpu.VMEM),
        compiler_params=pltpu.CompilerParams(vmem_limit_bytes=16 * MIB),
        name="pick_pieces",
    )(wanted, held)


HEADS_AT_ONCE = 2


def attention_kernel(
    flags_ref, query_ref, key_ref, value_ref, far_key_ref, far_value_ref, out_ref
):
    rows = query_ref.shape[0]
    factor = math.log2(math.e) / math.sqrt(HEAD_SIZE)
    row = lax.broadcasted_iota(jnp.int32, (rows, rows), 0)
    column = lax.broadcasted_iota(jnp.int32, (rows, rows), 1)
    causal = column <= row

    def attend(picks):
        keys = [key_ref[...]] + [far_key_ref[:, p, 0].reshape(rows, HEAD_SIZE) for p in picks]
        values = [value_ref[...]] + [far_value_ref[:, p, 0].reshape(rows, HEAD_SIZE) for p in picks]
        keys_across = jnp.concatenate(keys, axis=0).T
        value = jnp.concatenate(values, axis=0)
        value = jnp.concatenate([value, jnp.ones_like(value)], axis=1)

        def score(first):
            query = jnp.concatenate(
                [
                    query_ref[:, h * HEAD_SIZE : (h + 1) * HEAD_SIZE]
                    for h in range(first, first + HEADS_AT_ONCE)
                ],
                axis=0,
            )
            return jnp.dot(query, keys_across, preferred_element_type=jnp.float32)

        def finish(first, scores):
            weights = []
            for h in range(HEADS_AT_ONCE):
                part = scores[h * rows : (h + 1) * rows]
                own = jnp.where(causal, part[:, :rows], -1e30)
                part = jnp.concatenate([own, part[:, rows:]], axis=1) if picks else own
                shift = jnp.max(part, axis=1, keepdims=True) * factor
                weights.append(jnp.exp2(part * factor - shift).astype(jnp.bfloat16))
            both = jnp.dot(
                jnp.concatenate(weights, axis=0), value, preferred_element_type=jnp.float32
            )
            row_sum = both[:, HEAD_SIZE:]
            inverse = pl.reciprocal(row_sum, approx=True)
            inverse = inverse * (2.0 - row_sum * inverse)
            mixture = (both[:, :HEAD_SIZE] * inverse).astype(out_ref.dtype)
            for h in range(HEADS_AT_ONCE):
                head = first + h
                out_ref[:, head * HEAD_SIZE : (head + 1) * HEAD_SIZE] = mixture[
                    h * rows : (h + 1) * rows
                ]

        scores = score(0)
        for first in range(0, GROUP, HEADS_AT_ONCE):
            later = first + HEADS_AT_ONCE
            following = score(later) if later < GROUP else None
            finish(first, scores)
            scores = following

    first, second = flags_ref[0], flags_ref[1]

    @pl.when(first + second == 2)
    def _():
        attend((0, 1))

    @pl.when(first + second == 1)
    def _():
        attend((second,))

    @pl.when(first + second == 0)
    def _():
        attend(())


def attention(flags, queries, keys, values, far):
    rows = queries.shape[0]
    holders, _, _, piece_rows, _ = far.shape
    width = GROUP * HEAD_SIZE
    far_shape = (holders, 2, 1, piece_rows, HEAD_SIZE)
    scores = QUERY_HEADS * rows * 3 * rows
    return pl.pallas_call(
        attention_kernel,
        out_shape=jax.ShapeDtypeStruct(queries.shape, jnp.bfloat16),
        grid=(KEY_VALUE_HEADS,),
        in_specs=[
            pl.BlockSpec(memory_space=pltpu.SMEM),
            pl.BlockSpec((rows, width), lambda g: (0, g)),
            pl.BlockSpec((rows, HEAD_SIZE), lambda g: (0, g)),
            pl.BlockSpec((rows, HEAD_SIZE), lambda g: (0, g)),
            pl.BlockSpec(far_shape, lambda g: (0, 0, g, 0, 0)),
            pl.BlockSpec(far_shape, lambda g: (0, 0, g + KEY_VALUE_HEADS, 0, 0)),
        ],
        out_specs=pl.BlockSpec((rows, width), lambda g: (0, g)),
        compiler_params=pltpu.CompilerParams(vmem_limit_bytes=24 * MIB),
        cost_estimate=pl.CostEstimate(
            flops=4 * scores * HEAD_SIZE, bytes_accessed=6 * MIB, transcendentals=scores
        ),
        name="attention",
    )(flags, queries, keys, values, far, far)


def local(queries, all_key_states, all_value_states, selected):
    devices = lax.axis_size("ctx")
    my_block = lax.axis_index("ctx")
    rows = all_key_states.shape[0]
    piece_rows = rows // devices
    packed = pack(all_key_states, all_value_states, selected, devices)
    held = lax.all_to_all(packed, "ctx", split_axis=0, concat_axis=0, tiled=True)
    wanted = held[:, SLOTS * piece_rows, :2].astype(jnp.int32)
    wanted = jnp.clip(wanted, 0, devices - 1)
    chosen = pick_pieces(wanted, held)
    far = lax.all_to_all(chosen, "ctx", split_axis=0, concat_axis=0, tiled=True)
    far = far.reshape(devices, 2, SLOTS, piece_rows, HEAD_SIZE)
    if piece_rows % 16 != 0:
        far = far.transpose(1, 2, 0, 3, 4).reshape(1, 2, SLOTS, rows, HEAD_SIZE)
    first, second = selected[0, 0], selected[0, 1]
    first_valid = first < my_block
    second_valid = jnp.logical_and(second < my_block, second != first)
    flags = jnp.stack([first_valid, second_valid]).astype(jnp.int32)
    return attention(flags, queries, all_key_states, all_value_states, far)


def solution(mesh):
    placed = P(("groups", "ctx"), None)
    return jax.shard_map(
        local, mesh=mesh, in_specs=(placed,) * 4, out_specs=placed, check_vma=False
    )
```

```python
import math

import jax
import jax.numpy as jnp
from jax import lax
from jax.experimental import pallas as pl
from jax.experimental.pallas import tpu as pltpu
from jax.sharding import PartitionSpec as P

QUERY_HEADS = 32
KEY_VALUE_HEADS = 4
HEAD_SIZE = 128
GROUP = QUERY_HEADS // KEY_VALUE_HEADS
SLOTS = 2 * KEY_VALUE_HEADS
REQUEST_ROWS = 16
MIB = 1024 * 1024


def pack_kernel(selected_ref, key_ref, value_ref, out_ref):
    devices, piece_rows = out_ref.shape[0], key_ref.shape[0] // out_ref.shape[0]
    for slot in range(SLOTS):
        ref = key_ref if slot < KEY_VALUE_HEADS else value_ref
        head = slot % KEY_VALUE_HEADS
        part = ref[:, head * HEAD_SIZE : (head + 1) * HEAD_SIZE]
        out_ref[:, slot * piece_rows : (slot + 1) * piece_rows, :] = part.reshape(
            devices, piece_rows, HEAD_SIZE
        )
    lane = lax.broadcasted_iota(jnp.int32, (devices, REQUEST_ROWS, HEAD_SIZE), 2)
    request = jnp.where(lane == 0, selected_ref[0, 0], selected_ref[0, 1])
    out_ref[:, SLOTS * piece_rows :, :] = request.astype(jnp.float32).astype(jnp.bfloat16)


def pack(keys, values, selected, devices):
    rows = keys.shape[0]
    piece_rows = rows // devices
    shape = (devices, SLOTS * piece_rows + REQUEST_ROWS, HEAD_SIZE)
    if piece_rows % 16 == 0:
        return pl.pallas_call(
            pack_kernel,
            out_shape=jax.ShapeDtypeStruct(shape, jnp.bfloat16),
            in_specs=[
                pl.BlockSpec(memory_space=pltpu.SMEM),
                pl.BlockSpec(memory_space=pltpu.VMEM),
                pl.BlockSpec(memory_space=pltpu.VMEM),
            ],
            out_specs=pl.BlockSpec(memory_space=pltpu.VMEM),
            name="pack",
        )(selected, keys, values)
    both = jnp.concatenate([keys, values], axis=1)
    both = both.reshape(devices, piece_rows, SLOTS, HEAD_SIZE).transpose(0, 2, 1, 3)
    both = both.reshape(devices, SLOTS * piece_rows, HEAD_SIZE)
    lane = jnp.arange(HEAD_SIZE) == 0
    request = jnp.where(lane, selected[0, 0], selected[0, 1]).astype(jnp.bfloat16)
    request = jnp.broadcast_to(request, (devices, REQUEST_ROWS, HEAD_SIZE))
    return jnp.concatenate([both, request], axis=1)


def partner(position, step):
    return position ^ step


def pick_kernel(place_ref, wanted_ref, held_ref, *out_refs):
    rows = out_refs[0].shape[1]
    for step, out_ref in enumerate(out_refs):
        device = partner(place_ref[0], step)
        for pick in range(2):
            out_ref[pick] = held_ref[wanted_ref[device, pick], :rows, :]


def pick_pieces(place, wanted, held):
    devices, rows = held.shape[0], held.shape[1] - REQUEST_ROWS
    return pl.pallas_call(
        pick_kernel,
        out_shape=[jax.ShapeDtypeStruct((2, rows, HEAD_SIZE), jnp.bfloat16)] * devices,
        in_specs=[
            pl.BlockSpec(memory_space=pltpu.SMEM),
            pl.BlockSpec(memory_space=pltpu.SMEM),
            pl.BlockSpec(memory_space=pltpu.VMEM),
        ],
        out_specs=[pl.BlockSpec(memory_space=pltpu.VMEM)] * devices,
        compiler_params=pltpu.CompilerParams(vmem_limit_bytes=16 * MIB),
        name="pick_pieces",
    )(place, wanted, held)


def deliver(pieces):
    devices = len(pieces)
    moved = [None] * devices
    moved[0] = pieces[0]
    for step in reversed(range(1, devices)):
        pairs = [(i, partner(i, step)) for i in range(devices)]
        moved[step] = lax.ppermute(pieces[step], "ctx", pairs)
    return moved


HEADS_AT_ONCE = 2


def attention_kernel(flags_ref, query_ref, key_ref, value_ref, *refs):
    rows = query_ref.shape[0]
    far_refs, out_ref = refs[:-1], refs[-1]
    far_key_refs, far_value_refs = far_refs[: len(far_refs) // 2], far_refs[len(far_refs) // 2 :]
    factor = math.log2(math.e) / math.sqrt(HEAD_SIZE)
    row = lax.broadcasted_iota(jnp.int32, (rows, rows), 0)
    column = lax.broadcasted_iota(jnp.int32, (rows, rows), 1)
    causal = column <= row

    def attend(picks):
        keys = [key_ref[...]] + [ref[p, 0] for p in picks for ref in far_key_refs]
        values = [value_ref[...]] + [ref[p, 0] for p in picks for ref in far_value_refs]
        keys_across = jnp.concatenate(keys, axis=0).T
        value = jnp.concatenate(values, axis=0)
        value = jnp.concatenate([value, jnp.ones_like(value)], axis=1)

        def score(first):
            query = jnp.concatenate(
                [
                    query_ref[:, h * HEAD_SIZE : (h + 1) * HEAD_SIZE]
                    for h in range(first, first + HEADS_AT_ONCE)
                ],
                axis=0,
            )
            return jnp.dot(query, keys_across, preferred_element_type=jnp.float32)

        def finish(first, scores):
            weights = []
            for h in range(HEADS_AT_ONCE):
                part = scores[h * rows : (h + 1) * rows]
                own = jnp.where(causal, part[:, :rows], -1e30)
                part = jnp.concatenate([own, part[:, rows:]], axis=1) if picks else own
                shift = jnp.max(part, axis=1, keepdims=True) * factor
                weights.append(jnp.exp2(part * factor - shift).astype(jnp.bfloat16))
            both = jnp.dot(
                jnp.concatenate(weights, axis=0), value, preferred_element_type=jnp.float32
            )
            row_sum = both[:, HEAD_SIZE:]
            inverse = pl.reciprocal(row_sum, approx=True)
            inverse = inverse * (2.0 - row_sum * inverse)
            mixture = (both[:, :HEAD_SIZE] * inverse).astype(out_ref.dtype)
            for h in range(HEADS_AT_ONCE):
                head = first + h
                out_ref[:, head * HEAD_SIZE : (head + 1) * HEAD_SIZE] = mixture[
                    h * rows : (h + 1) * rows
                ]

        scores = score(0)
        for first in range(0, GROUP, HEADS_AT_ONCE):
            later = first + HEADS_AT_ONCE
            following = score(later) if later < GROUP else None
            finish(first, scores)
            scores = following

    first, second = flags_ref[0], flags_ref[1]

    @pl.when(first + second == 2)
    def _():
        attend((0, 1))

    @pl.when(first + second == 1)
    def _():
        attend((second,))

    @pl.when(first + second == 0)
    def _():
        attend(())


def attention(flags, queries, keys, values, far):
    rows = queries.shape[0]
    piece_rows = far[0].shape[2]
    width = GROUP * HEAD_SIZE
    far_shape = (2, 1, piece_rows, HEAD_SIZE)
    far_key = pl.BlockSpec(far_shape, lambda g: (0, g, 0, 0))
    far_value = pl.BlockSpec(far_shape, lambda g: (0, g + KEY_VALUE_HEADS, 0, 0))
    scores = QUERY_HEADS * rows * 3 * rows
    return pl.pallas_call(
        attention_kernel,
        out_shape=jax.ShapeDtypeStruct(queries.shape, jnp.bfloat16),
        grid=(KEY_VALUE_HEADS,),
        in_specs=[
            pl.BlockSpec(memory_space=pltpu.SMEM),
            pl.BlockSpec((rows, width), lambda g: (0, g)),
            pl.BlockSpec((rows, HEAD_SIZE), lambda g: (0, g)),
            pl.BlockSpec((rows, HEAD_SIZE), lambda g: (0, g)),
            *[far_key] * len(far),
            *[far_value] * len(far),
        ],
        out_specs=pl.BlockSpec((rows, width), lambda g: (0, g)),
        compiler_params=pltpu.CompilerParams(vmem_limit_bytes=24 * MIB),
        cost_estimate=pl.CostEstimate(
            flops=4 * scores * HEAD_SIZE, bytes_accessed=6 * MIB, transcendentals=scores
        ),
        name="attention",
    )(flags, queries, keys, values, *far, *far)


def local(queries, all_key_states, all_value_states, selected):
    devices = lax.axis_size("ctx")
    my_block = lax.axis_index("ctx")
    rows = all_key_states.shape[0]
    piece_rows = rows // devices
    packed = pack(all_key_states, all_value_states, selected, devices)
    held = lax.all_to_all(packed, "ctx", split_axis=0, concat_axis=0, tiled=True)
    wanted = held[:, SLOTS * piece_rows, :2].astype(jnp.int32)
    wanted = jnp.clip(wanted, 0, devices - 1)
    place = my_block.astype(jnp.int32)[None]
    moved = deliver(pick_pieces(place, wanted, held))
    far = [m.reshape(2, SLOTS, piece_rows, HEAD_SIZE) for m in moved]
    if piece_rows % 16 != 0:
        far = [jnp.concatenate(far, axis=2)]
    first, second = selected[0, 0], selected[0, 1]
    first_valid = first < my_block
    second_valid = jnp.logical_and(second < my_block, second != first)
    flags = jnp.stack([first_valid, second_valid]).astype(jnp.int32)
    return attention(flags, queries, all_key_states, all_value_states, far)


def solution(mesh):
    placed = P(("groups", "ctx"), None)
    return jax.shard_map(
        local, mesh=mesh, in_specs=(placed,) * 4, out_specs=placed, check_vma=False
    )
```

```python
import math

import jax
import jax.numpy as jnp
from jax import lax
from jax.experimental import pallas as pl
from jax.experimental.pallas import tpu as pltpu
from jax.sharding import PartitionSpec as P

QUERY_HEADS = 32
KEY_VALUE_HEADS = 4
HEAD_SIZE = 128
GROUP = QUERY_HEADS // KEY_VALUE_HEADS
SLOTS = 2 * KEY_VALUE_HEADS
REQUEST_ROWS = 16
MIB = 1024 * 1024


def pack_kernel(selected_ref, key_ref, value_ref, out_ref):
    devices, piece_rows = out_ref.shape[0], key_ref.shape[0] // out_ref.shape[0]
    for slot in range(SLOTS):
        ref = key_ref if slot < KEY_VALUE_HEADS else value_ref
        head = slot % KEY_VALUE_HEADS
        part = ref[:, head * HEAD_SIZE : (head + 1) * HEAD_SIZE]
        out_ref[:, slot * piece_rows : (slot + 1) * piece_rows, :] = part.reshape(
            devices, piece_rows, HEAD_SIZE
        )
    lane = lax.broadcasted_iota(jnp.int32, (devices, REQUEST_ROWS, HEAD_SIZE), 2)
    request = jnp.where(lane == 0, selected_ref[0, 0], selected_ref[0, 1])
    out_ref[:, SLOTS * piece_rows :, :] = request.astype(jnp.float32).astype(jnp.bfloat16)


def pack(keys, values, selected, devices):
    rows = keys.shape[0]
    piece_rows = rows // devices
    shape = (devices, SLOTS * piece_rows + REQUEST_ROWS, HEAD_SIZE)
    if piece_rows % 16 == 0:
        return pl.pallas_call(
            pack_kernel,
            out_shape=jax.ShapeDtypeStruct(shape, jnp.bfloat16),
            in_specs=[
                pl.BlockSpec(memory_space=pltpu.SMEM),
                pl.BlockSpec(memory_space=pltpu.VMEM),
                pl.BlockSpec(memory_space=pltpu.VMEM),
            ],
            out_specs=pl.BlockSpec(memory_space=pltpu.VMEM),
            name="pack",
        )(selected, keys, values)
    both = jnp.concatenate([keys, values], axis=1)
    both = both.reshape(devices, piece_rows, SLOTS, HEAD_SIZE).transpose(0, 2, 1, 3)
    both = both.reshape(devices, SLOTS * piece_rows, HEAD_SIZE)
    lane = jnp.arange(HEAD_SIZE) == 0
    request = jnp.where(lane, selected[0, 0], selected[0, 1]).astype(jnp.bfloat16)
    request = jnp.broadcast_to(request, (devices, REQUEST_ROWS, HEAD_SIZE))
    return jnp.concatenate([both, request], axis=1)


def pick_kernel(wanted_ref, held_ref, out_ref, done):
    rows = out_ref.shape[2]

    @pl.loop(0, out_ref.shape[0])
    def _(device):
        for pick in range(2):
            piece = held_ref.at[wanted_ref[device, pick], pl.ds(0, rows), :]
            pltpu.make_async_copy(piece, out_ref.at[device, pick], done).start()

    pltpu.make_async_copy(out_ref, out_ref, done).wait()


def pick_pieces(wanted, held):
    devices, rows = held.shape[0], held.shape[1] - REQUEST_ROWS
    return pl.pallas_call(
        pick_kernel,
        out_shape=jax.ShapeDtypeStruct((devices, 2, rows, HEAD_SIZE), jnp.bfloat16),
        in_specs=[
            pl.BlockSpec(memory_space=pltpu.SMEM),
            pl.BlockSpec(memory_space=pl.ANY),
        ],
        out_specs=pl.BlockSpec(memory_space=pl.ANY),
        scratch_shapes=[pltpu.SemaphoreType.DMA],
        name="pick_pieces",
    )(wanted, held)


HEADS_AT_ONCE = 2
FACTOR = math.log2(math.e) / math.sqrt(HEAD_SIZE)
LARGE_SUM = 2.0**100


def head_lanes(head):
    return slice(head * HEAD_SIZE, (head + 1) * HEAD_SIZE)


def with_ones(value):
    return jnp.concatenate([value, jnp.ones_like(value)], axis=1)


def inverse_of(positive):
    inverse = pl.reciprocal(positive, approx=True)
    return inverse * (2.0 - positive * inverse)


def stacked_queries(query_ref, first):
    heads = range(first, first + HEADS_AT_ONCE)
    return jnp.concatenate([query_ref[:, head_lanes(h)] for h in heads], axis=0)


def staggered(score, finish):
    scores = score(0)
    for first in range(0, GROUP, HEADS_AT_ONCE):
        later = first + HEADS_AT_ONCE
        following = score(later) if later < GROUP else None
        finish(first, scores)
        scores = following


def own_kernel(query_ref, key_ref, value_ref, out_ref, level_ref):
    rows = query_ref.shape[0]
    row = lax.broadcasted_iota(jnp.int32, (rows, rows), 0)
    column = lax.broadcasted_iota(jnp.int32, (rows, rows), 1)
    causal = column <= row
    lane = lax.broadcasted_iota(jnp.int32, (rows, HEAD_SIZE), 1)
    keys_across = key_ref[...].T
    value = with_ones(value_ref[...])

    def score(first):
        return jnp.dot(
            stacked_queries(query_ref, first), keys_across, preferred_element_type=jnp.float32
        )

    def finish(first, scores):
        weights, shifts = [], []
        for h in range(HEADS_AT_ONCE):
            part = jnp.where(causal, scores[h * rows : (h + 1) * rows], -1e30)
            shift = jnp.max(part, axis=1, keepdims=True) * FACTOR
            shifts.append(shift)
            weights.append(jnp.exp2(part * FACTOR - shift).astype(jnp.bfloat16))
        both = jnp.dot(
            jnp.concatenate(weights, axis=0), value, preferred_element_type=jnp.float32
        )
        for h in range(HEADS_AT_ONCE):
            part = both[h * rows : (h + 1) * rows]
            row_sum = part[:, HEAD_SIZE:]
            out_ref[:, head_lanes(first + h)] = part[:, :HEAD_SIZE] * inverse_of(row_sum)
            level = shifts[h] + jnp.log2(row_sum)
            level_ref[...] = jnp.where(lane == first + h, level, level_ref[...])

    level_ref[...] = jnp.zeros_like(level_ref)
    staggered(score, finish)


def own_attention(queries, keys, values):
    rows = queries.shape[0]
    width = GROUP * HEAD_SIZE
    scores = QUERY_HEADS * rows * rows
    return pl.pallas_call(
        own_kernel,
        out_shape=[
            jax.ShapeDtypeStruct(queries.shape, jnp.float32),
            jax.ShapeDtypeStruct((rows, KEY_VALUE_HEADS * HEAD_SIZE), jnp.float32),
        ],
        grid=(KEY_VALUE_HEADS,),
        in_specs=[
            pl.BlockSpec((rows, width), lambda g: (0, g)),
            pl.BlockSpec((rows, HEAD_SIZE), lambda g: (0, g)),
            pl.BlockSpec((rows, HEAD_SIZE), lambda g: (0, g)),
        ],
        out_specs=[
            pl.BlockSpec((rows, width), lambda g: (0, g)),
            pl.BlockSpec((rows, HEAD_SIZE), lambda g: (0, g)),
        ],
        compiler_params=pltpu.CompilerParams(vmem_limit_bytes=24 * MIB),
        cost_estimate=pl.CostEstimate(
            flops=4 * scores * HEAD_SIZE, bytes_accessed=7 * MIB, transcendentals=scores
        ),
        name="own_attention",
    )(queries, keys, values)


def far_kernel(selected_ref, query_ref, own_ref, level_ref, far_ref, out_ref, staged, copied):
    rows = query_ref.shape[0]
    width = GROUP * HEAD_SIZE
    my_block = lax.axis_index("ctx")
    chosen = selected_ref[0, 0], selected_ref[0, 1]
    first = chosen[0] < my_block
    second = jnp.logical_and(chosen[1] < my_block, chosen[1] != chosen[0])
    count = first.astype(jnp.int32) + second.astype(jnp.int32)

    @pl.loop(0, KEY_VALUE_HEADS)
    def _(group):
        lanes = pl.ds(pl.multiple_of(group * width, width), width)
        query = query_ref.at[:, lanes]
        own = own_ref.at[:, lanes]
        level = level_ref.at[:, pl.ds(pl.multiple_of(group * HEAD_SIZE, HEAD_SIZE), HEAD_SIZE)]
        out = staged.at[group]

        def attend(picks):
            def block(slot, pick):
                return far_ref[:, pick, slot].reshape(rows, HEAD_SIZE)

            keys_across = jnp.concatenate([block(group, p) for p in picks], axis=0).T
            value = with_ones(
                jnp.concatenate([block(group + KEY_VALUE_HEADS, p) for p in picks], axis=0)
            )

            def score(head):
                return jnp.dot(
                    stacked_queries(query, head), keys_across, preferred_element_type=jnp.float32
                )

            def quick():
                largest = jnp.zeros((8, HEAD_SIZE), jnp.float32)

                def finish(head, scores):
                    nonlocal largest
                    weights = []
                    for h in range(HEADS_AT_ONCE):
                        part = scores[h * rows : (h + 1) * rows]
                        mine = level[:, head + h : head + h + 1]
                        weights.append(jnp.exp2(part * FACTOR - mine).astype(jnp.bfloat16))
                    both = jnp.dot(
                        jnp.concatenate(weights, axis=0), value, preferred_element_type=jnp.float32
                    )
                    for h in range(HEADS_AT_ONCE):
                        part = both[h * rows : (h + 1) * rows]
                        row_sum = 1.0 + part[:, HEAD_SIZE:]
                        largest = jnp.maximum(
                            largest, jnp.max(row_sum.reshape(rows // 8, 8, HEAD_SIZE), axis=0)
                        )
                        mixture = own[:, head_lanes(head + h)] + part[:, :HEAD_SIZE]
                        out[:, head_lanes(head + h)] = (mixture * inverse_of(row_sum)).astype(
                            out.dtype
                        )

                staggered(score, finish)
                return jnp.max(largest)

            def careful():
                def finish(head, scores):
                    for h in range(HEADS_AT_ONCE):
                        part = scores[h * rows : (h + 1) * rows] * FACTOR
                        mine = level[:, head + h : head + h + 1]
                        shift = jnp.maximum(jnp.max(part, axis=1, keepdims=True), mine)
                        weights = jnp.exp2(part - shift).astype(jnp.bfloat16)
                        both = jnp.dot(weights, value, preferred_element_type=jnp.float32)
                        share = jnp.exp2(mine - shift)
                        mixture = own[:, head_lanes(head + h)] * share + both[:, :HEAD_SIZE]
                        out[:, head_lanes(head + h)] = (
                            mixture * inverse_of(share + both[:, HEAD_SIZE:])
                        ).astype(out.dtype)

                staggered(score, finish)

            largest = quick()

            @pl.when(largest > LARGE_SUM)
            def _():
                careful()

        @pl.when(count == 2)
        def _():
            attend((0, 1))

        @pl.when(count == 1)
        def _():
            attend((second.astype(jnp.int32),))

        @pl.when(count == 0)
        def _():
            out[...] = own[...].astype(out.dtype)

        pltpu.make_async_copy(out, out_ref.at[:, lanes], copied.at[group]).start()

    for group in range(KEY_VALUE_HEADS):
        lanes = slice(group * width, (group + 1) * width)
        pltpu.make_async_copy(staged.at[group], out_ref.at[:, lanes], copied.at[group]).wait()


def far_attention(selected, queries, own, level, far):
    rows = queries.shape[0]
    scores = QUERY_HEADS * rows * 2 * rows
    return pl.pallas_call(
        far_kernel,
        out_shape=jax.ShapeDtypeStruct(queries.shape, jnp.bfloat16),
        in_specs=[
            pl.BlockSpec(memory_space=pltpu.SMEM),
            *[pl.BlockSpec(memory_space=pltpu.VMEM)] * 4,
        ],
        out_specs=pl.BlockSpec(memory_space=pl.ANY),
        scratch_shapes=[
            pltpu.VMEM((KEY_VALUE_HEADS, rows, GROUP * HEAD_SIZE), jnp.bfloat16),
            pltpu.SemaphoreType.DMA((KEY_VALUE_HEADS,)),
        ],
        compiler_params=pltpu.CompilerParams(vmem_limit_bytes=28 * MIB),
        cost_estimate=pl.CostEstimate(
            flops=4 * scores * HEAD_SIZE, bytes_accessed=10 * MIB, transcendentals=scores
        ),
        name="far_attention",
    )(selected, queries, own, level, far)


def local(queries, all_key_states, all_value_states, selected):
    devices = lax.axis_size("ctx")
    rows = all_key_states.shape[0]
    piece_rows = rows // devices
    packed = pack(all_key_states, all_value_states, selected, devices)
    held = lax.all_to_all(packed, "ctx", split_axis=0, concat_axis=0, tiled=True)
    own, level = own_attention(queries, all_key_states, all_value_states)
    wanted = held[:, SLOTS * piece_rows, :2].astype(jnp.int32)
    wanted = jnp.clip(wanted, 0, devices - 1)
    chosen = pick_pieces(wanted, held)
    far = lax.all_to_all(chosen, "ctx", split_axis=0, concat_axis=0, tiled=True)
    far = far.reshape(devices, 2, SLOTS, piece_rows, HEAD_SIZE)
    if piece_rows % 16 != 0:
        far = far.transpose(1, 2, 0, 3, 4).reshape(1, 2, SLOTS, rows, HEAD_SIZE)
    return far_attention(selected, queries, own, level, far)


def solution(mesh):
    placed = P(("groups", "ctx"), None)
    return jax.shard_map(
        local, mesh=mesh, in_specs=(placed,) * 4, out_specs=placed, check_vma=False
    )
```

```python
import math

import jax
import jax.numpy as jnp
from jax import lax
from jax.experimental import pallas as pl
from jax.experimental.pallas import tpu as pltpu
from jax.sharding import PartitionSpec as P

QUERY_HEADS = 32
KEY_VALUE_HEADS = 4
HEAD_SIZE = 128
GROUP = QUERY_HEADS // KEY_VALUE_HEADS
SLOTS = 2 * KEY_VALUE_HEADS
REQUEST_ROWS = 16
MIB = 1024 * 1024


def pack_kernel(selected_ref, key_ref, value_ref, out_ref):
    devices, piece_rows = out_ref.shape[0], key_ref.shape[0] // out_ref.shape[0]
    for slot in range(SLOTS):
        ref = key_ref if slot < KEY_VALUE_HEADS else value_ref
        head = slot % KEY_VALUE_HEADS
        part = ref[:, head * HEAD_SIZE : (head + 1) * HEAD_SIZE]
        out_ref[:, slot * piece_rows : (slot + 1) * piece_rows, :] = part.reshape(
            devices, piece_rows, HEAD_SIZE
        )
    lane = lax.broadcasted_iota(jnp.int32, (devices, REQUEST_ROWS, HEAD_SIZE), 2)
    request = jnp.where(lane == 0, selected_ref[0, 0], selected_ref[0, 1])
    out_ref[:, SLOTS * piece_rows :, :] = request.astype(jnp.float32).astype(jnp.bfloat16)


def pack(keys, values, selected, devices):
    rows = keys.shape[0]
    piece_rows = rows // devices
    shape = (devices, SLOTS * piece_rows + REQUEST_ROWS, HEAD_SIZE)
    if piece_rows % 16 == 0:
        return pl.pallas_call(
            pack_kernel,
            out_shape=jax.ShapeDtypeStruct(shape, jnp.bfloat16),
            in_specs=[
                pl.BlockSpec(memory_space=pltpu.SMEM),
                pl.BlockSpec(memory_space=pltpu.VMEM),
                pl.BlockSpec(memory_space=pltpu.VMEM),
            ],
            out_specs=pl.BlockSpec(memory_space=pltpu.VMEM),
            name="pack",
        )(selected, keys, values)
    both = jnp.concatenate([keys, values], axis=1)
    both = both.reshape(devices, piece_rows, SLOTS, HEAD_SIZE).transpose(0, 2, 1, 3)
    both = both.reshape(devices, SLOTS * piece_rows, HEAD_SIZE)
    lane = jnp.arange(HEAD_SIZE) == 0
    request = jnp.where(lane, selected[0, 0], selected[0, 1]).astype(jnp.bfloat16)
    request = jnp.broadcast_to(request, (devices, REQUEST_ROWS, HEAD_SIZE))
    return jnp.concatenate([both, request], axis=1)


def pick_kernel(wanted_ref, held_ref, out_ref):
    rows = out_ref.shape[2]

    @pl.loop(0, out_ref.shape[0])
    def _(device):
        for pick in range(2):
            out_ref[device, pick] = held_ref[wanted_ref[device, pick], :rows, :]


def pick_pieces(wanted, held):
    devices, rows = held.shape[0], held.shape[1] - REQUEST_ROWS
    return pl.pallas_call(
        pick_kernel,
        out_shape=jax.ShapeDtypeStruct((devices, 2, rows, HEAD_SIZE), jnp.bfloat16),
        in_specs=[
            pl.BlockSpec(memory_space=pltpu.SMEM),
            pl.BlockSpec(memory_space=pltpu.VMEM),
        ],
        out_specs=pl.BlockSpec(memory_space=pltpu.VMEM),
        compiler_params=pltpu.CompilerParams(vmem_limit_bytes=16 * MIB),
        name="pick_pieces",
    )(wanted, held)


HEADS_AT_ONCE = 4
FACTOR = math.log2(math.e) / math.sqrt(HEAD_SIZE)
LARGE_SUM = 2.0**100


def head_lanes(head):
    return slice(head * HEAD_SIZE, (head + 1) * HEAD_SIZE)


def with_ones(value):
    return jnp.concatenate([value, jnp.ones_like(value)], axis=1)


def inverse_of(positive):
    inverse = pl.reciprocal(positive, approx=True)
    return inverse * (2.0 - positive * inverse)


def stacked_queries(query_ref, first):
    heads = range(first, first + HEADS_AT_ONCE)
    return jnp.concatenate([query_ref[:, head_lanes(h)] for h in heads], axis=0)


def staggered(steps, score, finish):
    scores = score(steps[0])
    for step, later in zip(steps, steps[1:] + [None]):
        following = None if later is None else score(later)
        finish(step, scores)
        scores = following


STEPS = list(range(0, GROUP, HEADS_AT_ONCE))


def own_kernel(query_ref, key_ref, value_ref, out_ref, level_ref):
    rows = query_ref.shape[0]
    row = lax.broadcasted_iota(jnp.int32, (rows, rows), 0)
    column = lax.broadcasted_iota(jnp.int32, (rows, rows), 1)
    causal = column <= row
    lane = lax.broadcasted_iota(jnp.int32, (rows, HEAD_SIZE), 1)
    keys_across = key_ref[...].T
    value = with_ones(value_ref[...])

    def score(first):
        return jnp.dot(
            stacked_queries(query_ref, first), keys_across, preferred_element_type=jnp.float32
        )

    def finish(first, scores):
        weights, shifts = [], []
        for h in range(HEADS_AT_ONCE):
            part = jnp.where(causal, scores[h * rows : (h + 1) * rows], -1e30)
            shift = jnp.max(part, axis=1, keepdims=True) * FACTOR
            shifts.append(shift)
            weights.append(jnp.exp2(part * FACTOR - shift).astype(jnp.bfloat16))
        both = jnp.dot(
            jnp.concatenate(weights, axis=0), value, preferred_element_type=jnp.float32
        )
        for h in range(HEADS_AT_ONCE):
            part = both[h * rows : (h + 1) * rows]
            row_sum = part[:, HEAD_SIZE:]
            out_ref[:, head_lanes(first + h)] = part[:, :HEAD_SIZE] * inverse_of(row_sum)
            level = shifts[h] + jnp.log2(row_sum)
            level_ref[...] = jnp.where(lane == first + h, level, level_ref[...])

    level_ref[...] = jnp.zeros_like(level_ref)
    staggered(STEPS, score, finish)


def own_attention(queries, keys, values):
    rows = queries.shape[0]
    width = GROUP * HEAD_SIZE
    scores = QUERY_HEADS * rows * rows
    return pl.pallas_call(
        own_kernel,
        out_shape=[
            jax.ShapeDtypeStruct(queries.shape, jnp.float32),
            jax.ShapeDtypeStruct((rows, KEY_VALUE_HEADS * HEAD_SIZE), jnp.float32),
        ],
        grid=(KEY_VALUE_HEADS,),
        in_specs=[
            pl.BlockSpec((rows, width), lambda g: (0, g)),
            pl.BlockSpec((rows, HEAD_SIZE), lambda g: (0, g)),
            pl.BlockSpec((rows, HEAD_SIZE), lambda g: (0, g)),
        ],
        out_specs=[
            pl.BlockSpec((rows, width), lambda g: (0, g)),
            pl.BlockSpec((rows, HEAD_SIZE), lambda g: (0, g)),
        ],
        compiler_params=pltpu.CompilerParams(vmem_limit_bytes=24 * MIB),
        cost_estimate=pl.CostEstimate(
            flops=4 * scores * HEAD_SIZE, bytes_accessed=7 * MIB, transcendentals=scores
        ),
        name="own_attention",
    )(queries, keys, values)


def far_kernel(
    selected_ref, query_ref, far_ref, own_hbm, level_hbm, out_ref, own_ref, level_ref, staged, sems
):
    rows = query_ref.shape[0]
    width = GROUP * HEAD_SIZE

    def lanes(group, size):
        start = group * size
        return pl.ds(start if isinstance(group, int) else pl.multiple_of(start, size), size)

    def fetch(group):
        wide, narrow = lanes(group, width), lanes(group, HEAD_SIZE)
        return (
            pltpu.make_async_copy(own_hbm.at[:, wide], own_ref.at[group], sems.at[0, group]),
            pltpu.make_async_copy(level_hbm.at[:, narrow], level_ref.at[group], sems.at[1, group]),
        )

    def send(group):
        out = out_ref.at[:, lanes(group, width)]
        return pltpu.make_async_copy(staged.at[group], out, sems.at[2, group])

    for group in range(KEY_VALUE_HEADS):
        for copy in fetch(group):
            copy.start()

    def arrive(group):
        for copy in fetch(group):
            copy.wait()

    def block(slot, picks):
        blocks = [far_ref[:, p, slot].reshape(rows, HEAD_SIZE) for p in picks]
        return jnp.concatenate(blocks, axis=0)

    def keys_and_values(group, picks):
        return block(group, picks).T, with_ones(block(group + KEY_VALUE_HEADS, picks))

    def score(group, head, keys_across):
        query = stacked_queries(query_ref.at[:, lanes(group, width)], head)
        return jnp.dot(query, keys_across, preferred_element_type=jnp.float32)

    def quick(group, head, scores, value, largest):
        weights = []
        for h in range(HEADS_AT_ONCE):
            part = scores[h * rows : (h + 1) * rows]
            mine = level_ref[group, :, head + h : head + h + 1]
            weights.append(jnp.exp2(part * FACTOR - mine).astype(jnp.bfloat16))
        both = jnp.dot(
            jnp.concatenate(weights, axis=0), value, preferred_element_type=jnp.float32
        )
        for h in range(HEADS_AT_ONCE):
            part = both[h * rows : (h + 1) * rows]
            row_sum = 1.0 + part[:, HEAD_SIZE:]
            largest = jnp.maximum(
                largest, jnp.max(row_sum.reshape(rows // 8, 8, HEAD_SIZE), axis=0)
            )
            mixture = own_ref[group, :, head_lanes(head + h)] + part[:, :HEAD_SIZE]
            staged[group, :, head_lanes(head + h)] = (mixture * inverse_of(row_sum)).astype(
                staged.dtype
            )
        return largest

    def careful(group, head, scores, value):
        for h in range(HEADS_AT_ONCE):
            part = scores[h * rows : (h + 1) * rows] * FACTOR
            mine = level_ref[group, :, head + h : head + h + 1]
            shift = jnp.maximum(jnp.max(part, axis=1, keepdims=True), mine)
            weights = jnp.exp2(part - shift).astype(jnp.bfloat16)
            both = jnp.dot(weights, value, preferred_element_type=jnp.float32)
            share = jnp.exp2(mine - shift)
            mixture = own_ref[group, :, head_lanes(head + h)] * share + both[:, :HEAD_SIZE]
            staged[group, :, head_lanes(head + h)] = (
                mixture * inverse_of(share + both[:, HEAD_SIZE:])
            ).astype(staged.dtype)

    nothing = jnp.zeros((8, HEAD_SIZE), jnp.float32)

    def attend_quickly(picks):
        held = {}
        largest = nothing

        def start(step):
            group, head = step
            if head == 0:
                held[group] = keys_and_values(group, picks)
            return score(group, head, held[group][0])

        def finish(step, scores):
            nonlocal largest
            group, head = step
            if head == 0:
                arrive(group)
            largest = quick(group, head, scores, held[group][1], largest)
            if head == STEPS[-1]:
                send(group).start()

        staggered([(g, h) for g in range(KEY_VALUE_HEADS) for h in STEPS], start, finish)
        return jnp.max(largest)

    def attend_carefully(picks):
        @pl.loop(0, KEY_VALUE_HEADS)
        def _(group):
            send(group).wait()
            keys_across, value = keys_and_values(group, picks)
            for head in STEPS:
                careful(group, head, score(group, head, keys_across), value)
            send(group).start()

    def attend(picks):
        largest = attend_quickly(picks)

        @pl.when(largest > LARGE_SUM)
        def _():
            attend_carefully(picks)

    my_block = lax.axis_index("ctx")
    chosen = selected_ref[0, 0], selected_ref[0, 1]
    first = chosen[0] < my_block
    second = jnp.logical_and(chosen[1] < my_block, chosen[1] != chosen[0])
    count = first.astype(jnp.int32) + second.astype(jnp.int32)

    @pl.when(count == 2)
    def _():
        attend((0, 1))

    @pl.when(count == 1)
    def _():
        attend((second.astype(jnp.int32),))

    @pl.when(count == 0)
    def _():
        for group in range(KEY_VALUE_HEADS):
            arrive(group)
            staged[group] = own_ref[group].astype(staged.dtype)
            send(group).start()

    for group in range(KEY_VALUE_HEADS):
        send(group).wait()


def far_attention(selected, queries, own, level, far):
    rows = queries.shape[0]
    scores = QUERY_HEADS * rows * 2 * rows
    return pl.pallas_call(
        far_kernel,
        out_shape=jax.ShapeDtypeStruct(queries.shape, jnp.bfloat16),
        in_specs=[
            pl.BlockSpec(memory_space=pltpu.SMEM),
            *[pl.BlockSpec(memory_space=pltpu.VMEM)] * 2,
            *[pl.BlockSpec(memory_space=pl.ANY)] * 2,
        ],
        out_specs=pl.BlockSpec(memory_space=pl.ANY),
        scratch_shapes=[
            pltpu.VMEM((KEY_VALUE_HEADS, rows, GROUP * HEAD_SIZE), jnp.float32),
            pltpu.VMEM((KEY_VALUE_HEADS, rows, HEAD_SIZE), jnp.float32),
            pltpu.VMEM((KEY_VALUE_HEADS, rows, GROUP * HEAD_SIZE), jnp.bfloat16),
            pltpu.SemaphoreType.DMA((3, KEY_VALUE_HEADS)),
        ],
        compiler_params=pltpu.CompilerParams(vmem_limit_bytes=28 * MIB),
        cost_estimate=pl.CostEstimate(
            flops=4 * scores * HEAD_SIZE, bytes_accessed=10 * MIB, transcendentals=scores
        ),
        name="far_attention",
    )(selected, queries, far, own, level)


def local(queries, all_key_states, all_value_states, selected):
    devices = lax.axis_size("ctx")
    rows = all_key_states.shape[0]
    piece_rows = rows // devices
    packed = pack(all_key_states, all_value_states, selected, devices)
    held = lax.all_to_all(packed, "ctx", split_axis=0, concat_axis=0, tiled=True)
    own, level = own_attention(queries, all_key_states, all_value_states)
    wanted = held[:, SLOTS * piece_rows, :2].astype(jnp.int32)
    wanted = jnp.clip(wanted, 0, devices - 1)
    chosen = pick_pieces(wanted, held)
    far = lax.all_to_all(chosen, "ctx", split_axis=0, concat_axis=0, tiled=True)
    far = far.reshape(devices, 2, SLOTS, piece_rows, HEAD_SIZE)
    if piece_rows % 16 != 0:
        far = far.transpose(1, 2, 0, 3, 4).reshape(1, 2, SLOTS, rows, HEAD_SIZE)
    return far_attention(selected, queries, own, level, far)


def solution(mesh):
    placed = P(("groups", "ctx"), None)
    return jax.shard_map(
        local, mesh=mesh, in_specs=(placed,) * 4, out_specs=placed, check_vma=False
    )
```

```python
import math

import jax
import jax.numpy as jnp
from jax import lax
from jax.experimental import pallas as pl
from jax.experimental.pallas import tpu as pltpu
from jax.sharding import PartitionSpec as P

QUERY_HEADS = 32
KEY_VALUE_HEADS = 4
HEAD_SIZE = 128
GROUP = QUERY_HEADS // KEY_VALUE_HEADS
SLOTS = 2 * KEY_VALUE_HEADS
REQUEST_ROWS = 16
MIB = 1024 * 1024


def pack_kernel(selected_ref, key_ref, value_ref, out_ref):
    devices, piece_rows = out_ref.shape[0], key_ref.shape[0] // out_ref.shape[0]
    for slot in range(SLOTS):
        ref = key_ref if slot < KEY_VALUE_HEADS else value_ref
        head = slot % KEY_VALUE_HEADS
        part = ref[:, head * HEAD_SIZE : (head + 1) * HEAD_SIZE]
        out_ref[:, slot * piece_rows : (slot + 1) * piece_rows, :] = part.reshape(
            devices, piece_rows, HEAD_SIZE
        )
    lane = lax.broadcasted_iota(jnp.int32, (devices, REQUEST_ROWS, HEAD_SIZE), 2)
    request = jnp.where(lane == 0, selected_ref[0, 0], selected_ref[0, 1])
    out_ref[:, SLOTS * piece_rows :, :] = request.astype(jnp.float32).astype(jnp.bfloat16)


def pack(keys, values, selected, devices):
    rows = keys.shape[0]
    piece_rows = rows // devices
    shape = (devices, SLOTS * piece_rows + REQUEST_ROWS, HEAD_SIZE)
    if piece_rows % 16 == 0:
        return pl.pallas_call(
            pack_kernel,
            out_shape=pltpu.VMEM(shape, jnp.bfloat16),
            in_specs=[
                pl.BlockSpec(memory_space=pltpu.SMEM),
                pl.BlockSpec(memory_space=pltpu.VMEM),
                pl.BlockSpec(memory_space=pltpu.VMEM),
            ],
            out_specs=pl.BlockSpec(memory_space=pltpu.VMEM),
            name="pack",
        )(selected, keys, values)
    both = jnp.concatenate([keys, values], axis=1)
    both = both.reshape(devices, piece_rows, SLOTS, HEAD_SIZE).transpose(0, 2, 1, 3)
    both = both.reshape(devices, SLOTS * piece_rows, HEAD_SIZE)
    lane = jnp.arange(HEAD_SIZE) == 0
    request = jnp.where(lane, selected[0, 0], selected[0, 1]).astype(jnp.bfloat16)
    request = jnp.broadcast_to(request, (devices, REQUEST_ROWS, HEAD_SIZE))
    return jnp.concatenate([both, request], axis=1)


def pick_kernel(wanted_ref, held_ref, out_ref):
    rows = out_ref.shape[2]

    @pl.loop(0, out_ref.shape[0])
    def _(device):
        for pick in range(2):
            out_ref[device, pick] = held_ref[wanted_ref[device, pick], :rows, :]


def pick_pieces(wanted, held):
    devices, rows = held.shape[0], held.shape[1] - REQUEST_ROWS
    return pl.pallas_call(
        pick_kernel,
        out_shape=pltpu.VMEM((devices, 2, rows, HEAD_SIZE), jnp.bfloat16),
        in_specs=[
            pl.BlockSpec(memory_space=pltpu.SMEM),
            pl.BlockSpec(memory_space=pltpu.VMEM),
        ],
        out_specs=pl.BlockSpec(memory_space=pltpu.VMEM),
        compiler_params=pltpu.CompilerParams(vmem_limit_bytes=16 * MIB),
        name="pick_pieces",
    )(wanted, held)


HEADS_AT_ONCE = 1
FACTOR = math.log2(math.e) / math.sqrt(HEAD_SIZE)
LARGE_SUM = 2.0**100


def head_lanes(head):
    return slice(head * HEAD_SIZE, (head + 1) * HEAD_SIZE)


def with_ones(value):
    return jnp.concatenate([value, jnp.ones_like(value)], axis=1)


def inverse_of(positive):
    return pl.reciprocal(positive, approx=True)


def stacked_queries(query_ref, first):
    heads = range(first, first + HEADS_AT_ONCE)
    return jnp.concatenate([query_ref[:, head_lanes(h)] for h in heads], axis=0)


def staggered(steps, score, finish):
    scores = score(steps[0])
    for step, later in zip(steps, steps[1:] + [None]):
        following = None if later is None else score(later)
        finish(step, scores)
        scores = following


STEPS = list(range(0, GROUP, HEADS_AT_ONCE))


def own_kernel(query_ref, key_ref, value_ref, out_ref, level_ref):
    rows = query_ref.shape[0]
    row = lax.broadcasted_iota(jnp.int32, (rows, rows), 0)
    column = lax.broadcasted_iota(jnp.int32, (rows, rows), 1)
    causal = column <= row
    lane = lax.broadcasted_iota(jnp.int32, (rows, HEAD_SIZE), 1)
    keys_across = key_ref[...].T
    value = with_ones(value_ref[...])

    def score(first):
        return jnp.dot(
            stacked_queries(query_ref, first), keys_across, preferred_element_type=jnp.float32
        )

    def finish(first, scores):
        weights, shifts = [], []
        for h in range(HEADS_AT_ONCE):
            part = jnp.where(causal, scores[h * rows : (h + 1) * rows], -1e30)
            shift = jnp.max(part, axis=1, keepdims=True) * FACTOR
            shifts.append(shift)
            weights.append(jnp.exp2(part * FACTOR - shift).astype(jnp.bfloat16))
        both = jnp.dot(
            jnp.concatenate(weights, axis=0), value, preferred_element_type=jnp.float32
        )
        for h in range(HEADS_AT_ONCE):
            part = both[h * rows : (h + 1) * rows]
            row_sum = part[:, HEAD_SIZE:]
            out_ref[:, head_lanes(first + h)] = part[:, :HEAD_SIZE] * inverse_of(row_sum)
            level = shifts[h] + jnp.log2(row_sum)
            level_ref[...] = jnp.where(lane == first + h, level, level_ref[...])

    level_ref[...] = jnp.zeros_like(level_ref)
    staggered(STEPS, score, finish)


def own_attention(queries, keys, values):
    rows = queries.shape[0]
    width = GROUP * HEAD_SIZE
    scores = QUERY_HEADS * rows * rows
    return pl.pallas_call(
        own_kernel,
        out_shape=[
            pltpu.HBM(queries.shape, jnp.float32),
            pltpu.HBM((rows, KEY_VALUE_HEADS * HEAD_SIZE), jnp.float32),
        ],
        grid=(KEY_VALUE_HEADS,),
        in_specs=[
            pl.BlockSpec((rows, width), lambda g: (0, g)),
            pl.BlockSpec((rows, HEAD_SIZE), lambda g: (0, g)),
            pl.BlockSpec((rows, HEAD_SIZE), lambda g: (0, g)),
        ],
        out_specs=[
            pl.BlockSpec((rows, width), lambda g: (0, g)),
            pl.BlockSpec((rows, HEAD_SIZE), lambda g: (0, g)),
        ],
        compiler_params=pltpu.CompilerParams(vmem_limit_bytes=24 * MIB),
        cost_estimate=pl.CostEstimate(
            flops=4 * scores * HEAD_SIZE, bytes_accessed=7 * MIB, transcendentals=scores
        ),
        name="own_attention",
    )(queries, keys, values)


def far_kernel(
    selected_ref, query_ref, far_ref, own_hbm, level_hbm, out_ref, own_ref, level_ref, staged, sems
):
    rows = query_ref.shape[0]
    width = GROUP * HEAD_SIZE

    def lanes(group, size):
        start = group * size
        return pl.ds(start if isinstance(group, int) else pl.multiple_of(start, size), size)

    def fetch(group):
        wide, narrow = lanes(group, width), lanes(group, HEAD_SIZE)
        return (
            pltpu.make_async_copy(own_hbm.at[:, wide], own_ref.at[group], sems.at[0, group]),
            pltpu.make_async_copy(level_hbm.at[:, narrow], level_ref.at[group], sems.at[1, group]),
        )

    def send(group):
        out = out_ref.at[:, lanes(group, width)]
        return pltpu.make_async_copy(staged.at[group], out, sems.at[2, group])

    for group in range(KEY_VALUE_HEADS):
        for copy in fetch(group):
            copy.start()

    def arrive(group):
        for copy in fetch(group):
            copy.wait()

    def block(slot, picks):
        blocks = [far_ref[:, p, slot].reshape(rows, HEAD_SIZE) for p in picks]
        return jnp.concatenate(blocks, axis=0)

    def keys_and_values(group, picks):
        return block(group, picks).T, with_ones(block(group + KEY_VALUE_HEADS, picks))

    def score(group, head, keys_across):
        query = stacked_queries(query_ref.at[:, lanes(group, width)], head)
        return jnp.dot(query, keys_across, preferred_element_type=jnp.float32)

    def quick(group, head, scores, value, largest):
        weights = []
        for h in range(HEADS_AT_ONCE):
            part = scores[h * rows : (h + 1) * rows]
            mine = level_ref[group, :, head + h : head + h + 1]
            weights.append(jnp.exp2(part * FACTOR - mine).astype(jnp.bfloat16))
        both = jnp.dot(
            jnp.concatenate(weights, axis=0), value, preferred_element_type=jnp.float32
        )
        for h in range(HEADS_AT_ONCE):
            part = both[h * rows : (h + 1) * rows]
            row_sum = 1.0 + part[:, HEAD_SIZE:]
            largest = jnp.maximum(
                largest, jnp.max(row_sum.reshape(rows // 8, 8, HEAD_SIZE), axis=0)
            )
            mixture = own_ref[group, :, head_lanes(head + h)] + part[:, :HEAD_SIZE]
            staged[group, :, head_lanes(head + h)] = (mixture * inverse_of(row_sum)).astype(
                staged.dtype
            )
        return largest

    def careful(group, head, scores, value):
        for h in range(HEADS_AT_ONCE):
            part = scores[h * rows : (h + 1) * rows] * FACTOR
            mine = level_ref[group, :, head + h : head + h + 1]
            shift = jnp.maximum(jnp.max(part, axis=1, keepdims=True), mine)
            weights = jnp.exp2(part - shift).astype(jnp.bfloat16)
            both = jnp.dot(weights, value, preferred_element_type=jnp.float32)
            share = jnp.exp2(mine - shift)
            mixture = own_ref[group, :, head_lanes(head + h)] * share + both[:, :HEAD_SIZE]
            staged[group, :, head_lanes(head + h)] = (
                mixture * inverse_of(share + both[:, HEAD_SIZE:])
            ).astype(staged.dtype)

    nothing = jnp.zeros((8, HEAD_SIZE), jnp.float32)

    def attend_quickly(picks):
        held = {}
        largest = nothing

        def start(step):
            group, head = step
            if head == 0:
                held[group] = keys_and_values(group, picks)
            return score(group, head, held[group][0])

        def finish(step, scores):
            nonlocal largest
            group, head = step
            if head == 0:
                arrive(group)
            largest = quick(group, head, scores, held[group][1], largest)
            if head == STEPS[-1]:
                send(group).start()

        staggered([(g, h) for g in range(KEY_VALUE_HEADS) for h in STEPS], start, finish)
        return jnp.max(largest)

    def attend_carefully(picks):
        @pl.loop(0, KEY_VALUE_HEADS)
        def _(group):
            send(group).wait()
            keys_across, value = keys_and_values(group, picks)
            for head in STEPS:
                careful(group, head, score(group, head, keys_across), value)
            send(group).start()

    def attend(picks):
        largest = attend_quickly(picks)

        @pl.when(largest > LARGE_SUM)
        def _():
            attend_carefully(picks)

    my_block = lax.axis_index("ctx")
    chosen = selected_ref[0, 0], selected_ref[0, 1]
    first = chosen[0] < my_block
    second = jnp.logical_and(chosen[1] < my_block, chosen[1] != chosen[0])
    count = first.astype(jnp.int32) + second.astype(jnp.int32)

    @pl.when(count == 2)
    def _():
        attend((0, 1))

    @pl.when(count == 1)
    def _():
        attend((second.astype(jnp.int32),))

    @pl.when(count == 0)
    def _():
        for group in range(KEY_VALUE_HEADS):
            arrive(group)
            staged[group] = own_ref[group].astype(staged.dtype)
            send(group).start()

    for group in range(KEY_VALUE_HEADS):
        send(group).wait()


def far_attention(selected, queries, own, level, far):
    rows = queries.shape[0]
    scores = QUERY_HEADS * rows * 2 * rows
    own = pltpu.with_memory_space_constraint(own, pltpu.HBM)
    level = pltpu.with_memory_space_constraint(level, pltpu.HBM)
    return pl.pallas_call(
        far_kernel,
        out_shape=jax.ShapeDtypeStruct(queries.shape, jnp.bfloat16),
        in_specs=[
            pl.BlockSpec(memory_space=pltpu.SMEM),
            *[pl.BlockSpec(memory_space=pltpu.VMEM)] * 2,
            *[pl.BlockSpec(memory_space=pl.ANY)] * 2,
        ],
        out_specs=pl.BlockSpec(memory_space=pl.ANY),
        scratch_shapes=[
            pltpu.VMEM((KEY_VALUE_HEADS, rows, GROUP * HEAD_SIZE), jnp.float32),
            pltpu.VMEM((KEY_VALUE_HEADS, rows, HEAD_SIZE), jnp.float32),
            pltpu.VMEM((KEY_VALUE_HEADS, rows, GROUP * HEAD_SIZE), jnp.bfloat16),
            pltpu.SemaphoreType.DMA((3, KEY_VALUE_HEADS)),
        ],
        compiler_params=pltpu.CompilerParams(vmem_limit_bytes=28 * MIB),
        cost_estimate=pl.CostEstimate(
            flops=4 * scores * HEAD_SIZE, bytes_accessed=10 * MIB, transcendentals=scores
        ),
        name="far_attention",
    )(selected, queries, far, own, level)


def local(queries, all_key_states, all_value_states, selected):
    devices = lax.axis_size("ctx")
    rows = all_key_states.shape[0]
    piece_rows = rows // devices
    packed = pack(all_key_states, all_value_states, selected, devices)
    held = lax.all_to_all(packed, "ctx", split_axis=0, concat_axis=0, tiled=True)
    own, level = own_attention(queries, all_key_states, all_value_states)
    wanted = held[:, SLOTS * piece_rows, :2].astype(jnp.int32)
    wanted = jnp.clip(wanted, 0, devices - 1)
    chosen = pick_pieces(wanted, held)
    far = lax.all_to_all(chosen, "ctx", split_axis=0, concat_axis=0, tiled=True)
    far = far.reshape(devices, 2, SLOTS, piece_rows, HEAD_SIZE)
    if piece_rows % 16 != 0:
        far = far.transpose(1, 2, 0, 3, 4).reshape(1, 2, SLOTS, rows, HEAD_SIZE)
    return far_attention(selected, queries, own, level, far)


def solution(mesh):
    placed = P(("groups", "ctx"), None)
    return jax.shard_map(
        local, mesh=mesh, in_specs=(placed,) * 4, out_specs=placed, check_vma=False
    )
```

```python
import math

import jax
import jax.numpy as jnp
from jax import lax
from jax.experimental import pallas as pl
from jax.experimental.pallas import tpu as pltpu
from jax.sharding import PartitionSpec as P

QUERY_HEADS = 32
KEY_VALUE_HEADS = 4
HEAD_SIZE = 128
GROUP = QUERY_HEADS // KEY_VALUE_HEADS
SLOTS = 2 * KEY_VALUE_HEADS
REQUEST_ROWS = 16
MIB = 1024 * 1024


def pack_kernel(selected_ref, key_ref, value_ref, out_ref):
    devices, piece_rows = out_ref.shape[0], key_ref.shape[0] // out_ref.shape[0]
    for slot in range(SLOTS):
        ref = key_ref if slot < KEY_VALUE_HEADS else value_ref
        head = slot % KEY_VALUE_HEADS
        part = ref[:, head * HEAD_SIZE : (head + 1) * HEAD_SIZE]
        out_ref[:, slot * piece_rows : (slot + 1) * piece_rows, :] = part.reshape(
            devices, piece_rows, HEAD_SIZE
        )
    lane = lax.broadcasted_iota(jnp.int32, (devices, REQUEST_ROWS, HEAD_SIZE), 2)
    request = jnp.where(lane == 0, selected_ref[0, 0], selected_ref[0, 1])
    out_ref[:, SLOTS * piece_rows :, :] = request.astype(jnp.float32).astype(jnp.bfloat16)


def pack(keys, values, selected, devices):
    rows = keys.shape[0]
    piece_rows = rows // devices
    shape = (devices, SLOTS * piece_rows + REQUEST_ROWS, HEAD_SIZE)
    if piece_rows % 16 == 0:
        return pl.pallas_call(
            pack_kernel,
            out_shape=pltpu.VMEM(shape, jnp.bfloat16),
            in_specs=[
                pl.BlockSpec(memory_space=pltpu.SMEM),
                pl.BlockSpec(memory_space=pltpu.VMEM),
                pl.BlockSpec(memory_space=pltpu.VMEM),
            ],
            out_specs=pl.BlockSpec(memory_space=pltpu.VMEM),
            name="pack",
        )(selected, keys, values)
    both = jnp.concatenate([keys, values], axis=1)
    both = both.reshape(devices, piece_rows, SLOTS, HEAD_SIZE).transpose(0, 2, 1, 3)
    both = both.reshape(devices, SLOTS * piece_rows, HEAD_SIZE)
    lane = jnp.arange(HEAD_SIZE) == 0
    request = jnp.where(lane, selected[0, 0], selected[0, 1]).astype(jnp.bfloat16)
    request = jnp.broadcast_to(request, (devices, REQUEST_ROWS, HEAD_SIZE))
    return jnp.concatenate([both, request], axis=1)


def pick_kernel(wanted_ref, held_ref, out_ref):
    rows = out_ref.shape[2]

    @pl.loop(0, out_ref.shape[0])
    def _(device):
        for pick in range(2):
            out_ref[device, pick] = held_ref[wanted_ref[device, pick], :rows, :]


def pick_pieces(wanted, held):
    devices, rows = held.shape[0], held.shape[1] - REQUEST_ROWS
    return pl.pallas_call(
        pick_kernel,
        out_shape=pltpu.VMEM((devices, 2, rows, HEAD_SIZE), jnp.bfloat16),
        in_specs=[
            pl.BlockSpec(memory_space=pltpu.SMEM),
            pl.BlockSpec(memory_space=pltpu.VMEM),
        ],
        out_specs=pl.BlockSpec(memory_space=pltpu.VMEM),
        compiler_params=pltpu.CompilerParams(vmem_limit_bytes=16 * MIB),
        name="pick_pieces",
    )(wanted, held)


FACTOR = math.log2(math.e) / math.sqrt(HEAD_SIZE)
PAIR = 2
LARGE_SUM = 2.0**100


def head_lanes(head):
    return slice(head * HEAD_SIZE, (head + 1) * HEAD_SIZE)


def with_ones(value):
    return jnp.concatenate([value, jnp.ones_like(value)], axis=1)


def inverse_of(positive):
    return pl.reciprocal(positive, approx=True)


def dot(a, b):
    return jnp.dot(a, b, preferred_element_type=jnp.float32)


def stack_heads(wide):
    heads = wide.shape[1] // HEAD_SIZE
    return jnp.concatenate([wide[:, head_lanes(h)] for h in range(heads)], axis=0)


def own_kernel(query_ref, key_ref, value_ref, out_ref, level_ref):
    rows = query_ref.shape[0]
    row = lax.broadcasted_iota(jnp.int32, (rows, rows), 0)
    column = lax.broadcasted_iota(jnp.int32, (rows, rows), 1)
    causal = column <= row
    keys_across = key_ref[...].T
    value = with_ones(value_ref[...])

    def score(first):
        lanes = slice(first * HEAD_SIZE, (first + PAIR) * HEAD_SIZE)
        return dot(stack_heads(query_ref[:, lanes]), keys_across)

    def finish(first, scores):
        weights, shifts = [], []
        for h in range(PAIR):
            part = jnp.where(causal, scores[h * rows : (h + 1) * rows], -1e30)
            shift = jnp.max(part, axis=1, keepdims=True) * FACTOR
            shifts.append(shift)
            weights.append(jnp.exp2(part * FACTOR - shift).astype(jnp.bfloat16))
        both = dot(jnp.concatenate(weights, axis=0), value)
        for h in range(PAIR):
            part = both[h * rows : (h + 1) * rows]
            row_sum = part[:, HEAD_SIZE:]
            out_ref[:, head_lanes(first + h)] = part[:, :HEAD_SIZE] / row_sum
            level_ref[:, head_lanes(first + h)] = shifts[h] + jnp.log2(row_sum)

    scores = score(0)
    for first in range(0, GROUP, PAIR):
        following = score(first + PAIR) if first + PAIR < GROUP else None
        finish(first, scores)
        scores = following


def own_attention(queries, keys, values):
    rows = queries.shape[0]
    width = GROUP * HEAD_SIZE
    scores = QUERY_HEADS * rows * rows
    return pl.pallas_call(
        own_kernel,
        out_shape=[pltpu.VMEM(queries.shape, jnp.float32)] * 2,
        grid=(KEY_VALUE_HEADS,),
        in_specs=[
            pl.BlockSpec((rows, width), lambda g: (0, g)),
            pl.BlockSpec((rows, HEAD_SIZE), lambda g: (0, g)),
            pl.BlockSpec((rows, HEAD_SIZE), lambda g: (0, g)),
        ],
        out_specs=[pl.BlockSpec((rows, width), lambda g: (0, g))] * 2,
        compiler_params=pltpu.CompilerParams(vmem_limit_bytes=16 * MIB),
        cost_estimate=pl.CostEstimate(
            flops=4 * scores * HEAD_SIZE, bytes_accessed=11 * MIB, transcendentals=scores
        ),
        name="own_attention",
    )(queries, keys, values)


def far_kernel(
    selected_ref,
    query_ref,
    far_ref,
    own_ref,
    level_ref,
    out_ref,
    keys_ref,
    values_ref,
    scores_ref,
    other_scores_ref,
    staged,
    sems,
):
    rows = query_ref.shape[0]
    pair_width = PAIR * HEAD_SIZE
    step_width = 2 * pair_width
    steps = query_ref.shape[1] // step_width
    steps_of_group = steps // KEY_VALUE_HEADS

    def lanes(index, size):
        return pl.ds(pl.multiple_of(index * size, size), size)

    def send(step):
        out = out_ref.at[:, lanes(step, step_width)]
        return pltpu.make_async_copy(staged.at[step], out, sems.at[step])

    def finish_own(step):
        staged[step] = own_ref[:, lanes(step, step_width)].astype(staged.dtype)

    def attend(picks):
        count = len(picks) * rows

        def block(slot):
            blocks = [far_ref[:, p, slot].reshape(rows, HEAD_SIZE) for p in picks]
            return jnp.concatenate(blocks, axis=0)

        @pl.loop(0, KEY_VALUE_HEADS)
        def _(group):
            keys_ref[group, :, :count] = block(group).T
            values_ref[group, :count] = with_ones(block(group + KEY_VALUE_HEADS))

        def score(pair, group, buffer):
            query = stack_heads(query_ref[:, lanes(pair, pair_width)])
            buffer[:, :count] = dot(query, keys_ref[group, :, :count])

        def repeat(narrow):
            return jnp.concatenate([narrow] * (count // HEAD_SIZE), axis=1)

        def quick(pair, group, buffer, step, half, largest):
            level = level_ref[:, lanes(pair, pair_width)]
            own = own_ref[:, lanes(pair, pair_width)]
            weights = [
                jnp.exp2(
                    buffer[h * rows : (h + 1) * rows, :count] * FACTOR
                    - repeat(level[:, head_lanes(h)])
                ).astype(jnp.bfloat16)
                for h in range(PAIR)
            ]
            both = dot(jnp.concatenate(weights, axis=0), values_ref[group, :count])
            for h in range(PAIR):
                part = both[h * rows : (h + 1) * rows]
                row_sum = 1.0 + part[:, HEAD_SIZE:]
                largest = jnp.maximum(
                    largest, jnp.max(row_sum.reshape(rows // 8, 8, HEAD_SIZE), axis=0)
                )
                mixture = own[:, head_lanes(h)] + part[:, :HEAD_SIZE]
                staged[step, :, head_lanes(half * PAIR + h)] = (
                    mixture * inverse_of(row_sum)
                ).astype(staged.dtype)
            return largest

        def careful(pair, group, buffer, step, half):
            score(pair, group, buffer)
            level = level_ref[:, lanes(pair, pair_width)]
            own = own_ref[:, lanes(pair, pair_width)]
            for h in range(PAIR):
                part = buffer[h * rows : (h + 1) * rows, :count] * FACTOR
                mine = level[:, head_lanes(h)]
                shift = jnp.maximum(jnp.max(part, axis=1, keepdims=True), mine)
                weights = jnp.exp2(part - repeat(shift)).astype(jnp.bfloat16)
                both = dot(weights, values_ref[group, :count])
                share = jnp.exp2(mine - shift)
                mixture = own[:, head_lanes(h)] * share + both[:, :HEAD_SIZE]
                staged[step, :, head_lanes(half * PAIR + h)] = (
                    mixture * inverse_of(share + both[:, HEAD_SIZE:])
                ).astype(staged.dtype)

        def body(step, largest):
            group = step // steps_of_group
            following = jnp.minimum(step + 1, steps - 1)
            score(2 * step + 1, group, other_scores_ref)
            largest = quick(2 * step, group, scores_ref, step, 0, largest)
            score(2 * following, following // steps_of_group, scores_ref)
            largest = quick(2 * step + 1, group, other_scores_ref, step, 1, largest)
            send(step).start()
            return largest

        score(0, 0, scores_ref)
        largest = lax.fori_loop(0, steps, body, jnp.zeros((8, HEAD_SIZE), jnp.float32))

        @pl.when(jnp.max(largest) > LARGE_SUM)
        def _():
            @pl.loop(0, steps)
            def _(step):
                send(step).wait()
                for half in range(2):
                    careful(2 * step + half, step // steps_of_group, scores_ref, step, half)
                send(step).start()

    my_block = lax.axis_index("ctx")
    chosen = selected_ref[0, 0], selected_ref[0, 1]
    first = chosen[0] < my_block
    second = jnp.logical_and(chosen[1] < my_block, chosen[1] != chosen[0])
    valid = first.astype(jnp.int32) + second.astype(jnp.int32)

    @pl.when(valid == 2)
    def _():
        attend((0, 1))

    @pl.when(valid == 1)
    def _():
        attend((second.astype(jnp.int32),))

    @pl.when(valid == 0)
    def _():
        @pl.loop(0, steps)
        def _(step):
            finish_own(step)
            send(step).start()

    @pl.loop(0, steps)
    def _(step):
        send(step).wait()


def far_attention(selected, queries, own, level, far):
    rows = queries.shape[0]
    scores = QUERY_HEADS * rows * 2 * rows
    step_width = 2 * PAIR * HEAD_SIZE
    steps = queries.shape[1] // step_width
    own = pltpu.with_memory_space_constraint(own, pltpu.VMEM)
    level = pltpu.with_memory_space_constraint(level, pltpu.VMEM)
    return pl.pallas_call(
        far_kernel,
        out_shape=jax.ShapeDtypeStruct(queries.shape, jnp.bfloat16),
        in_specs=[
            pl.BlockSpec(memory_space=pltpu.SMEM),
            *[pl.BlockSpec(memory_space=pltpu.VMEM)] * 4,
        ],
        out_specs=pl.BlockSpec(memory_space=pl.ANY),
        scratch_shapes=[
            pltpu.VMEM((KEY_VALUE_HEADS, HEAD_SIZE, 2 * rows), jnp.bfloat16),
            pltpu.VMEM((KEY_VALUE_HEADS, 2 * rows, 2 * HEAD_SIZE), jnp.bfloat16),
            pltpu.VMEM((PAIR * rows, 2 * rows), jnp.float32),
            pltpu.VMEM((PAIR * rows, 2 * rows), jnp.float32),
            pltpu.VMEM((steps, rows, step_width), jnp.bfloat16),
            pltpu.SemaphoreType.DMA((steps,)),
        ],
        compiler_params=pltpu.CompilerParams(vmem_limit_bytes=24 * MIB),
        cost_estimate=pl.CostEstimate(
            flops=4 * scores * HEAD_SIZE, bytes_accessed=10 * MIB, transcendentals=scores
        ),
        name="far_attention",
    )(selected, queries, far, own, level)


def local(queries, all_key_states, all_value_states, selected):
    devices = lax.axis_size("ctx")
    rows = all_key_states.shape[0]
    piece_rows = rows // devices
    packed = pack(all_key_states, all_value_states, selected, devices)
    held = lax.all_to_all(packed, "ctx", split_axis=0, concat_axis=0, tiled=True)
    own, level = own_attention(queries, all_key_states, all_value_states)
    wanted = held[:, SLOTS * piece_rows, :2].astype(jnp.int32)
    wanted = jnp.clip(wanted, 0, devices - 1)
    chosen = pick_pieces(wanted, held)
    far = lax.all_to_all(chosen, "ctx", split_axis=0, concat_axis=0, tiled=True)
    far = far.reshape(devices, 2, SLOTS, piece_rows, HEAD_SIZE)
    if piece_rows % 16 != 0:
        far = far.transpose(1, 2, 0, 3, 4).reshape(1, 2, SLOTS, rows, HEAD_SIZE)
    return far_attention(selected, queries, own, level, far)


def solution(mesh):
    placed = P(("groups", "ctx"), None)
    return jax.shard_map(
        local, mesh=mesh, in_specs=(placed,) * 4, out_specs=placed, check_vma=False
    )
```

```python
import math

import jax
import jax.numpy as jnp
from jax import lax
from jax.experimental import pallas as pl
from jax.experimental.pallas import tpu as pltpu
from jax.sharding import PartitionSpec as P

QUERY_HEADS = 32
KEY_VALUE_HEADS = 4
HEAD_SIZE = 128
GROUP = QUERY_HEADS // KEY_VALUE_HEADS
SLOTS = 2 * KEY_VALUE_HEADS
REQUEST_ROWS = 16
COPIES = 2
MIB = 1024 * 1024


def pack_kernel(selected_ref, key_ref, value_ref, out_ref):
    devices = out_ref.shape[0]
    shares = devices // COPIES
    piece_rows = key_ref.shape[0] // shares
    for slot in range(SLOTS):
        ref = key_ref if slot < KEY_VALUE_HEADS else value_ref
        head = slot % KEY_VALUE_HEADS
        part = ref[:, head * HEAD_SIZE : (head + 1) * HEAD_SIZE]
        part = part.reshape(shares, piece_rows, HEAD_SIZE)
        for copy in range(COPIES):
            out_ref[
                copy * shares : (copy + 1) * shares,
                slot * piece_rows : (slot + 1) * piece_rows,
                :,
            ] = part
    lane = lax.broadcasted_iota(jnp.int32, (devices, REQUEST_ROWS, HEAD_SIZE), 2)
    request = jnp.where(lane == 0, selected_ref[0, 0], selected_ref[0, 1])
    out_ref[:, SLOTS * piece_rows :, :] = request.astype(jnp.float32).astype(jnp.bfloat16)


def pack(keys, values, selected, devices):
    shares = devices // COPIES
    piece_rows = keys.shape[0] // shares
    shape = (devices, SLOTS * piece_rows + REQUEST_ROWS, HEAD_SIZE)
    if piece_rows % 16 == 0:
        return pl.pallas_call(
            pack_kernel,
            out_shape=pltpu.VMEM(shape, jnp.bfloat16),
            in_specs=[
                pl.BlockSpec(memory_space=pltpu.SMEM),
                pl.BlockSpec(memory_space=pltpu.VMEM),
                pl.BlockSpec(memory_space=pltpu.VMEM),
            ],
            out_specs=pl.BlockSpec(memory_space=pltpu.VMEM),
            name="pack",
        )(selected, keys, values)
    both = jnp.concatenate([keys, values], axis=1)
    both = both.reshape(shares, piece_rows, SLOTS, HEAD_SIZE).transpose(0, 2, 1, 3)
    both = both.reshape(shares, SLOTS * piece_rows, HEAD_SIZE)
    lane = jnp.arange(HEAD_SIZE) == 0
    request = jnp.where(lane, selected[0, 0], selected[0, 1]).astype(jnp.bfloat16)
    request = jnp.broadcast_to(request, (shares, REQUEST_ROWS, HEAD_SIZE))
    return jnp.concatenate([jnp.concatenate([both, request], axis=1)] * COPIES, axis=0)


def partner(position, step):
    return position ^ step


def pick_kernel(wanted_ref, held_ref, *out_refs):
    rows = out_refs[0].shape[1]
    me = lax.axis_index("ctx")
    for step, out_ref in enumerate(out_refs):
        device = partner(me, step)
        for pick in range(2):
            out_ref[pick] = held_ref[wanted_ref[device, pick], :rows, :]


def pick_pieces(wanted, held):
    devices, rows = held.shape[0], held.shape[1] - REQUEST_ROWS
    shares = devices // COPIES
    return pl.pallas_call(
        pick_kernel,
        out_shape=[jax.ShapeDtypeStruct((2, rows, HEAD_SIZE), jnp.bfloat16)] * shares,
        in_specs=[
            pl.BlockSpec(memory_space=pltpu.SMEM),
            pl.BlockSpec(memory_space=pltpu.VMEM),
        ],
        out_specs=[pl.BlockSpec(memory_space=pltpu.VMEM)] * shares,
        compiler_params=pltpu.CompilerParams(vmem_limit_bytes=16 * MIB),
        name="pick_pieces",
    )(wanted, held)


def deliver(pieces, devices):
    moved = [pieces[0]] + [None] * (len(pieces) - 1)
    for step in reversed(range(1, len(pieces))):
        pairs = [(i, partner(i, step)) for i in range(devices)]
        moved[step] = lax.ppermute(pieces[step], "ctx", pairs)
    return moved


HEADS_AT_ONCE = 2
FACTOR = math.log2(math.e) / math.sqrt(HEAD_SIZE)
LARGE_SUM = 2.0**100


def head_lanes(head):
    return slice(head * HEAD_SIZE, (head + 1) * HEAD_SIZE)


def with_ones(value):
    return jnp.concatenate([value, jnp.ones_like(value)], axis=1)


def inverse_of(positive):
    return pl.reciprocal(positive, approx=True)


def stacked_queries(query_ref, first):
    heads = range(first, first + HEADS_AT_ONCE)
    return jnp.concatenate([query_ref[:, head_lanes(h)] for h in heads], axis=0)


def staggered(steps, score, finish):
    scores = score(steps[0])
    for step, later in zip(steps, steps[1:] + [None]):
        following = None if later is None else score(later)
        finish(step, scores)
        scores = following


STEPS = list(range(0, GROUP, HEADS_AT_ONCE))


def own_kernel(query_ref, key_ref, value_ref, out_ref, level_ref):
    rows = query_ref.shape[0]
    row = lax.broadcasted_iota(jnp.int32, (rows, rows), 0)
    column = lax.broadcasted_iota(jnp.int32, (rows, rows), 1)
    causal = column <= row
    lane = lax.broadcasted_iota(jnp.int32, (rows, HEAD_SIZE), 1)
    keys_across = key_ref[...].T
    value = with_ones(value_ref[...])

    def score(first):
        return jnp.dot(
            stacked_queries(query_ref, first), keys_across, preferred_element_type=jnp.float32
        )

    def finish(first, scores):
        weights, shifts = [], []
        for h in range(HEADS_AT_ONCE):
            part = jnp.where(causal, scores[h * rows : (h + 1) * rows], -1e30)
            shift = jnp.max(part, axis=1, keepdims=True) * FACTOR
            shifts.append(shift)
            weights.append(jnp.exp2(part * FACTOR - shift).astype(jnp.bfloat16))
        both = jnp.dot(
            jnp.concatenate(weights, axis=0), value, preferred_element_type=jnp.float32
        )
        for h in range(HEADS_AT_ONCE):
            part = both[h * rows : (h + 1) * rows]
            row_sum = part[:, HEAD_SIZE:]
            out_ref[:, head_lanes(first + h)] = part[:, :HEAD_SIZE] * inverse_of(row_sum)
            level = shifts[h] + jnp.log2(row_sum)
            level_ref[...] = jnp.where(lane == first + h, level, level_ref[...])

    level_ref[...] = jnp.zeros_like(level_ref)
    staggered(STEPS, score, finish)


def own_attention(queries, keys, values):
    rows = queries.shape[0]
    width = GROUP * HEAD_SIZE
    scores = QUERY_HEADS * rows * rows
    return pl.pallas_call(
        own_kernel,
        out_shape=[
            pltpu.HBM(queries.shape, jnp.float32),
            pltpu.HBM((rows, KEY_VALUE_HEADS * HEAD_SIZE), jnp.float32),
        ],
        grid=(KEY_VALUE_HEADS,),
        in_specs=[
            pl.BlockSpec((rows, width), lambda g: (0, g)),
            pl.BlockSpec((rows, HEAD_SIZE), lambda g: (0, g)),
            pl.BlockSpec((rows, HEAD_SIZE), lambda g: (0, g)),
        ],
        out_specs=[
            pl.BlockSpec((rows, width), lambda g: (0, g)),
            pl.BlockSpec((rows, HEAD_SIZE), lambda g: (0, g)),
        ],
        compiler_params=pltpu.CompilerParams(vmem_limit_bytes=24 * MIB),
        cost_estimate=pl.CostEstimate(
            flops=4 * scores * HEAD_SIZE, bytes_accessed=7 * MIB, transcendentals=scores
        ),
        name="own_attention",
    )(queries, keys, values)


def far_kernel(selected_ref, query_ref, own_hbm, level_hbm, *refs):
    *far_refs, out_ref, own_ref, level_ref, staged, sems = refs
    rows = query_ref.shape[0]
    width = GROUP * HEAD_SIZE

    def lanes(group, size):
        start = group * size
        return pl.ds(start if isinstance(group, int) else pl.multiple_of(start, size), size)

    def fetch(group, which):
        size, source, target = (
            (width, own_hbm, own_ref) if which == 0 else (HEAD_SIZE, level_hbm, level_ref)
        )
        part = source.at[:, lanes(group, size)]
        return pltpu.make_async_copy(part, target.at[group], sems.at[which, group])

    def send(group):
        out = out_ref.at[:, lanes(group, width)]
        return pltpu.make_async_copy(staged.at[group], out, sems.at[2, group])

    for group in range(KEY_VALUE_HEADS):
        fetch(group, 1).start()
        fetch(group, 0).start()

    def arrive(group, which):
        fetch(group, which).wait()

    def block(slot, picks):
        return jnp.concatenate([ref[p, slot] for p in picks for ref in far_refs], axis=0)

    def keys_and_values(group, picks):
        return block(group, picks).T, with_ones(block(group + KEY_VALUE_HEADS, picks))

    def score(group, head, keys_across):
        query = stacked_queries(query_ref.at[:, lanes(group, width)], head)
        return jnp.dot(query, keys_across, preferred_element_type=jnp.float32)

    def quick(group, head, scores, value, largest):
        weights = []
        for h in range(HEADS_AT_ONCE):
            part = scores[h * rows : (h + 1) * rows]
            mine = level_ref[group, :, head + h : head + h + 1]
            weights.append(jnp.exp2(part * FACTOR - mine).astype(jnp.bfloat16))
        both = jnp.dot(
            jnp.concatenate(weights, axis=0), value, preferred_element_type=jnp.float32
        )
        if head == 0:
            arrive(group, 0)
        for h in range(HEADS_AT_ONCE):
            part = both[h * rows : (h + 1) * rows]
            row_sum = 1.0 + part[:, HEAD_SIZE:]
            largest = jnp.maximum(
                largest, jnp.max(row_sum.reshape(rows // 8, 8, HEAD_SIZE), axis=0)
            )
            mixture = own_ref[group, :, head_lanes(head + h)] + part[:, :HEAD_SIZE]
            staged[group, :, head_lanes(head + h)] = (mixture * inverse_of(row_sum)).astype(
                staged.dtype
            )
        return largest

    def careful(group, head, scores, value):
        for h in range(HEADS_AT_ONCE):
            part = scores[h * rows : (h + 1) * rows] * FACTOR
            mine = level_ref[group, :, head + h : head + h + 1]
            shift = jnp.maximum(jnp.max(part, axis=1, keepdims=True), mine)
            weights = jnp.exp2(part - shift).astype(jnp.bfloat16)
            both = jnp.dot(weights, value, preferred_element_type=jnp.float32)
            share = jnp.exp2(mine - shift)
            mixture = own_ref[group, :, head_lanes(head + h)] * share + both[:, :HEAD_SIZE]
            staged[group, :, head_lanes(head + h)] = (
                mixture * inverse_of(share + both[:, HEAD_SIZE:])
            ).astype(staged.dtype)

    nothing = jnp.zeros((8, HEAD_SIZE), jnp.float32)

    def attend_quickly(picks):
        held = {g: keys_and_values(g, picks) for g in range(KEY_VALUE_HEADS)}
        largest = nothing

        def start(step):
            group, head = step
            return score(group, head, held[group][0])

        def finish(step, scores):
            nonlocal largest
            group, head = step
            if head == 0:
                arrive(group, 1)
            largest = quick(group, head, scores, held[group][1], largest)
            if head == STEPS[-1]:
                send(group).start()

        staggered([(g, h) for g in range(KEY_VALUE_HEADS) for h in STEPS], start, finish)
        return jnp.max(largest)

    def attend_carefully(picks):
        @pl.loop(0, KEY_VALUE_HEADS)
        def _(group):
            send(group).wait()
            keys_across, value = keys_and_values(group, picks)
            for head in STEPS:
                careful(group, head, score(group, head, keys_across), value)
            send(group).start()

    def attend(picks):
        largest = attend_quickly(picks)

        @pl.when(largest > LARGE_SUM)
        def _():
            attend_carefully(picks)

    my_block = lax.axis_index("ctx")
    chosen = selected_ref[0, 0], selected_ref[0, 1]
    first = chosen[0] < my_block
    second = jnp.logical_and(chosen[1] < my_block, chosen[1] != chosen[0])
    count = first.astype(jnp.int32) + second.astype(jnp.int32)

    @pl.when(count == 2)
    def _():
        attend((0, 1))

    @pl.when(count == 1)
    def _():
        attend((second.astype(jnp.int32),))

    @pl.when(count == 0)
    def _():
        for group in range(KEY_VALUE_HEADS):
            arrive(group, 0)
            arrive(group, 1)
            staged[group] = own_ref[group].astype(staged.dtype)
            send(group).start()

    for group in range(KEY_VALUE_HEADS):
        send(group).wait()


def far_attention(selected, queries, own, level, far):
    rows = queries.shape[0]
    scores = QUERY_HEADS * rows * 2 * rows
    own = pltpu.with_memory_space_constraint(own, pltpu.HBM)
    level = pltpu.with_memory_space_constraint(level, pltpu.HBM)
    return pl.pallas_call(
        far_kernel,
        out_shape=jax.ShapeDtypeStruct(queries.shape, jnp.bfloat16),
        in_specs=[
            pl.BlockSpec(memory_space=pltpu.SMEM),
            pl.BlockSpec(memory_space=pltpu.VMEM),
            *[pl.BlockSpec(memory_space=pl.ANY)] * 2,
            *[pl.BlockSpec(memory_space=pltpu.VMEM)] * len(far),
        ],
        out_specs=pl.BlockSpec(memory_space=pl.ANY),
        scratch_shapes=[
            pltpu.VMEM((KEY_VALUE_HEADS, rows, GROUP * HEAD_SIZE), jnp.float32),
            pltpu.VMEM((KEY_VALUE_HEADS, rows, HEAD_SIZE), jnp.float32),
            pltpu.VMEM((KEY_VALUE_HEADS, rows, GROUP * HEAD_SIZE), jnp.bfloat16),
            pltpu.SemaphoreType.DMA((3, KEY_VALUE_HEADS)),
        ],
        compiler_params=pltpu.CompilerParams(vmem_limit_bytes=28 * MIB),
        cost_estimate=pl.CostEstimate(
            flops=4 * scores * HEAD_SIZE, bytes_accessed=10 * MIB, transcendentals=scores
        ),
        name="far_attention",
    )(selected, queries, own, level, *far)


def local(queries, all_key_states, all_value_states, selected):
    devices = lax.axis_size("ctx")
    rows = all_key_states.shape[0]
    piece_rows = rows * COPIES // devices
    packed = pack(all_key_states, all_value_states, selected, devices)
    held = lax.all_to_all(packed, "ctx", split_axis=0, concat_axis=0, tiled=True)
    own, level = own_attention(queries, all_key_states, all_value_states)
    wanted = held[:, SLOTS * piece_rows, :2].astype(jnp.int32)
    wanted = jnp.clip(wanted, 0, devices - 1)
    moved = deliver(pick_pieces(wanted, held), devices)
    far = [m.reshape(2, SLOTS, piece_rows, HEAD_SIZE) for m in moved]
    if piece_rows % 16 != 0:
        far = [jnp.concatenate(far, axis=2)]
    return far_attention(selected, queries, own, level, far)


def solution(mesh):
    placed = P(("groups", "ctx"), None)
    return jax.shard_map(
        local, mesh=mesh, in_specs=(placed,) * 4, out_specs=placed, check_vma=False
    )
```

```python
import functools
import math

import jax
import jax.numpy as jnp
from jax import lax
from jax.experimental import pallas as pl
from jax.experimental.pallas import tpu as pltpu
from jax.sharding import PartitionSpec as P

QUERY_HEADS = 32
KEY_VALUE_HEADS = 4
HEAD_SIZE = 128
GROUP = QUERY_HEADS // KEY_VALUE_HEADS
SLOTS = 2 * KEY_VALUE_HEADS
REQUEST_ROWS = 16
COPIES = 2
MIB = 1024 * 1024


def pack_kernel(selected_ref, key_ref, value_ref, out_ref):
    devices = out_ref.shape[0]
    shares = devices // COPIES
    piece_rows = key_ref.shape[0] // shares
    for slot in range(SLOTS):
        ref = key_ref if slot < KEY_VALUE_HEADS else value_ref
        head = slot % KEY_VALUE_HEADS
        part = ref[:, head * HEAD_SIZE : (head + 1) * HEAD_SIZE]
        part = part.reshape(shares, piece_rows, HEAD_SIZE)
        for copy in range(COPIES):
            out_ref[
                copy * shares : (copy + 1) * shares,
                slot * piece_rows : (slot + 1) * piece_rows,
                :,
            ] = part
    lane = lax.broadcasted_iota(jnp.int32, (devices, REQUEST_ROWS, HEAD_SIZE), 2)
    request = jnp.where(lane == 0, selected_ref[0, 0], selected_ref[0, 1])
    out_ref[:, SLOTS * piece_rows :, :] = request.astype(jnp.float32).astype(jnp.bfloat16)


def pack(keys, values, selected, devices):
    shares = devices // COPIES
    piece_rows = keys.shape[0] // shares
    shape = (devices, SLOTS * piece_rows + REQUEST_ROWS, HEAD_SIZE)
    if piece_rows % 16 == 0:
        return pl.pallas_call(
            pack_kernel,
            out_shape=jax.ShapeDtypeStruct(shape, jnp.bfloat16),
            in_specs=[
                pl.BlockSpec(memory_space=pltpu.SMEM),
                pl.BlockSpec(memory_space=pltpu.VMEM),
                pl.BlockSpec(memory_space=pltpu.VMEM),
            ],
            out_specs=pl.BlockSpec(memory_space=pltpu.VMEM),
            name="pack",
        )(selected, keys, values)
    both = jnp.concatenate([keys, values], axis=1)
    both = both.reshape(shares, piece_rows, SLOTS, HEAD_SIZE).transpose(0, 2, 1, 3)
    both = both.reshape(shares, SLOTS * piece_rows, HEAD_SIZE)
    lane = jnp.arange(HEAD_SIZE) == 0
    request = jnp.where(lane, selected[0, 0], selected[0, 1]).astype(jnp.bfloat16)
    request = jnp.broadcast_to(request, (shares, REQUEST_ROWS, HEAD_SIZE))
    return jnp.concatenate([jnp.concatenate([both, request], axis=1)] * COPIES, axis=0)


def partner(position, step):
    return position ^ step


def pick_kernel(wanted_ref, held_ref, *out_refs):
    rows = out_refs[0].shape[1]
    me = lax.axis_index("ctx")
    for step, out_ref in enumerate(out_refs):
        device = partner(me, step)
        for pick in range(2):
            out_ref[pick] = held_ref[wanted_ref[device, pick], :rows, :]


def pick_pieces(wanted, held):
    devices, rows = held.shape[0], held.shape[1] - REQUEST_ROWS
    shares = devices // COPIES
    return pl.pallas_call(
        pick_kernel,
        out_shape=[jax.ShapeDtypeStruct((2, rows, HEAD_SIZE), jnp.bfloat16)] * shares,
        in_specs=[
            pl.BlockSpec(memory_space=pltpu.SMEM),
            pl.BlockSpec(memory_space=pltpu.VMEM),
        ],
        out_specs=[pl.BlockSpec(memory_space=pltpu.VMEM)] * shares,
        compiler_params=pltpu.CompilerParams(vmem_limit_bytes=16 * MIB),
        name="pick_pieces",
    )(wanted, held)


def delivery_order(shares):
    half, quarter = shares // 2, shares // 4
    apart = zip(range(half, half + quarter), range(quarter, half))
    return [s for pair in apart for s in pair] + [*range(half + quarter, shares), *range(1, quarter)]


def deliver(pieces, devices):
    moved = [pieces[0]]
    for step in delivery_order(len(pieces)):
        pairs = [(i, partner(i, step)) for i in range(devices)]
        moved.append(lax.ppermute(pieces[step], "ctx", pairs))
    return moved


FACTOR = math.log2(math.e) / math.sqrt(HEAD_SIZE)
PAIR = 2
LARGE_SUM = 2.0**100


def head_lanes(head):
    return slice(head * HEAD_SIZE, (head + 1) * HEAD_SIZE)


def with_ones(value):
    return jnp.concatenate([value, jnp.ones_like(value)], axis=1)


def inverse_of(positive):
    return pl.reciprocal(positive, approx=True)


def dot(a, b):
    return jnp.dot(a, b, preferred_element_type=jnp.float32)


def stack_heads(wide):
    heads = wide.shape[1] // HEAD_SIZE
    return jnp.concatenate([wide[:, head_lanes(h)] for h in range(heads)], axis=0)


def own_kernel(query_ref, key_ref, value_ref, out_ref, level_ref):
    rows = query_ref.shape[0]
    row = lax.broadcasted_iota(jnp.int32, (rows, rows), 0)
    column = lax.broadcasted_iota(jnp.int32, (rows, rows), 1)
    causal = column <= row
    keys_across = key_ref[...].T
    value = with_ones(value_ref[...])

    def score(first):
        lanes = slice(first * HEAD_SIZE, (first + PAIR) * HEAD_SIZE)
        return dot(stack_heads(query_ref[:, lanes]), keys_across)

    def finish(first, scores):
        weights, shifts = [], []
        for h in range(PAIR):
            part = jnp.where(causal, scores[h * rows : (h + 1) * rows], -1e30)
            shift = jnp.max(part, axis=1, keepdims=True) * FACTOR
            shifts.append(shift)
            weights.append(jnp.exp2(part * FACTOR - shift).astype(jnp.bfloat16))
        both = dot(jnp.concatenate(weights, axis=0), value)
        for h in range(PAIR):
            part = both[h * rows : (h + 1) * rows]
            row_sum = part[:, HEAD_SIZE:]
            out_ref[:, head_lanes(first + h)] = part[:, :HEAD_SIZE] / row_sum
            level_ref[:, head_lanes(first + h)] = shifts[h] + jnp.log2(row_sum)

    scores = score(0)
    for first in range(0, GROUP, PAIR):
        following = score(first + PAIR) if first + PAIR < GROUP else None
        finish(first, scores)
        scores = following


def own_attention(queries, keys, values):
    rows = queries.shape[0]
    width = GROUP * HEAD_SIZE
    scores = QUERY_HEADS * rows * rows
    return pl.pallas_call(
        own_kernel,
        out_shape=[pltpu.HBM(queries.shape, jnp.float32)] * 2,
        grid=(KEY_VALUE_HEADS,),
        in_specs=[
            pl.BlockSpec((rows, width), lambda g: (0, g)),
            pl.BlockSpec((rows, HEAD_SIZE), lambda g: (0, g)),
            pl.BlockSpec((rows, HEAD_SIZE), lambda g: (0, g)),
        ],
        out_specs=[pl.BlockSpec((rows, width), lambda g: (0, g))] * 2,
        compiler_params=pltpu.CompilerParams(vmem_limit_bytes=16 * MIB),
        cost_estimate=pl.CostEstimate(
            flops=4 * scores * HEAD_SIZE, bytes_accessed=11 * MIB, transcendentals=scores
        ),
        name="own_attention",
    )(queries, keys, values)


def far_kernel(selected_ref, query_ref, own_ref, level_ref, *refs, last):
    if last:
        *far_refs, out_ref, keys_ref, values_ref, scores_ref, other_scores_ref, staged, sems = refs
    else:
        *far_refs, out_ref, new_level_ref, keys_ref, values_ref, scores_ref, other_scores_ref = refs
    rows = query_ref.shape[0]
    pair_width = PAIR * HEAD_SIZE
    step_width = 2 * pair_width
    steps = query_ref.shape[1] // step_width
    steps_of_group = steps // KEY_VALUE_HEADS

    def lanes(index, size):
        return pl.ds(pl.multiple_of(index * size, size), size)

    def send(step):
        out = out_ref.at[:, lanes(step, step_width)]
        return pltpu.make_async_copy(staged.at[step], out, sems.at[step])

    def store(step, head, mixture, row_sum, level):
        result = mixture * inverse_of(row_sum)
        if last:
            staged[step, :, head_lanes(head)] = result.astype(staged.dtype)
        else:
            out_ref[:, lanes(2 * PAIR * step + head, HEAD_SIZE)] = result
            new_level_ref[:, lanes(2 * PAIR * step + head, HEAD_SIZE)] = level + jnp.log2(row_sum)

    def attend(picks):
        count = len(picks) * sum(ref.shape[2] for ref in far_refs)

        def block(slot):
            return jnp.concatenate([ref[p, slot] for p in picks for ref in far_refs], axis=0)

        @pl.loop(0, KEY_VALUE_HEADS)
        def _(group):
            keys_ref[group, :, :count] = block(group).T
            values_ref[group, :count] = with_ones(block(group + KEY_VALUE_HEADS))

        def score(pair, group, buffer):
            query = stack_heads(query_ref[:, lanes(pair, pair_width)])
            buffer[:, :count] = dot(query, keys_ref[group, :, :count])

        def repeat(narrow):
            return jnp.concatenate([narrow] * (count // HEAD_SIZE), axis=1)

        def quick(pair, group, buffer, step, half, largest):
            level = level_ref[:, lanes(pair, pair_width)]
            own = own_ref[:, lanes(pair, pair_width)]
            weights = [
                jnp.exp2(
                    buffer[h * rows : (h + 1) * rows, :count] * FACTOR
                    - repeat(level[:, head_lanes(h)])
                ).astype(jnp.bfloat16)
                for h in range(PAIR)
            ]
            both = dot(jnp.concatenate(weights, axis=0), values_ref[group, :count])
            for h in range(PAIR):
                part = both[h * rows : (h + 1) * rows]
                row_sum = 1.0 + part[:, HEAD_SIZE:]
                largest = jnp.maximum(
                    largest, jnp.max(row_sum.reshape(rows // 8, 8, HEAD_SIZE), axis=0)
                )
                mixture = own[:, head_lanes(h)] + part[:, :HEAD_SIZE]
                store(step, half * PAIR + h, mixture, row_sum, level[:, head_lanes(h)])
            return largest

        def careful(pair, group, buffer, step, half):
            score(pair, group, buffer)
            level = level_ref[:, lanes(pair, pair_width)]
            own = own_ref[:, lanes(pair, pair_width)]
            for h in range(PAIR):
                part = buffer[h * rows : (h + 1) * rows, :count] * FACTOR
                mine = level[:, head_lanes(h)]
                shift = jnp.maximum(jnp.max(part, axis=1, keepdims=True), mine)
                weights = jnp.exp2(part - repeat(shift)).astype(jnp.bfloat16)
                both = dot(weights, values_ref[group, :count])
                share = jnp.exp2(mine - shift)
                mixture = own[:, head_lanes(h)] * share + both[:, :HEAD_SIZE]
                store(step, half * PAIR + h, mixture, share + both[:, HEAD_SIZE:], shift)

        def body(step, largest):
            group = step // steps_of_group
            following = jnp.minimum(step + 1, steps - 1)
            score(2 * step + 1, group, other_scores_ref)
            largest = quick(2 * step, group, scores_ref, step, 0, largest)
            score(2 * following, following // steps_of_group, scores_ref)
            largest = quick(2 * step + 1, group, other_scores_ref, step, 1, largest)
            if last:
                send(step).start()
            return largest

        score(0, 0, scores_ref)
        largest = lax.fori_loop(0, steps, body, jnp.zeros((8, HEAD_SIZE), jnp.float32))

        @pl.when(jnp.max(largest) > LARGE_SUM)
        def _():
            @pl.loop(0, steps)
            def _(step):
                if last:
                    send(step).wait()
                for half in range(2):
                    careful(2 * step + half, step // steps_of_group, scores_ref, step, half)
                if last:
                    send(step).start()

    my_block = lax.axis_index("ctx")
    chosen = selected_ref[0, 0], selected_ref[0, 1]
    first = chosen[0] < my_block
    second = jnp.logical_and(chosen[1] < my_block, chosen[1] != chosen[0])
    valid = first.astype(jnp.int32) + second.astype(jnp.int32)

    @pl.when(valid == 2)
    def _():
        attend((0, 1))

    @pl.when(valid == 1)
    def _():
        attend((second.astype(jnp.int32),))

    @pl.when(valid == 0)
    def _():
        @pl.loop(0, steps)
        def _(step):
            wide = lanes(step, step_width)
            if last:
                staged[step] = own_ref[:, wide].astype(staged.dtype)
                send(step).start()
            else:
                out_ref[:, wide] = own_ref[:, wide]
                new_level_ref[:, wide] = level_ref[:, wide]

    if last:

        @pl.loop(0, steps)
        def _(step):
            send(step).wait()


def far_attention(selected, queries, own, level, far, last):
    rows = queries.shape[0]
    keys = 2 * sum(piece.shape[2] for piece in far)
    scores = QUERY_HEADS * rows * keys
    step_width = 2 * PAIR * HEAD_SIZE
    steps = queries.shape[1] // step_width
    in_vmem = pl.BlockSpec(memory_space=pltpu.VMEM)
    scratch = [
        pltpu.VMEM((KEY_VALUE_HEADS, HEAD_SIZE, keys), jnp.bfloat16),
        pltpu.VMEM((KEY_VALUE_HEADS, keys, 2 * HEAD_SIZE), jnp.bfloat16),
        pltpu.VMEM((PAIR * rows, keys), jnp.float32),
        pltpu.VMEM((PAIR * rows, keys), jnp.float32),
    ]
    if last:
        out_shape = jax.ShapeDtypeStruct(queries.shape, jnp.bfloat16)
        out_specs = pl.BlockSpec(memory_space=pl.ANY)
        scratch += [
            pltpu.VMEM((steps, rows, step_width), jnp.bfloat16),
            pltpu.SemaphoreType.DMA((steps,)),
        ]
    else:
        out_shape = [jax.ShapeDtypeStruct(queries.shape, jnp.float32)] * 2
        out_specs = [in_vmem] * 2
    return pl.pallas_call(
        functools.partial(far_kernel, last=last),
        out_shape=out_shape,
        in_specs=[pl.BlockSpec(memory_space=pltpu.SMEM), *[in_vmem] * (3 + len(far))],
        out_specs=out_specs,
        scratch_shapes=scratch,
        compiler_params=pltpu.CompilerParams(vmem_limit_bytes=28 * MIB),
        cost_estimate=pl.CostEstimate(
            flops=4 * scores * HEAD_SIZE, bytes_accessed=10 * MIB, transcendentals=scores
        ),
        name="late_attention" if last else "early_attention",
    )(selected, queries, own, level, *far)


def local(queries, all_key_states, all_value_states, selected):
    devices = lax.axis_size("ctx")
    rows = all_key_states.shape[0]
    piece_rows = rows * COPIES // devices
    packed = pack(all_key_states, all_value_states, selected, devices)
    held = lax.all_to_all(packed, "ctx", split_axis=0, concat_axis=0, tiled=True)
    own, level = own_attention(queries, all_key_states, all_value_states)
    held, own, level = lax.optimization_barrier((held, own, level))
    wanted = held[:, SLOTS * piece_rows, :2].astype(jnp.int32)
    wanted = jnp.clip(wanted, 0, devices - 1)
    moved = deliver(pick_pieces(wanted, held), devices)
    far = [m.reshape(2, SLOTS, piece_rows, HEAD_SIZE) for m in moved]
    early, late = far[: len(far) // 2], far[len(far) // 2 :]
    if piece_rows % 16 != 0:
        early, late = [jnp.concatenate(early, axis=2)], [jnp.concatenate(late, axis=2)]
    own, level = far_attention(selected, queries, own, level, early, last=False)
    return far_attention(selected, queries, own, level, late, last=True)


def solution(mesh):
    placed = P(("groups", "ctx"), None)
    return jax.shard_map(
        local, mesh=mesh, in_specs=(placed,) * 4, out_specs=placed, check_vma=False
    )
```

```python
import functools
import math

import jax
import jax.numpy as jnp
from jax import lax
from jax.experimental import pallas as pl
from jax.experimental.pallas import tpu as pltpu
from jax.sharding import PartitionSpec as P

QUERY_HEADS = 32
KEY_VALUE_HEADS = 4
HEAD_SIZE = 128
GROUP = QUERY_HEADS // KEY_VALUE_HEADS
SLOTS = 2 * KEY_VALUE_HEADS
COPIES = 2
MIB = 1024 * 1024


def pack_kernel(key_ref, value_ref, out_ref):
    shares = out_ref.shape[0] // COPIES
    piece_rows = key_ref.shape[0] // shares
    for slot in range(SLOTS):
        ref = key_ref if slot < KEY_VALUE_HEADS else value_ref
        head = slot % KEY_VALUE_HEADS
        part = ref[:, head * HEAD_SIZE : (head + 1) * HEAD_SIZE]
        part = part.reshape(shares, piece_rows, HEAD_SIZE)
        for copy in range(COPIES):
            out_ref[
                copy * shares : (copy + 1) * shares,
                slot * piece_rows : (slot + 1) * piece_rows,
                :,
            ] = part


def pack(keys, values, devices):
    shares = devices // COPIES
    piece_rows = keys.shape[0] // shares
    if piece_rows % 16 == 0:
        return pl.pallas_call(
            pack_kernel,
            out_shape=jax.ShapeDtypeStruct(
                (devices, SLOTS * piece_rows, HEAD_SIZE), jnp.bfloat16
            ),
            in_specs=[pl.BlockSpec(memory_space=pltpu.VMEM)] * 2,
            out_specs=pl.BlockSpec(memory_space=pltpu.VMEM),
            name="pack",
        )(keys, values)
    both = jnp.concatenate([keys, values], axis=1)
    both = both.reshape(shares, piece_rows, SLOTS, HEAD_SIZE).transpose(0, 2, 1, 3)
    both = both.reshape(shares, SLOTS * piece_rows, HEAD_SIZE)
    return jnp.concatenate([both] * COPIES, axis=0)


def partner(position, step):
    return position ^ step


def swap(array, step, devices):
    return lax.ppermute(array, "ctx", [(i, partner(i, step)) for i in range(devices)])


def exchange_requests(selected, shares, devices):
    requests = selected
    step = 1
    while step < shares:
        requests = jnp.concatenate([requests, swap(requests, step, devices)], axis=0)
        step *= 2
    return requests


def pick_kernel(requests_ref, held_ref, *out_refs):
    for step, out_ref in enumerate(out_refs):
        for pick in range(2):
            out_ref[pick] = held_ref[requests_ref[step, pick]]


def pick_pieces(requests, held):
    devices, rows, _ = held.shape
    shares = devices // COPIES
    return pl.pallas_call(
        pick_kernel,
        out_shape=[jax.ShapeDtypeStruct((2, rows, HEAD_SIZE), jnp.bfloat16)] * shares,
        in_specs=[
            pl.BlockSpec(memory_space=pltpu.SMEM),
            pl.BlockSpec(memory_space=pltpu.VMEM),
        ],
        out_specs=[pl.BlockSpec(memory_space=pltpu.VMEM)] * shares,
        compiler_params=pltpu.CompilerParams(vmem_limit_bytes=16 * MIB),
        name="pick_pieces",
    )(requests, held)


def delivery_order(shares):
    half, quarter = shares // 2, shares // 4
    apart = zip(range(half, half + quarter), range(quarter, half))
    return [*range(1, quarter), *[s for pair in apart for s in pair], *range(half + quarter, shares)]


def deliver(pieces, devices):
    order = delivery_order(len(pieces))
    return [pieces[0]] + [swap(pieces[step], step, devices) for step in order]


FACTOR = math.log2(math.e) / math.sqrt(HEAD_SIZE)
PAIR = 2
LARGE_SUM = 2.0**100


def head_lanes(head):
    return slice(head * HEAD_SIZE, (head + 1) * HEAD_SIZE)


def with_ones(value):
    return jnp.concatenate([value, jnp.ones_like(value)], axis=1)


def inverse_of(positive):
    return pl.reciprocal(positive, approx=True)


def dot(a, b):
    return jnp.dot(a, b, preferred_element_type=jnp.float32)


def stack_heads(wide):
    heads = wide.shape[1] // HEAD_SIZE
    return jnp.concatenate([wide[:, head_lanes(h)] for h in range(heads)], axis=0)


def own_kernel(query_ref, key_ref, value_ref, out_ref, level_ref):
    rows = query_ref.shape[0]
    row = lax.broadcasted_iota(jnp.int32, (rows, rows), 0)
    column = lax.broadcasted_iota(jnp.int32, (rows, rows), 1)
    causal = column <= row
    keys_across = key_ref[...].T
    value = with_ones(value_ref[...])

    def score(first):
        lanes = slice(first * HEAD_SIZE, (first + PAIR) * HEAD_SIZE)
        return dot(stack_heads(query_ref[:, lanes]), keys_across)

    def finish(first, scores):
        weights, shifts = [], []
        for h in range(PAIR):
            part = jnp.where(causal, scores[h * rows : (h + 1) * rows], -1e30)
            shift = jnp.max(part, axis=1, keepdims=True) * FACTOR
            shifts.append(shift)
            weights.append(jnp.exp2(part * FACTOR - shift).astype(jnp.bfloat16))
        both = dot(jnp.concatenate(weights, axis=0), value)
        for h in range(PAIR):
            part = both[h * rows : (h + 1) * rows]
            row_sum = part[:, HEAD_SIZE:]
            out_ref[:, head_lanes(first + h)] = part[:, :HEAD_SIZE] / row_sum
            level_ref[:, head_lanes(first + h)] = shifts[h] + jnp.log2(row_sum)

    scores = score(0)
    for first in range(0, GROUP, PAIR):
        following = score(first + PAIR) if first + PAIR < GROUP else None
        finish(first, scores)
        scores = following


def own_attention(queries, keys, values):
    rows = queries.shape[0]
    width = GROUP * HEAD_SIZE
    scores = QUERY_HEADS * rows * rows
    return pl.pallas_call(
        own_kernel,
        out_shape=[pltpu.HBM(queries.shape, jnp.float32)] * 2,
        grid=(KEY_VALUE_HEADS,),
        in_specs=[
            pl.BlockSpec((rows, width), lambda g: (0, g)),
            pl.BlockSpec((rows, HEAD_SIZE), lambda g: (0, g)),
            pl.BlockSpec((rows, HEAD_SIZE), lambda g: (0, g)),
        ],
        out_specs=[pl.BlockSpec((rows, width), lambda g: (0, g))] * 2,
        compiler_params=pltpu.CompilerParams(vmem_limit_bytes=16 * MIB),
        cost_estimate=pl.CostEstimate(
            flops=4 * scores * HEAD_SIZE, bytes_accessed=11 * MIB, transcendentals=scores
        ),
        name="own_attention",
    )(queries, keys, values)


def far_kernel(selected_ref, query_ref, own_in, level_in, *refs, last):
    if last:
        *far_refs, out_ref, staged, sems = refs
        own_ref, level_ref = own_in, level_in
    else:
        *far_refs, out_ref, new_level_ref, own_ref, level_ref, sems = refs
    rows = query_ref.shape[0]
    width = GROUP * HEAD_SIZE

    def wide(group):
        start = group * width
        return pl.ds(start if isinstance(group, int) else pl.multiple_of(start, width), width)

    def fetch(group, which):
        source, target = ((own_in, own_ref), (level_in, level_ref))[which]
        lanes = wide(group)
        return pltpu.make_async_copy(
            source.at[:, lanes], target.at[:, lanes], sems.at[which, group]
        )

    def send(group):
        lanes = wide(group)
        return pltpu.make_async_copy(staged.at[:, lanes], out_ref.at[:, lanes], sems.at[group])

    if not last:
        for group in range(KEY_VALUE_HEADS):
            fetch(group, 1).start()
            fetch(group, 0).start()

    def head_of(group, head):
        start = (group * GROUP + head) * HEAD_SIZE
        fixed = isinstance(group, int)
        return pl.ds(start if fixed else pl.multiple_of(start, HEAD_SIZE), HEAD_SIZE)

    def store(lanes, mixture, row_sum, level):
        result = mixture * inverse_of(row_sum)
        if last:
            staged[:, lanes] = result.astype(staged.dtype)
        else:
            out_ref[:, lanes] = result
            new_level_ref[:, lanes] = level + jnp.log2(row_sum)

    def attend(picks):
        count = len(picks) * sum(ref.shape[2] for ref in far_refs)

        def block(slot):
            return jnp.concatenate([ref[p, slot] for p in picks for ref in far_refs], axis=0)

        def keys_and_values(group):
            return block(group).T, with_ones(block(group + KEY_VALUE_HEADS))

        def repeat(narrow):
            return jnp.concatenate([narrow] * (count // HEAD_SIZE), axis=1)

        def quick(group, head, scores, value, largest):
            lanes = head_of(group, head)
            level = level_ref[:, lanes]
            weights = jnp.exp2(scores * FACTOR - repeat(level)).astype(jnp.bfloat16)
            both = dot(weights, value)
            row_sum = 1.0 + both[:, HEAD_SIZE:]
            store(lanes, own_ref[:, lanes] + both[:, :HEAD_SIZE], row_sum, level)
            return jnp.maximum(
                largest, jnp.max(row_sum.reshape(rows // 8, 8, HEAD_SIZE), axis=0)
            )

        def careful(group, head, scores, value):
            lanes = head_of(group, head)
            part = scores * FACTOR
            level = level_ref[:, lanes]
            shift = jnp.maximum(jnp.max(part, axis=1, keepdims=True), level)
            weights = jnp.exp2(part - repeat(shift)).astype(jnp.bfloat16)
            both = dot(weights, value)
            share = jnp.exp2(level - shift)
            mixture = own_ref[:, lanes] * share + both[:, :HEAD_SIZE]
            store(lanes, mixture, share + both[:, HEAD_SIZE:], shift)

        def score(group, head, keys_across):
            return dot(query_ref[:, head_of(group, head)], keys_across)

        largest = jnp.zeros((8, HEAD_SIZE), jnp.float32)
        order = [(g, h) for g in range(KEY_VALUE_HEADS) for h in range(GROUP)]
        held = {0: keys_and_values(0)}
        scores = score(0, 0, held[0][0])
        for (group, head), later in zip(order, order[1:] + [None]):
            following = None
            if later is not None:
                if later[0] not in held:
                    held[later[0]] = keys_and_values(later[0])
                following = score(*later, held[later[0]][0])
            if head == 0 and not last:
                fetch(group, 1).wait()
                fetch(group, 0).wait()
            largest = quick(group, head, scores, held[group][1], largest)
            if head == GROUP - 1 and last:
                send(group).start()
            scores = following

        @pl.when(jnp.max(largest) > LARGE_SUM)
        def _():
            @pl.loop(0, KEY_VALUE_HEADS)
            def _(group):
                if last:
                    send(group).wait()
                keys_across, value = keys_and_values(group)
                for head in range(GROUP):
                    careful(group, head, score(group, head, keys_across), value)
                if last:
                    send(group).start()

    my_block = lax.axis_index("ctx")
    chosen = selected_ref[0, 0], selected_ref[0, 1]
    first = chosen[0] < my_block
    second = jnp.logical_and(chosen[1] < my_block, chosen[1] != chosen[0])
    valid = first.astype(jnp.int32) + second.astype(jnp.int32)

    @pl.when(valid == 2)
    def _():
        attend((0, 1))

    @pl.when(valid == 1)
    def _():
        attend((second.astype(jnp.int32),))

    @pl.when(valid == 0)
    def _():
        @pl.loop(0, KEY_VALUE_HEADS)
        def _(group):
            lanes = wide(group)
            if last:
                staged[:, lanes] = own_ref[:, lanes].astype(staged.dtype)
                send(group).start()
            else:
                fetch(group, 1).wait()
                fetch(group, 0).wait()
                out_ref[:, lanes] = own_ref[:, lanes]
                new_level_ref[:, lanes] = level_ref[:, lanes]

    if last:

        @pl.loop(0, KEY_VALUE_HEADS)
        def _(group):
            send(group).wait()


def far_attention(selected, queries, own, level, far, last):
    rows = queries.shape[0]
    scores = QUERY_HEADS * rows * 2 * sum(piece.shape[2] for piece in far)
    in_vmem = pl.BlockSpec(memory_space=pltpu.VMEM)
    anywhere = pl.BlockSpec(memory_space=pl.ANY)
    if last:
        earlier = in_vmem
        out_shape = jax.ShapeDtypeStruct(queries.shape, jnp.bfloat16)
        out_specs = anywhere
        scratch = [
            pltpu.VMEM(queries.shape, jnp.bfloat16),
            pltpu.SemaphoreType.DMA((KEY_VALUE_HEADS,)),
        ]
    else:
        earlier = anywhere
        own = pltpu.with_memory_space_constraint(own, pltpu.HBM)
        level = pltpu.with_memory_space_constraint(level, pltpu.HBM)
        out_shape = [jax.ShapeDtypeStruct(queries.shape, jnp.float32)] * 2
        out_specs = [in_vmem] * 2
        scratch = [
            pltpu.VMEM(queries.shape, jnp.float32),
            pltpu.VMEM(queries.shape, jnp.float32),
            pltpu.SemaphoreType.DMA((2, KEY_VALUE_HEADS)),
        ]
    return pl.pallas_call(
        functools.partial(far_kernel, last=last),
        out_shape=out_shape,
        in_specs=[
            pl.BlockSpec(memory_space=pltpu.SMEM),
            in_vmem,
            earlier,
            earlier,
            *[in_vmem] * len(far),
        ],
        out_specs=out_specs,
        scratch_shapes=scratch,
        compiler_params=pltpu.CompilerParams(vmem_limit_bytes=30 * MIB),
        cost_estimate=pl.CostEstimate(
            flops=4 * scores * HEAD_SIZE, bytes_accessed=10 * MIB, transcendentals=scores
        ),
        name="late_attention" if last else "early_attention",
    )(selected, queries, own, level, *far)


def local(queries, all_key_states, all_value_states, selected):
    devices = lax.axis_size("ctx")
    rows = all_key_states.shape[0]
    piece_rows = rows * COPIES // devices
    packed = pack(all_key_states, all_value_states, devices)
    packed, queries = lax.optimization_barrier((packed, queries))
    held = lax.all_to_all(packed, "ctx", split_axis=0, concat_axis=0, tiled=True)
    own, level = own_attention(queries, all_key_states, all_value_states)
    mine, own, level = lax.optimization_barrier((selected, own, level))
    requests = exchange_requests(mine, devices // COPIES, devices)
    requests = jnp.clip(requests, 0, devices - 1)
    moved = deliver(pick_pieces(requests, held), devices)
    far = [m.reshape(2, SLOTS, piece_rows, HEAD_SIZE) for m in moved]
    early, late = far[: len(far) // 2], far[len(far) // 2 :]
    if piece_rows % 16 != 0:
        early, late = [jnp.concatenate(early, axis=2)], [jnp.concatenate(late, axis=2)]
    own, level = far_attention(selected, queries, own, level, early, last=False)
    return far_attention(selected, queries, own, level, late, last=True)


def solution(mesh):
    placed = P(("groups", "ctx"), None)
    return jax.shard_map(
        local, mesh=mesh, in_specs=(placed,) * 4, out_specs=placed, check_vma=False
    )
```

```python
import functools
import math

import jax
import jax.numpy as jnp
from jax import lax
from jax.experimental import pallas as pl
from jax.experimental.pallas import tpu as pltpu
from jax.sharding import PartitionSpec as P

QUERY_HEADS = 32
KEY_VALUE_HEADS = 4
HEAD_SIZE = 128
GROUP = QUERY_HEADS // KEY_VALUE_HEADS
SLOTS = 2 * KEY_VALUE_HEADS
COPIES = 2
MIB = 1024 * 1024


def pack_kernel(key_ref, value_ref, out_ref, staged, arrived, left):
    shares, piece_rows, _ = key_ref.shape
    half = KEY_VALUE_HEADS * piece_rows

    def take(slot):
        ref = key_ref if slot < KEY_VALUE_HEADS else value_ref
        head = slot % KEY_VALUE_HEADS
        lanes = pl.ds(head * HEAD_SIZE, HEAD_SIZE)
        rows = pl.ds(slot * piece_rows, piece_rows)
        return pltpu.make_async_copy(
            ref.at[:, :, lanes], staged.at[:, rows, :], arrived.at[slot]
        )

    def give(which, copy):
        rows = pl.ds(which * half, half)
        return pltpu.make_async_copy(
            staged.at[:, rows, :],
            out_ref.at[pl.ds(copy * shares, shares), rows, :],
            left.at[which, copy],
        )

    for slot in range(SLOTS):
        take(slot).start()
    for which in range(2):
        for head in range(KEY_VALUE_HEADS):
            take(which * KEY_VALUE_HEADS + head).wait()
        for copy in range(COPIES):
            give(which, copy).start()
    for which in range(2):
        for copy in range(COPIES):
            give(which, copy).wait()


def pack(keys, values, devices):
    shares = devices // COPIES
    piece_rows = keys.shape[0] // shares
    if piece_rows % 16 == 0:
        split = (shares, piece_rows, keys.shape[1])
        return pl.pallas_call(
            pack_kernel,
            out_shape=jax.ShapeDtypeStruct(
                (devices, SLOTS * piece_rows, HEAD_SIZE), jnp.bfloat16
            ),
            in_specs=[pl.BlockSpec(memory_space=pl.ANY)] * 2,
            out_specs=pl.BlockSpec(memory_space=pl.ANY),
            scratch_shapes=[
                pltpu.VMEM((shares, SLOTS * piece_rows, HEAD_SIZE), jnp.bfloat16),
                pltpu.SemaphoreType.DMA((SLOTS,)),
                pltpu.SemaphoreType.DMA((2, COPIES)),
            ],
            name="pack",
        )(keys.reshape(split), values.reshape(split))
    both = jnp.concatenate([keys, values], axis=1)
    both = both.reshape(shares, piece_rows, SLOTS, HEAD_SIZE).transpose(0, 2, 1, 3)
    both = both.reshape(shares, SLOTS * piece_rows, HEAD_SIZE)
    return jnp.concatenate([both] * COPIES, axis=0)


def partner(position, step):
    return position ^ step


def swap(array, step, devices):
    return lax.ppermute(array, "ctx", [(i, partner(i, step)) for i in range(devices)])


def exchange_requests(selected, shares, devices):
    requests = selected
    step = 1
    while step < shares:
        requests = jnp.concatenate([requests, swap(requests, step, devices)], axis=0)
        step *= 2
    return requests


def pick_kernel(requests_ref, held_ref, *out_refs):
    for step, out_ref in enumerate(out_refs):
        for pick in range(2):
            out_ref[pick] = held_ref[requests_ref[step, pick]]


def pick_pieces(requests, held):
    devices, rows, _ = held.shape
    shares = devices // COPIES
    return pl.pallas_call(
        pick_kernel,
        out_shape=[jax.ShapeDtypeStruct((2, rows, HEAD_SIZE), jnp.bfloat16)] * shares,
        in_specs=[
            pl.BlockSpec(memory_space=pltpu.SMEM),
            pl.BlockSpec(memory_space=pltpu.VMEM),
        ],
        out_specs=[pl.BlockSpec(memory_space=pltpu.VMEM)] * shares,
        compiler_params=pltpu.CompilerParams(vmem_limit_bytes=16 * MIB),
        name="pick_pieces",
    )(requests, held)


def delivery_order(shares):
    half, quarter = shares // 2, shares // 4
    apart = zip(range(half, half + quarter), range(quarter, half))
    return [*range(1, quarter), *[s for pair in apart for s in pair], *range(half + quarter, shares)]


def deliver(pieces, devices):
    order = delivery_order(len(pieces))
    return [pieces[0]] + [swap(pieces[step], step, devices) for step in order]


FACTOR = math.log2(math.e) / math.sqrt(HEAD_SIZE)
PAIR = 2
LARGE_SUM = 2.0**100


def head_lanes(head):
    return slice(head * HEAD_SIZE, (head + 1) * HEAD_SIZE)


def with_ones(value):
    return jnp.concatenate([value, jnp.ones_like(value)], axis=1)


def inverse_of(positive):
    return pl.reciprocal(positive, approx=True)


def dot(a, b):
    return jnp.dot(a, b, preferred_element_type=jnp.float32)


def stack_heads(wide):
    heads = wide.shape[1] // HEAD_SIZE
    return jnp.concatenate([wide[:, head_lanes(h)] for h in range(heads)], axis=0)


def own_kernel(query_ref, key_ref, value_ref, out_ref, level_ref):
    rows = query_ref.shape[0]
    row = lax.broadcasted_iota(jnp.int32, (rows, rows), 0)
    column = lax.broadcasted_iota(jnp.int32, (rows, rows), 1)
    causal = column <= row
    lane = lax.broadcasted_iota(jnp.int32, (rows, HEAD_SIZE), 1)
    keys_across = key_ref[...].T
    value = with_ones(value_ref[...])

    def score(first):
        lanes = slice(first * HEAD_SIZE, (first + PAIR) * HEAD_SIZE)
        return dot(stack_heads(query_ref[:, lanes]), keys_across)

    def finish(first, scores):
        weights, shifts = [], []
        for h in range(PAIR):
            part = jnp.where(causal, scores[h * rows : (h + 1) * rows], -1e30)
            shift = jnp.max(part, axis=1, keepdims=True) * FACTOR
            shifts.append(shift)
            weights.append(jnp.exp2(part * FACTOR - shift).astype(jnp.bfloat16))
        both = dot(jnp.concatenate(weights, axis=0), value)
        for h in range(PAIR):
            part = both[h * rows : (h + 1) * rows]
            row_sum = part[:, HEAD_SIZE:]
            out_ref[:, head_lanes(first + h)] = part[:, :HEAD_SIZE] / row_sum
            level = shifts[h] + jnp.log2(row_sum)
            level_ref[...] = jnp.where(lane == first + h, level, level_ref[...])

    level_ref[...] = jnp.zeros_like(level_ref)
    scores = score(0)
    for first in range(0, GROUP, PAIR):
        following = score(first + PAIR) if first + PAIR < GROUP else None
        finish(first, scores)
        scores = following


def own_attention(queries, keys, values):
    rows = queries.shape[0]
    width = GROUP * HEAD_SIZE
    scores = QUERY_HEADS * rows * rows
    return pl.pallas_call(
        own_kernel,
        out_shape=[
            pltpu.HBM(queries.shape, jnp.float32),
            pltpu.HBM((rows, KEY_VALUE_HEADS * HEAD_SIZE), jnp.float32),
        ],
        grid=(KEY_VALUE_HEADS,),
        in_specs=[
            pl.BlockSpec((rows, width), lambda g: (0, g)),
            pl.BlockSpec((rows, HEAD_SIZE), lambda g: (0, g)),
            pl.BlockSpec((rows, HEAD_SIZE), lambda g: (0, g)),
        ],
        out_specs=[
            pl.BlockSpec((rows, width), lambda g: (0, g)),
            pl.BlockSpec((rows, HEAD_SIZE), lambda g: (0, g)),
        ],
        compiler_params=pltpu.CompilerParams(vmem_limit_bytes=16 * MIB),
        cost_estimate=pl.CostEstimate(
            flops=4 * scores * HEAD_SIZE, bytes_accessed=7 * MIB, transcendentals=scores
        ),
        name="own_attention",
    )(queries, keys, values)


def far_kernel(selected_ref, query_ref, own_in, level_in, *refs, last):
    if last:
        *far_refs, out_ref, staged, sems = refs
        own_ref, level_ref = own_in, level_in
    else:
        *far_refs, out_ref, new_level_ref, own_ref, level_ref, sems = refs
    rows = query_ref.shape[0]
    width = GROUP * HEAD_SIZE

    def wide(group):
        start = group * width
        return pl.ds(start if isinstance(group, int) else pl.multiple_of(start, width), width)

    def narrow(group):
        start = group * HEAD_SIZE
        fixed = isinstance(group, int)
        return pl.ds(start if fixed else pl.multiple_of(start, HEAD_SIZE), HEAD_SIZE)

    def level_of(group, head):
        if last:
            return level_ref[:, head_of(group, head)]
        one = level_ref[:, narrow(group)][:, head : head + 1]
        return jnp.broadcast_to(one, (rows, HEAD_SIZE))

    def fetch(group, which):
        source, target = ((own_in, own_ref), (level_in, level_ref))[which]
        lanes = wide(group) if which == 0 else narrow(group)
        return pltpu.make_async_copy(
            source.at[:, lanes], target.at[:, lanes], sems.at[which, group]
        )

    def send(group):
        lanes = wide(group)
        return pltpu.make_async_copy(staged.at[:, lanes], out_ref.at[:, lanes], sems.at[group])

    if not last:
        for group in range(KEY_VALUE_HEADS):
            fetch(group, 1).start()
            fetch(group, 0).start()

    def head_of(group, head):
        start = (group * GROUP + head) * HEAD_SIZE
        fixed = isinstance(group, int)
        return pl.ds(start if fixed else pl.multiple_of(start, HEAD_SIZE), HEAD_SIZE)

    def store(lanes, mixture, row_sum, level):
        result = mixture * inverse_of(row_sum)
        if last:
            staged[:, lanes] = result.astype(staged.dtype)
        else:
            out_ref[:, lanes] = result
            new_level_ref[:, lanes] = level + jnp.log2(row_sum)

    def attend(picks):
        count = len(picks) * sum(ref.shape[2] for ref in far_refs)

        def block(slot):
            return jnp.concatenate([ref[p, slot] for p in picks for ref in far_refs], axis=0)

        def keys_and_values(group):
            return block(group).T, with_ones(block(group + KEY_VALUE_HEADS))

        def repeat(narrow):
            return jnp.concatenate([narrow] * (count // HEAD_SIZE), axis=1)

        def quick(group, head, scores, value, largest):
            lanes = head_of(group, head)
            level = level_of(group, head)
            weights = jnp.exp2(scores * FACTOR - repeat(level)).astype(jnp.bfloat16)
            both = dot(weights, value)
            row_sum = 1.0 + both[:, HEAD_SIZE:]
            store(lanes, own_ref[:, lanes] + both[:, :HEAD_SIZE], row_sum, level)
            return jnp.maximum(
                largest, jnp.max(row_sum.reshape(rows // 8, 8, HEAD_SIZE), axis=0)
            )

        def careful(group, head, scores, value):
            lanes = head_of(group, head)
            part = scores * FACTOR
            level = level_of(group, head)
            shift = jnp.maximum(jnp.max(part, axis=1, keepdims=True), level)
            weights = jnp.exp2(part - repeat(shift)).astype(jnp.bfloat16)
            both = dot(weights, value)
            share = jnp.exp2(level - shift)
            mixture = own_ref[:, lanes] * share + both[:, :HEAD_SIZE]
            store(lanes, mixture, share + both[:, HEAD_SIZE:], shift)

        def score(group, head, keys_across):
            return dot(query_ref[:, head_of(group, head)], keys_across)

        largest = jnp.zeros((8, HEAD_SIZE), jnp.float32)
        order = [(g, h) for g in range(KEY_VALUE_HEADS) for h in range(GROUP)]
        held = {0: keys_and_values(0)}
        scores = score(0, 0, held[0][0])
        for (group, head), later in zip(order, order[1:] + [None]):
            following = None
            if later is not None:
                if later[0] not in held:
                    held[later[0]] = keys_and_values(later[0])
                following = score(*later, held[later[0]][0])
            if head == 0 and not last:
                fetch(group, 1).wait()
                fetch(group, 0).wait()
            largest = quick(group, head, scores, held[group][1], largest)
            if head == GROUP - 1 and last:
                send(group).start()
            scores = following

        @pl.when(jnp.max(largest) > LARGE_SUM)
        def _():
            @pl.loop(0, KEY_VALUE_HEADS)
            def _(group):
                if last:
                    send(group).wait()
                keys_across, value = keys_and_values(group)
                for head in range(GROUP):
                    careful(group, head, score(group, head, keys_across), value)
                if last:
                    send(group).start()

    my_block = lax.axis_index("ctx")
    chosen = selected_ref[0, 0], selected_ref[0, 1]
    first = chosen[0] < my_block
    second = jnp.logical_and(chosen[1] < my_block, chosen[1] != chosen[0])
    valid = first.astype(jnp.int32) + second.astype(jnp.int32)

    @pl.when(valid == 2)
    def _():
        attend((0, 1))

    @pl.when(valid == 1)
    def _():
        attend((second.astype(jnp.int32),))

    @pl.when(valid == 0)
    def _():
        @pl.loop(0, KEY_VALUE_HEADS)
        def _(group):
            lanes = wide(group)
            if last:
                staged[:, lanes] = own_ref[:, lanes].astype(staged.dtype)
                send(group).start()
            else:
                fetch(group, 1).wait()
                fetch(group, 0).wait()
                out_ref[:, lanes] = own_ref[:, lanes]
                for head in range(GROUP):
                    new_level_ref[:, head_of(group, head)] = level_of(group, head)

    if last:

        @pl.loop(0, KEY_VALUE_HEADS)
        def _(group):
            send(group).wait()


def far_attention(selected, queries, own, level, far, last):
    rows = queries.shape[0]
    scores = QUERY_HEADS * rows * 2 * sum(piece.shape[2] for piece in far)
    in_vmem = pl.BlockSpec(memory_space=pltpu.VMEM)
    anywhere = pl.BlockSpec(memory_space=pl.ANY)
    if last:
        earlier = in_vmem
        out_shape = jax.ShapeDtypeStruct(queries.shape, jnp.bfloat16)
        out_specs = anywhere
        scratch = [
            pltpu.VMEM(queries.shape, jnp.bfloat16),
            pltpu.SemaphoreType.DMA((KEY_VALUE_HEADS,)),
        ]
    else:
        earlier = anywhere
        own = pltpu.with_memory_space_constraint(own, pltpu.HBM)
        level = pltpu.with_memory_space_constraint(level, pltpu.HBM)
        out_shape = [jax.ShapeDtypeStruct(queries.shape, jnp.float32)] * 2
        out_specs = [in_vmem] * 2
        scratch = [
            pltpu.VMEM(queries.shape, jnp.float32),
            pltpu.VMEM(level.shape, jnp.float32),
            pltpu.SemaphoreType.DMA((2, KEY_VALUE_HEADS)),
        ]
    return pl.pallas_call(
        functools.partial(far_kernel, last=last),
        out_shape=out_shape,
        in_specs=[
            pl.BlockSpec(memory_space=pltpu.SMEM),
            in_vmem,
            earlier,
            earlier,
            *[in_vmem] * len(far),
        ],
        out_specs=out_specs,
        scratch_shapes=scratch,
        compiler_params=pltpu.CompilerParams(vmem_limit_bytes=30 * MIB),
        cost_estimate=pl.CostEstimate(
            flops=4 * scores * HEAD_SIZE, bytes_accessed=10 * MIB, transcendentals=scores
        ),
        name="late_attention" if last else "early_attention",
    )(selected, queries, own, level, *far)


def local(queries, all_key_states, all_value_states, selected):
    devices = lax.axis_size("ctx")
    rows = all_key_states.shape[0]
    piece_rows = rows * COPIES // devices
    packed = pack(all_key_states, all_value_states, devices)
    packed, queries = lax.optimization_barrier((packed, queries))
    held = lax.all_to_all(packed, "ctx", split_axis=0, concat_axis=0, tiled=True)
    own, level = own_attention(queries, all_key_states, all_value_states)
    mine, own, level = lax.optimization_barrier((selected, own, level))
    requests = exchange_requests(mine, devices // COPIES, devices)
    requests = jnp.clip(requests, 0, devices - 1)
    moved = deliver(pick_pieces(requests, held), devices)
    far = [m.reshape(2, SLOTS, piece_rows, HEAD_SIZE) for m in moved]
    early, late = far[: len(far) // 2], far[len(far) // 2 :]
    if piece_rows % 16 != 0:
        early, late = [jnp.concatenate(early, axis=2)], [jnp.concatenate(late, axis=2)]
    own, level = far_attention(selected, queries, own, level, early, last=False)
    return far_attention(selected, queries, own, level, late, last=True)


def solution(mesh):
    placed = P(("groups", "ctx"), None)
    return jax.shard_map(
        local, mesh=mesh, in_specs=(placed,) * 4, out_specs=placed, check_vma=False
    )
```

```python
import functools
import math

import jax
import jax.numpy as jnp
from jax import lax
from jax.experimental import pallas as pl
from jax.experimental.pallas import tpu as pltpu
from jax.sharding import PartitionSpec as P

QUERY_HEADS = 32
KEY_VALUE_HEADS = 4
HEAD_SIZE = 128
GROUP = QUERY_HEADS // KEY_VALUE_HEADS
SLOTS = 2 * KEY_VALUE_HEADS
COPIES = 2
MIB = 1024 * 1024


def pack_kernel(key_ref, value_ref, out_ref, staged, arrived, left):
    shares, piece_rows, _ = key_ref.shape
    half = KEY_VALUE_HEADS * piece_rows

    def take(slot):
        ref = key_ref if slot < KEY_VALUE_HEADS else value_ref
        head = slot % KEY_VALUE_HEADS
        lanes = pl.ds(head * HEAD_SIZE, HEAD_SIZE)
        rows = pl.ds(slot * piece_rows, piece_rows)
        return pltpu.make_async_copy(
            ref.at[:, :, lanes], staged.at[:, rows, :], arrived.at[slot]
        )

    def give(which, copy):
        rows = pl.ds(which * half, half)
        return pltpu.make_async_copy(
            staged.at[:, rows, :],
            out_ref.at[pl.ds(copy * shares, shares), rows, :],
            left.at[which, copy],
        )

    for slot in range(SLOTS):
        take(slot).start()
    for which in range(2):
        for head in range(KEY_VALUE_HEADS):
            take(which * KEY_VALUE_HEADS + head).wait()
        for copy in range(COPIES):
            give(which, copy).start()
    for which in range(2):
        for copy in range(COPIES):
            give(which, copy).wait()


def pack(keys, values, devices):
    shares = devices // COPIES
    piece_rows = keys.shape[0] // shares
    if piece_rows % 16 == 0:
        split = (shares, piece_rows, keys.shape[1])
        return pl.pallas_call(
            pack_kernel,
            out_shape=jax.ShapeDtypeStruct(
                (devices, SLOTS * piece_rows, HEAD_SIZE), jnp.bfloat16
            ),
            in_specs=[pl.BlockSpec(memory_space=pl.ANY)] * 2,
            out_specs=pl.BlockSpec(memory_space=pl.ANY),
            scratch_shapes=[
                pltpu.VMEM((shares, SLOTS * piece_rows, HEAD_SIZE), jnp.bfloat16),
                pltpu.SemaphoreType.DMA((SLOTS,)),
                pltpu.SemaphoreType.DMA((2, COPIES)),
            ],
            name="pack",
        )(keys.reshape(split), values.reshape(split))
    both = jnp.concatenate([keys, values], axis=1)
    both = both.reshape(shares, piece_rows, SLOTS, HEAD_SIZE).transpose(0, 2, 1, 3)
    both = both.reshape(shares, SLOTS * piece_rows, HEAD_SIZE)
    return jnp.concatenate([both] * COPIES, axis=0)


def partner(position, step):
    return position ^ step


def swap(array, step, devices):
    return lax.ppermute(array, "ctx", [(i, partner(i, step)) for i in range(devices)])


def exchange_requests(selected, shares, devices):
    requests = selected
    step = 1
    while step < shares:
        requests = jnp.concatenate([requests, swap(requests, step, devices)], axis=0)
        step *= 2
    return requests


def pick_kernel(requests_ref, held_ref, *out_refs):
    for step, out_ref in enumerate(out_refs):
        for pick in range(2):
            out_ref[pick] = held_ref[requests_ref[step, pick]]


def pick_pieces(requests, held):
    devices, rows, _ = held.shape
    shares = devices // COPIES
    return pl.pallas_call(
        pick_kernel,
        out_shape=[jax.ShapeDtypeStruct((2, rows, HEAD_SIZE), jnp.bfloat16)] * shares,
        in_specs=[
            pl.BlockSpec(memory_space=pltpu.SMEM),
            pl.BlockSpec(memory_space=pltpu.VMEM),
        ],
        out_specs=[pl.BlockSpec(memory_space=pltpu.VMEM)] * shares,
        compiler_params=pltpu.CompilerParams(vmem_limit_bytes=16 * MIB),
        name="pick_pieces",
    )(requests, held)


def delivery_order(shares):
    half, quarter = shares // 2, shares // 4
    apart = zip(range(half, half + quarter), range(quarter, half))
    return [*range(1, quarter), *[s for pair in apart for s in pair], *range(half + quarter, shares)]


def deliver(pieces, devices):
    order = delivery_order(len(pieces))
    return [pieces[0]] + [swap(pieces[step], step, devices) for step in order]


FACTOR = math.log2(math.e) / math.sqrt(HEAD_SIZE)
PAIR = 2
LARGE_SUM = 2.0**100


def head_lanes(head):
    return slice(head * HEAD_SIZE, (head + 1) * HEAD_SIZE)


def with_ones(value):
    return jnp.concatenate([value, jnp.ones_like(value)], axis=1)


def inverse_of(positive):
    return pl.reciprocal(positive, approx=True)


def dot(a, b):
    return jnp.dot(a, b, preferred_element_type=jnp.float32)


def stack_heads(wide):
    heads = wide.shape[1] // HEAD_SIZE
    return jnp.concatenate([wide[:, head_lanes(h)] for h in range(heads)], axis=0)


def own_kernel(query_ref, key_ref, value_ref, out_ref, level_ref):
    rows = query_ref.shape[0]
    row = lax.broadcasted_iota(jnp.int32, (rows, rows), 0)
    column = lax.broadcasted_iota(jnp.int32, (rows, rows), 1)
    causal = column <= row
    lane = lax.broadcasted_iota(jnp.int32, (rows, HEAD_SIZE), 1)
    keys_across = key_ref[...].T
    value = with_ones(value_ref[...])

    def score(first):
        lanes = slice(first * HEAD_SIZE, (first + PAIR) * HEAD_SIZE)
        return dot(stack_heads(query_ref[:, lanes]), keys_across)

    def finish(first, scores):
        weights, shifts = [], []
        for h in range(PAIR):
            part = jnp.where(causal, scores[h * rows : (h + 1) * rows], -1e30)
            shift = jnp.max(part, axis=1, keepdims=True) * FACTOR
            shifts.append(shift)
            weights.append(jnp.exp2(part * FACTOR - shift).astype(jnp.bfloat16))
        both = dot(jnp.concatenate(weights, axis=0), value)
        for h in range(PAIR):
            part = both[h * rows : (h + 1) * rows]
            row_sum = part[:, HEAD_SIZE:]
            out_ref[:, head_lanes(first + h)] = part[:, :HEAD_SIZE] / row_sum
            level = shifts[h] + jnp.log2(row_sum)
            level_ref[...] = jnp.where(lane == first + h, level, level_ref[...])

    level_ref[...] = jnp.zeros_like(level_ref)
    scores = score(0)
    for first in range(0, GROUP, PAIR):
        following = score(first + PAIR) if first + PAIR < GROUP else None
        finish(first, scores)
        scores = following


def own_attention(queries, keys, values):
    rows = queries.shape[0]
    width = GROUP * HEAD_SIZE
    scores = QUERY_HEADS * rows * rows
    return pl.pallas_call(
        own_kernel,
        out_shape=[
            pltpu.HBM(queries.shape, jnp.float32),
            pltpu.HBM((rows, KEY_VALUE_HEADS * HEAD_SIZE), jnp.float32),
        ],
        grid=(KEY_VALUE_HEADS,),
        in_specs=[
            pl.BlockSpec((rows, width), lambda g: (0, g)),
            pl.BlockSpec((rows, HEAD_SIZE), lambda g: (0, g)),
            pl.BlockSpec((rows, HEAD_SIZE), lambda g: (0, g)),
        ],
        out_specs=[
            pl.BlockSpec((rows, width), lambda g: (0, g)),
            pl.BlockSpec((rows, HEAD_SIZE), lambda g: (0, g)),
        ],
        compiler_params=pltpu.CompilerParams(vmem_limit_bytes=16 * MIB),
        cost_estimate=pl.CostEstimate(
            flops=4 * scores * HEAD_SIZE, bytes_accessed=7 * MIB, transcendentals=scores
        ),
        name="own_attention",
    )(queries, keys, values)


def far_kernel(selected_ref, query_ref, own_in, level_in, *refs, first_call, last):
    own_ref, level_ref = own_in, level_in
    if last:
        *far_refs, out_ref, staged, sems = refs
    elif first_call:
        *far_refs, out_ref, new_level_ref, own_ref, level_ref, sems = refs
    else:
        *far_refs, out_ref, new_level_ref = refs
    rows = query_ref.shape[0]
    width = GROUP * HEAD_SIZE

    def wide(group):
        start = group * width
        return pl.ds(start if isinstance(group, int) else pl.multiple_of(start, width), width)

    def narrow(group):
        start = group * HEAD_SIZE
        fixed = isinstance(group, int)
        return pl.ds(start if fixed else pl.multiple_of(start, HEAD_SIZE), HEAD_SIZE)

    def level_of(group, head):
        if not first_call:
            return level_ref[:, head_of(group, head)]
        one = level_ref[:, narrow(group)][:, head : head + 1]
        return jnp.broadcast_to(one, (rows, HEAD_SIZE))

    def fetch(group, which):
        source, target = ((own_in, own_ref), (level_in, level_ref))[which]
        lanes = wide(group) if which == 0 else narrow(group)
        return pltpu.make_async_copy(
            source.at[:, lanes], target.at[:, lanes], sems.at[which, group]
        )

    def send(group):
        lanes = wide(group)
        return pltpu.make_async_copy(staged.at[:, lanes], out_ref.at[:, lanes], sems.at[group])

    if first_call:
        for group in range(KEY_VALUE_HEADS):
            fetch(group, 1).start()
            fetch(group, 0).start()

    def head_of(group, head):
        start = (group * GROUP + head) * HEAD_SIZE
        fixed = isinstance(group, int)
        return pl.ds(start if fixed else pl.multiple_of(start, HEAD_SIZE), HEAD_SIZE)

    def store(lanes, mixture, row_sum, level):
        result = mixture * inverse_of(row_sum)
        if last:
            staged[:, lanes] = result.astype(staged.dtype)
        else:
            out_ref[:, lanes] = result
            new_level_ref[:, lanes] = level + jnp.log2(row_sum)

    def attend(picks):
        count = len(picks) * sum(ref.shape[2] for ref in far_refs)

        def block(slot):
            return jnp.concatenate([ref[p, slot] for p in picks for ref in far_refs], axis=0)

        def keys_and_values(group):
            return block(group).T, with_ones(block(group + KEY_VALUE_HEADS))

        def repeat(narrow):
            whole = jnp.concatenate([narrow] * pl.cdiv(count, HEAD_SIZE), axis=1)
            return whole[:, :count]

        def quick(group, head, scores, value, largest):
            lanes = head_of(group, head)
            level = level_of(group, head)
            weights = jnp.exp2(scores * FACTOR - repeat(level)).astype(jnp.bfloat16)
            both = dot(weights, value)
            row_sum = 1.0 + both[:, HEAD_SIZE:]
            store(lanes, own_ref[:, lanes] + both[:, :HEAD_SIZE], row_sum, level)
            return jnp.maximum(
                largest, jnp.max(row_sum.reshape(rows // 8, 8, HEAD_SIZE), axis=0)
            )

        def careful(group, head, scores, value):
            lanes = head_of(group, head)
            part = scores * FACTOR
            level = level_of(group, head)
            shift = jnp.maximum(jnp.max(part, axis=1, keepdims=True), level)
            weights = jnp.exp2(part - repeat(shift)).astype(jnp.bfloat16)
            both = dot(weights, value)
            share = jnp.exp2(level - shift)
            mixture = own_ref[:, lanes] * share + both[:, :HEAD_SIZE]
            store(lanes, mixture, share + both[:, HEAD_SIZE:], shift)

        def score(group, head, keys_across):
            return dot(query_ref[:, head_of(group, head)], keys_across)

        largest = jnp.zeros((8, HEAD_SIZE), jnp.float32)
        order = [(g, h) for g in range(KEY_VALUE_HEADS) for h in range(GROUP)]
        held = {0: keys_and_values(0)}
        scores = score(0, 0, held[0][0])
        for (group, head), later in zip(order, order[1:] + [None]):
            following = None
            if later is not None:
                if later[0] not in held:
                    held[later[0]] = keys_and_values(later[0])
                following = score(*later, held[later[0]][0])
            if head == 0 and first_call:
                fetch(group, 1).wait()
                fetch(group, 0).wait()
            largest = quick(group, head, scores, held[group][1], largest)
            if head == GROUP - 1 and last:
                send(group).start()
            scores = following

        @pl.when(jnp.max(largest) > LARGE_SUM)
        def _():
            @pl.loop(0, KEY_VALUE_HEADS)
            def _(group):
                if last:
                    send(group).wait()
                keys_across, value = keys_and_values(group)
                for head in range(GROUP):
                    careful(group, head, score(group, head, keys_across), value)
                if last:
                    send(group).start()

    my_block = lax.axis_index("ctx")
    chosen = selected_ref[0, 0], selected_ref[0, 1]
    first = chosen[0] < my_block
    second = jnp.logical_and(chosen[1] < my_block, chosen[1] != chosen[0])
    valid = first.astype(jnp.int32) + second.astype(jnp.int32)

    @pl.when(valid == 2)
    def _():
        attend((0, 1))

    @pl.when(valid == 1)
    def _():
        attend((second.astype(jnp.int32),))

    @pl.when(valid == 0)
    def _():
        @pl.loop(0, KEY_VALUE_HEADS)
        def _(group):
            lanes = wide(group)
            if last:
                staged[:, lanes] = own_ref[:, lanes].astype(staged.dtype)
                send(group).start()
            else:
                if first_call:
                    fetch(group, 1).wait()
                    fetch(group, 0).wait()
                out_ref[:, lanes] = own_ref[:, lanes]
                for head in range(GROUP):
                    new_level_ref[:, head_of(group, head)] = level_of(group, head)

    if last:

        @pl.loop(0, KEY_VALUE_HEADS)
        def _(group):
            send(group).wait()


def far_attention(selected, queries, own, level, far, first_call=False, last=False):
    rows = queries.shape[0]
    scores = QUERY_HEADS * rows * 2 * sum(piece.shape[2] for piece in far)
    in_vmem = pl.BlockSpec(memory_space=pltpu.VMEM)
    anywhere = pl.BlockSpec(memory_space=pl.ANY)
    earlier, scratch = in_vmem, []
    out_shape, out_specs = [jax.ShapeDtypeStruct(queries.shape, jnp.float32)] * 2, [in_vmem] * 2
    if first_call:
        earlier = anywhere
        own = pltpu.with_memory_space_constraint(own, pltpu.HBM)
        level = pltpu.with_memory_space_constraint(level, pltpu.HBM)
        scratch = [
            pltpu.VMEM(own.shape, jnp.float32),
            pltpu.VMEM(level.shape, jnp.float32),
            pltpu.SemaphoreType.DMA((2, KEY_VALUE_HEADS)),
        ]
    if last:
        out_shape = jax.ShapeDtypeStruct(queries.shape, jnp.bfloat16)
        out_specs = anywhere
        scratch = [
            pltpu.VMEM(queries.shape, jnp.bfloat16),
            pltpu.SemaphoreType.DMA((KEY_VALUE_HEADS,)),
        ]
    return pl.pallas_call(
        functools.partial(far_kernel, first_call=first_call, last=last),
        out_shape=out_shape,
        in_specs=[
            pl.BlockSpec(memory_space=pltpu.SMEM),
            in_vmem,
            earlier,
            earlier,
            *[in_vmem] * len(far),
        ],
        out_specs=out_specs,
        scratch_shapes=scratch,
        compiler_params=pltpu.CompilerParams(vmem_limit_bytes=30 * MIB),
        cost_estimate=pl.CostEstimate(
            flops=4 * scores * HEAD_SIZE, bytes_accessed=10 * MIB, transcendentals=scores
        ),
        name="early_attention" if first_call else "late_attention" if last else "middle_attention",
    )(selected, queries, own, level, *far)


def local(queries, all_key_states, all_value_states, selected):
    devices = lax.axis_size("ctx")
    rows = all_key_states.shape[0]
    piece_rows = rows * COPIES // devices
    packed = pack(all_key_states, all_value_states, devices)
    packed, queries = lax.optimization_barrier((packed, queries))
    held = lax.all_to_all(packed, "ctx", split_axis=0, concat_axis=0, tiled=True)
    own, level = own_attention(queries, all_key_states, all_value_states)
    mine, own, level = lax.optimization_barrier((selected, own, level))
    requests = exchange_requests(mine, devices // COPIES, devices)
    requests = jnp.clip(requests, 0, devices - 1)
    moved = deliver(pick_pieces(requests, held), devices)
    far = [m.reshape(2, SLOTS, piece_rows, HEAD_SIZE) for m in moved]
    half, quarter = len(far) // 2, len(far) // 4
    parts = [far[:half], far[half:-quarter], far[-quarter:]]
    if piece_rows % 16 != 0:
        parts = [[jnp.concatenate(part, axis=2)] for part in parts]
    own, level = far_attention(selected, queries, own, level, parts[0], first_call=True)
    own, level = far_attention(selected, queries, own, level, parts[1])
    return far_attention(selected, queries, own, level, parts[2], last=True)


def solution(mesh):
    placed = P(("groups", "ctx"), None)
    return jax.shard_map(
        local, mesh=mesh, in_specs=(placed,) * 4, out_specs=placed, check_vma=False
    )
```

```python
import functools
import math

import jax
import jax.numpy as jnp
from jax import lax
from jax.experimental import pallas as pl
from jax.experimental.pallas import tpu as pltpu
from jax.sharding import PartitionSpec as P

QUERY_HEADS = 32
KEY_VALUE_HEADS = 4
HEAD_SIZE = 128
GROUP = QUERY_HEADS // KEY_VALUE_HEADS
SLOTS = 2 * KEY_VALUE_HEADS
COPIES = 2
MIB = 1024 * 1024


def pack_kernel(key_ref, value_ref, out_ref, staged, arrived, left):
    shares, piece_rows, _ = key_ref.shape
    half = KEY_VALUE_HEADS * piece_rows

    def take(slot):
        ref = key_ref if slot < KEY_VALUE_HEADS else value_ref
        head = slot % KEY_VALUE_HEADS
        lanes = pl.ds(head * HEAD_SIZE, HEAD_SIZE)
        rows = pl.ds(slot * piece_rows, piece_rows)
        return pltpu.make_async_copy(
            ref.at[:, :, lanes], staged.at[:, rows, :], arrived.at[slot]
        )

    def give(which, copy):
        rows = pl.ds(which * half, half)
        return pltpu.make_async_copy(
            staged.at[:, rows, :],
            out_ref.at[pl.ds(copy * shares, shares), rows, :],
            left.at[which, copy],
        )

    for slot in range(SLOTS):
        take(slot).start()
    for which in range(2):
        for head in range(KEY_VALUE_HEADS):
            take(which * KEY_VALUE_HEADS + head).wait()
        for copy in range(COPIES):
            give(which, copy).start()
    for which in range(2):
        for copy in range(COPIES):
            give(which, copy).wait()


def pack(keys, values, devices):
    shares = devices // COPIES
    piece_rows = keys.shape[0] // shares
    if piece_rows % 16 == 0:
        split = (shares, piece_rows, keys.shape[1])
        return pl.pallas_call(
            pack_kernel,
            out_shape=jax.ShapeDtypeStruct(
                (devices, SLOTS * piece_rows, HEAD_SIZE), jnp.bfloat16
            ),
            in_specs=[pl.BlockSpec(memory_space=pl.ANY)] * 2,
            out_specs=pl.BlockSpec(memory_space=pl.ANY),
            scratch_shapes=[
                pltpu.VMEM((shares, SLOTS * piece_rows, HEAD_SIZE), jnp.bfloat16),
                pltpu.SemaphoreType.DMA((SLOTS,)),
                pltpu.SemaphoreType.DMA((2, COPIES)),
            ],
            name="pack",
        )(keys.reshape(split), values.reshape(split))
    both = jnp.concatenate([keys, values], axis=1)
    both = both.reshape(shares, piece_rows, SLOTS, HEAD_SIZE).transpose(0, 2, 1, 3)
    both = both.reshape(shares, SLOTS * piece_rows, HEAD_SIZE)
    return jnp.concatenate([both] * COPIES, axis=0)


def partner(position, step):
    return position ^ step


def swap(array, step, devices):
    return lax.ppermute(array, "ctx", [(i, partner(i, step)) for i in range(devices)])


def exchange_requests(selected, shares, devices):
    requests = selected
    step = 1
    while step < shares:
        requests = jnp.concatenate([requests, swap(requests, step, devices)], axis=0)
        step *= 2
    return requests


def pick_kernel(requests_ref, held_ref, *out_refs):
    for step, out_ref in enumerate(out_refs):
        for pick in range(2):
            out_ref[pick] = held_ref[requests_ref[step, pick]]


def pick_pieces(requests, held):
    devices, rows, _ = held.shape
    shares = devices // COPIES
    return pl.pallas_call(
        pick_kernel,
        out_shape=[jax.ShapeDtypeStruct((2, rows, HEAD_SIZE), jnp.bfloat16)] * shares,
        in_specs=[
            pl.BlockSpec(memory_space=pltpu.SMEM),
            pl.BlockSpec(memory_space=pltpu.VMEM),
        ],
        out_specs=[pl.BlockSpec(memory_space=pltpu.VMEM)] * shares,
        compiler_params=pltpu.CompilerParams(vmem_limit_bytes=16 * MIB),
        name="pick_pieces",
    )(requests, held)


def delivery_order(shares):
    half, quarter = shares // 2, shares // 4
    apart = zip(range(half, half + quarter), range(quarter, half))
    return [*range(1, quarter), *[s for pair in apart for s in pair], *range(half + quarter, shares)]


def deliver(pieces, devices):
    order = delivery_order(len(pieces))
    return [pieces[0]] + [swap(pieces[step], step, devices) for step in order]


FACTOR = math.log2(math.e) / math.sqrt(HEAD_SIZE)
PAIR = 2
LARGE_SUM = 2.0**100


def head_lanes(head):
    return slice(head * HEAD_SIZE, (head + 1) * HEAD_SIZE)


def with_ones(value):
    return jnp.concatenate([value, jnp.ones_like(value)], axis=1)


def inverse_of(positive):
    return pl.reciprocal(positive, approx=True)


def dot(a, b):
    return jnp.dot(a, b, preferred_element_type=jnp.float32)


def stack_heads(wide):
    heads = wide.shape[1] // HEAD_SIZE
    return jnp.concatenate([wide[:, head_lanes(h)] for h in range(heads)], axis=0)


def own_kernel(query_ref, key_ref, value_ref, out_ref, level_ref):
    rows = query_ref.shape[0]
    row = lax.broadcasted_iota(jnp.int32, (rows, rows), 0)
    column = lax.broadcasted_iota(jnp.int32, (rows, rows), 1)
    causal = column <= row
    lane = lax.broadcasted_iota(jnp.int32, (rows, HEAD_SIZE), 1)
    keys_across = key_ref[...].T
    value = with_ones(value_ref[...])

    def score(first):
        lanes = slice(first * HEAD_SIZE, (first + PAIR) * HEAD_SIZE)
        return dot(stack_heads(query_ref[:, lanes]), keys_across)

    def finish(first, scores):
        weights, shifts = [], []
        for h in range(PAIR):
            part = jnp.where(causal, scores[h * rows : (h + 1) * rows], -1e30)
            shift = jnp.max(part, axis=1, keepdims=True) * FACTOR
            shifts.append(shift)
            weights.append(jnp.exp2(part * FACTOR - shift).astype(jnp.bfloat16))
        both = dot(jnp.concatenate(weights, axis=0), value)
        for h in range(PAIR):
            part = both[h * rows : (h + 1) * rows]
            row_sum = part[:, HEAD_SIZE:]
            out_ref[:, head_lanes(first + h)] = part[:, :HEAD_SIZE] / row_sum
            level = shifts[h] + jnp.log2(row_sum)
            level_ref[...] = jnp.where(lane == first + h, level, level_ref[...])

    level_ref[...] = jnp.zeros_like(level_ref)
    scores = score(0)
    for first in range(0, GROUP, PAIR):
        following = score(first + PAIR) if first + PAIR < GROUP else None
        finish(first, scores)
        scores = following


def own_attention(queries, keys, values):
    rows = queries.shape[0]
    width = GROUP * HEAD_SIZE
    scores = QUERY_HEADS * rows * rows
    return pl.pallas_call(
        own_kernel,
        out_shape=[
            pltpu.HBM(queries.shape, jnp.float32),
            pltpu.HBM((rows, KEY_VALUE_HEADS * HEAD_SIZE), jnp.float32),
        ],
        grid=(KEY_VALUE_HEADS,),
        in_specs=[
            pl.BlockSpec((rows, width), lambda g: (0, g)),
            pl.BlockSpec((rows, HEAD_SIZE), lambda g: (0, g)),
            pl.BlockSpec((rows, HEAD_SIZE), lambda g: (0, g)),
        ],
        out_specs=[
            pl.BlockSpec((rows, width), lambda g: (0, g)),
            pl.BlockSpec((rows, HEAD_SIZE), lambda g: (0, g)),
        ],
        compiler_params=pltpu.CompilerParams(vmem_limit_bytes=16 * MIB),
        cost_estimate=pl.CostEstimate(
            flops=4 * scores * HEAD_SIZE, bytes_accessed=7 * MIB, transcendentals=scores
        ),
        name="own_attention",
    )(queries, keys, values)


def far_kernel(selected_ref, query_ref, own_in, level_in, *refs, last):
    if last:
        *far_refs, out_ref, staged, sems = refs
        own_ref, level_ref = own_in, level_in
    else:
        *far_refs, out_ref, new_level_ref, own_ref, level_ref, sems = refs
    rows = query_ref.shape[0]
    width = GROUP * HEAD_SIZE

    def wide(group):
        start = group * width
        return pl.ds(start if isinstance(group, int) else pl.multiple_of(start, width), width)

    def narrow(group):
        start = group * HEAD_SIZE
        fixed = isinstance(group, int)
        return pl.ds(start if fixed else pl.multiple_of(start, HEAD_SIZE), HEAD_SIZE)

    def level_of(group, head):
        if last:
            return level_ref[:, head_of(group, head)]
        one = level_ref[:, narrow(group)][:, head : head + 1]
        return jnp.broadcast_to(one, (rows, HEAD_SIZE))

    def fetch(group, which):
        source, target = ((own_in, own_ref), (level_in, level_ref))[which]
        lanes = wide(group) if which == 0 else narrow(group)
        return pltpu.make_async_copy(
            source.at[:, lanes], target.at[:, lanes], sems.at[which, group]
        )

    def send(group):
        lanes = wide(group)
        return pltpu.make_async_copy(staged.at[:, lanes], out_ref.at[:, lanes], sems.at[group])

    if not last:
        for group in range(KEY_VALUE_HEADS):
            fetch(group, 1).start()
            fetch(group, 0).start()

    def head_of(group, head):
        start = (group * GROUP + head) * HEAD_SIZE
        fixed = isinstance(group, int)
        return pl.ds(start if fixed else pl.multiple_of(start, HEAD_SIZE), HEAD_SIZE)

    def store(lanes, mixture, row_sum, level):
        result = mixture * inverse_of(row_sum)
        if last:
            staged[:, lanes] = result.astype(staged.dtype)
        else:
            out_ref[:, lanes] = result
            new_level_ref[:, lanes] = level + jnp.log2(row_sum)

    def attend(picks):
        count = len(picks) * sum(ref.shape[2] for ref in far_refs)

        def block(slot):
            return jnp.concatenate([ref[p, slot] for p in picks for ref in far_refs], axis=0)

        def keys_and_values(group):
            value = block(group + KEY_VALUE_HEADS)
            return block(group).T, value if last else with_ones(value)

        def repeat(narrow):
            return jnp.concatenate([narrow] * (count // HEAD_SIZE), axis=1)

        def total(both, weights):
            if last:
                return jnp.sum(weights.astype(jnp.float32), axis=1, keepdims=True)
            return both[:, HEAD_SIZE:]

        def quick(group, head, scores, value, largest):
            lanes = head_of(group, head)
            level = level_of(group, head)
            weights = jnp.exp2(scores * FACTOR - repeat(level)).astype(jnp.bfloat16)
            both = dot(weights, value)
            row_sum = 1.0 + total(both, weights)
            store(lanes, own_ref[:, lanes] + both[:, :HEAD_SIZE], row_sum, level)
            row_sum = jnp.broadcast_to(row_sum, (rows, HEAD_SIZE))
            return jnp.maximum(
                largest, jnp.max(row_sum.reshape(rows // 8, 8, HEAD_SIZE), axis=0)
            )

        def careful(group, head, scores, value):
            lanes = head_of(group, head)
            part = scores * FACTOR
            level = level_of(group, head)
            shift = jnp.maximum(jnp.max(part, axis=1, keepdims=True), level)
            weights = jnp.exp2(part - repeat(shift)).astype(jnp.bfloat16)
            both = dot(weights, value)
            share = jnp.exp2(level - shift)
            mixture = own_ref[:, lanes] * share + both[:, :HEAD_SIZE]
            store(lanes, mixture, share + total(both, weights), shift)

        def score(group, head, keys_across):
            return dot(query_ref[:, head_of(group, head)], keys_across)

        largest = jnp.zeros((8, HEAD_SIZE), jnp.float32)
        order = [(g, h) for g in range(KEY_VALUE_HEADS) for h in range(GROUP)]
        held = {0: keys_and_values(0)}
        scores = score(0, 0, held[0][0])
        for (group, head), later in zip(order, order[1:] + [None]):
            following = None
            if later is not None:
                if later[0] not in held:
                    held[later[0]] = keys_and_values(later[0])
                following = score(*later, held[later[0]][0])
            if head == 0 and not last:
                fetch(group, 1).wait()
                fetch(group, 0).wait()
            largest = quick(group, head, scores, held[group][1], largest)
            if head == GROUP - 1 and last:
                send(group).start()
            scores = following

        @pl.when(jnp.max(largest) > LARGE_SUM)
        def _():
            @pl.loop(0, KEY_VALUE_HEADS)
            def _(group):
                if last:
                    send(group).wait()
                keys_across, value = keys_and_values(group)
                for head in range(GROUP):
                    careful(group, head, score(group, head, keys_across), value)
                if last:
                    send(group).start()

    my_block = lax.axis_index("ctx")
    chosen = selected_ref[0, 0], selected_ref[0, 1]
    first = chosen[0] < my_block
    second = jnp.logical_and(chosen[1] < my_block, chosen[1] != chosen[0])
    valid = first.astype(jnp.int32) + second.astype(jnp.int32)

    @pl.when(valid == 2)
    def _():
        attend((0, 1))

    @pl.when(valid == 1)
    def _():
        attend((second.astype(jnp.int32),))

    @pl.when(valid == 0)
    def _():
        @pl.loop(0, KEY_VALUE_HEADS)
        def _(group):
            lanes = wide(group)
            if last:
                staged[:, lanes] = own_ref[:, lanes].astype(staged.dtype)
                send(group).start()
            else:
                fetch(group, 1).wait()
                fetch(group, 0).wait()
                out_ref[:, lanes] = own_ref[:, lanes]
                for head in range(GROUP):
                    new_level_ref[:, head_of(group, head)] = level_of(group, head)

    if last:

        @pl.loop(0, KEY_VALUE_HEADS)
        def _(group):
            send(group).wait()


def far_attention(selected, queries, own, level, far, last):
    rows = queries.shape[0]
    scores = QUERY_HEADS * rows * 2 * sum(piece.shape[2] for piece in far)
    in_vmem = pl.BlockSpec(memory_space=pltpu.VMEM)
    anywhere = pl.BlockSpec(memory_space=pl.ANY)
    if last:
        earlier = in_vmem
        out_shape = jax.ShapeDtypeStruct(queries.shape, jnp.bfloat16)
        out_specs = anywhere
        scratch = [
            pltpu.VMEM(queries.shape, jnp.bfloat16),
            pltpu.SemaphoreType.DMA((KEY_VALUE_HEADS,)),
        ]
    else:
        earlier = anywhere
        own = pltpu.with_memory_space_constraint(own, pltpu.HBM)
        level = pltpu.with_memory_space_constraint(level, pltpu.HBM)
        out_shape = [jax.ShapeDtypeStruct(queries.shape, jnp.float32)] * 2
        out_specs = [in_vmem] * 2
        scratch = [
            pltpu.VMEM(queries.shape, jnp.float32),
            pltpu.VMEM(level.shape, jnp.float32),
            pltpu.SemaphoreType.DMA((2, KEY_VALUE_HEADS)),
        ]
    return pl.pallas_call(
        functools.partial(far_kernel, last=last),
        out_shape=out_shape,
        in_specs=[
            pl.BlockSpec(memory_space=pltpu.SMEM),
            in_vmem,
            earlier,
            earlier,
            *[in_vmem] * len(far),
        ],
        out_specs=out_specs,
        scratch_shapes=scratch,
        compiler_params=pltpu.CompilerParams(vmem_limit_bytes=30 * MIB),
        cost_estimate=pl.CostEstimate(
            flops=4 * scores * HEAD_SIZE, bytes_accessed=10 * MIB, transcendentals=scores
        ),
        name="late_attention" if last else "early_attention",
    )(selected, queries, own, level, *far)


def local(queries, all_key_states, all_value_states, selected):
    devices = lax.axis_size("ctx")
    rows = all_key_states.shape[0]
    piece_rows = rows * COPIES // devices
    packed = pack(all_key_states, all_value_states, devices)
    packed, queries = lax.optimization_barrier((packed, queries))
    held = lax.all_to_all(packed, "ctx", split_axis=0, concat_axis=0, tiled=True)
    own, level = own_attention(queries, all_key_states, all_value_states)
    mine, own, level = lax.optimization_barrier((selected, own, level))
    requests = exchange_requests(mine, devices // COPIES, devices)
    requests = jnp.clip(requests, 0, devices - 1)
    moved = deliver(pick_pieces(requests, held), devices)
    far = [m.reshape(2, SLOTS, piece_rows, HEAD_SIZE) for m in moved]
    early, late = far[: len(far) // 2], far[len(far) // 2 :]
    if piece_rows % 16 != 0:
        early, late = [jnp.concatenate(early, axis=2)], [jnp.concatenate(late, axis=2)]
    own, level = far_attention(selected, queries, own, level, early, last=False)
    return far_attention(selected, queries, own, level, late, last=True)


def solution(mesh):
    placed = P(("groups", "ctx"), None)
    return jax.shard_map(
        local, mesh=mesh, in_specs=(placed,) * 4, out_specs=placed, check_vma=False
    )
```

```python
import functools
import math

import jax
import jax.numpy as jnp
from jax import lax
from jax.experimental import pallas as pl
from jax.experimental.pallas import tpu as pltpu
from jax.sharding import PartitionSpec as P

QUERY_HEADS = 32
KEY_VALUE_HEADS = 4
HEAD_SIZE = 128
GROUP = QUERY_HEADS // KEY_VALUE_HEADS
MIB = 1024 * 1024


def partner(position, step):
    return position ^ step


def swap(array, step, devices):
    return lax.ppermute(array, "ctx", [(i, partner(i, step)) for i in range(devices)])


def exchange_requests(selected, shares, devices):
    requests = selected
    step = 1
    while step < shares:
        requests = jnp.concatenate([requests, swap(requests, step, devices)], axis=0)
        step *= 2
    return requests


def cut_kernel(*refs, run):
    in_refs, out_refs = refs[:-run], refs[-run:]
    rows = in_refs[0].shape[0] // run
    me = lax.rem(lax.axis_index("ctx"), run)
    for step, out_ref in enumerate(out_refs):
        share = pl.ds(pl.multiple_of(partner(me, step) * rows, rows), rows)
        parts = [
            ref[share, head * HEAD_SIZE : (head + 1) * HEAD_SIZE]
            for ref in in_refs
            for head in range(KEY_VALUE_HEADS)
        ]
        out_ref[...] = jnp.concatenate(parts, axis=0)


def cut(arrays, run):
    rows = arrays[0].shape[0] // run
    heads = len(arrays) * KEY_VALUE_HEADS
    if rows % 16 == 0:
        in_vmem = pl.BlockSpec(memory_space=pltpu.VMEM)
        return pl.pallas_call(
            functools.partial(cut_kernel, run=run),
            out_shape=[jax.ShapeDtypeStruct((heads * rows, HEAD_SIZE), jnp.bfloat16)] * run,
            in_specs=[in_vmem] * len(arrays),
            out_specs=[in_vmem] * run,
            compiler_params=pltpu.CompilerParams(vmem_limit_bytes=16 * MIB),
            name="cut",
        )(*arrays)
    whole = jnp.concatenate(arrays, axis=1).reshape(run, rows, heads, HEAD_SIZE)
    whole = whole.transpose(0, 2, 1, 3).reshape(run, heads * rows, HEAD_SIZE)
    me = lax.rem(lax.axis_index("ctx"), run)
    whole = jnp.take(whole, partner(jnp.arange(run), me), axis=0)
    return [whole[step] for step in range(run)]


def pick_kernel(requests_ref, *refs, run, start):
    near_refs, over_refs = refs[:run], refs[run : 2 * run]
    out_refs, held_ref = refs[2 * run : -1], refs[-1]
    rows = held_ref.shape[1]
    for step in range(run):
        held_ref[step] = near_refs[step][start : start + rows]
        held_ref[run + step] = over_refs[step][...]
    me = lax.axis_index("ctx")
    for step, out_ref in enumerate(out_refs):
        for pick in range(2):
            block = requests_ref[step, pick]
            place = partner(lax.rem(block, run), lax.rem(me, run))
            other_run = (lax.div(block, run) != lax.div(me, run)).astype(jnp.int32)
            out_ref[pick] = held_ref[place + run * other_run]


def pick_pieces(requests, near, over, start):
    run, rows = len(near), over[0].shape[0]
    in_vmem = pl.BlockSpec(memory_space=pltpu.VMEM)
    return pl.pallas_call(
        functools.partial(pick_kernel, run=run, start=start),
        out_shape=[jax.ShapeDtypeStruct((2, rows, HEAD_SIZE), jnp.bfloat16)] * run,
        in_specs=[pl.BlockSpec(memory_space=pltpu.SMEM), *[in_vmem] * (2 * run)],
        out_specs=[in_vmem] * run,
        scratch_shapes=[pltpu.VMEM((2 * run, rows, HEAD_SIZE), jnp.bfloat16)],
        compiler_params=pltpu.CompilerParams(vmem_limit_bytes=16 * MIB),
        name="pick_pieces",
    )(requests, *near, *over)


def delivery_order(shares):
    half, quarter = shares // 2, shares // 4
    apart = zip(range(half, half + quarter), range(quarter, half))
    return [*range(1, quarter), *[s for pair in apart for s in pair], *range(half + quarter, shares)]


def trade(pieces, devices):
    moved = {0: pieces[0]}
    for step in delivery_order(len(pieces)):
        moved[step] = swap(pieces[step], step, devices)
    return [moved[step] for step in range(len(pieces))]


FACTOR = math.log2(math.e) / math.sqrt(HEAD_SIZE)
PAIR = 2
LARGE_SUM = 2.0**100


def head_lanes(head):
    return slice(head * HEAD_SIZE, (head + 1) * HEAD_SIZE)


def with_ones(value):
    return jnp.concatenate([value, jnp.ones_like(value)], axis=1)


def inverse_of(positive):
    return pl.reciprocal(positive, approx=True)


def dot(a, b):
    return jnp.dot(a, b, preferred_element_type=jnp.float32)


def stack_heads(wide):
    heads = wide.shape[1] // HEAD_SIZE
    return jnp.concatenate([wide[:, head_lanes(h)] for h in range(heads)], axis=0)


def own_kernel(query_ref, key_ref, value_ref, out_ref, level_ref):
    rows = query_ref.shape[0]
    row = lax.broadcasted_iota(jnp.int32, (rows, rows), 0)
    column = lax.broadcasted_iota(jnp.int32, (rows, rows), 1)
    causal = column <= row
    lane = lax.broadcasted_iota(jnp.int32, (rows, HEAD_SIZE), 1)
    keys_across = key_ref[...].T
    value = with_ones(value_ref[...])

    def score(first):
        lanes = slice(first * HEAD_SIZE, (first + PAIR) * HEAD_SIZE)
        return dot(stack_heads(query_ref[:, lanes]), keys_across)

    def finish(first, scores):
        weights, shifts = [], []
        for h in range(PAIR):
            part = jnp.where(causal, scores[h * rows : (h + 1) * rows], -1e30)
            shift = jnp.max(part, axis=1, keepdims=True) * FACTOR
            shifts.append(shift)
            weights.append(jnp.exp2(part * FACTOR - shift).astype(jnp.bfloat16))
        both = dot(jnp.concatenate(weights, axis=0), value)
        for h in range(PAIR):
            part = both[h * rows : (h + 1) * rows]
            row_sum = part[:, HEAD_SIZE:]
            out_ref[:, head_lanes(first + h)] = part[:, :HEAD_SIZE] / row_sum
            level = shifts[h] + jnp.log2(row_sum)
            level_ref[...] = jnp.where(lane == first + h, level, level_ref[...])

    level_ref[...] = jnp.zeros_like(level_ref)
    scores = score(0)
    for first in range(0, GROUP, PAIR):
        following = score(first + PAIR) if first + PAIR < GROUP else None
        finish(first, scores)
        scores = following


def own_attention(queries, keys, values):
    rows = queries.shape[0]
    width = GROUP * HEAD_SIZE
    scores = QUERY_HEADS * rows * rows
    return pl.pallas_call(
        own_kernel,
        out_shape=[
            pltpu.HBM(queries.shape, jnp.float32),
            pltpu.HBM((rows, KEY_VALUE_HEADS * HEAD_SIZE), jnp.float32),
        ],
        grid=(KEY_VALUE_HEADS,),
        in_specs=[
            pl.BlockSpec((rows, width), lambda g: (0, g)),
            pl.BlockSpec((rows, HEAD_SIZE), lambda g: (0, g)),
            pl.BlockSpec((rows, HEAD_SIZE), lambda g: (0, g)),
        ],
        out_specs=[
            pl.BlockSpec((rows, width), lambda g: (0, g)),
            pl.BlockSpec((rows, HEAD_SIZE), lambda g: (0, g)),
        ],
        compiler_params=pltpu.CompilerParams(vmem_limit_bytes=16 * MIB),
        cost_estimate=pl.CostEstimate(
            flops=4 * scores * HEAD_SIZE, bytes_accessed=7 * MIB, transcendentals=scores
        ),
        name="own_attention",
    )(queries, keys, values)


def far_kernel(selected_ref, query_ref, own_in, level_in, *refs, last):
    if last:
        *far_refs, out_ref, staged, sems = refs
        own_ref, level_ref = own_in, level_in
    else:
        *far_refs, out_ref, new_level_ref, own_ref, level_ref, sems = refs
    rows = query_ref.shape[0]
    width = GROUP * HEAD_SIZE

    def wide(group):
        start = group * width
        return pl.ds(start if isinstance(group, int) else pl.multiple_of(start, width), width)

    def narrow(group):
        start = group * HEAD_SIZE
        fixed = isinstance(group, int)
        return pl.ds(start if fixed else pl.multiple_of(start, HEAD_SIZE), HEAD_SIZE)

    def level_of(group, head):
        if last:
            return level_ref[:, head_of(group, head)]
        one = level_ref[:, narrow(group)][:, head : head + 1]
        return jnp.broadcast_to(one, (rows, HEAD_SIZE))

    def fetch(group, which):
        source, target = ((own_in, own_ref), (level_in, level_ref))[which]
        lanes = wide(group) if which == 0 else narrow(group)
        return pltpu.make_async_copy(
            source.at[:, lanes], target.at[:, lanes], sems.at[which, group]
        )

    def send(group):
        lanes = wide(group)
        return pltpu.make_async_copy(staged.at[:, lanes], out_ref.at[:, lanes], sems.at[group])

    if not last:
        for group in range(KEY_VALUE_HEADS):
            fetch(group, 1).start()
            fetch(group, 0).start()

    def head_of(group, head):
        start = (group * GROUP + head) * HEAD_SIZE
        fixed = isinstance(group, int)
        return pl.ds(start if fixed else pl.multiple_of(start, HEAD_SIZE), HEAD_SIZE)

    def store(lanes, mixture, row_sum, level):
        result = mixture * inverse_of(row_sum)
        if last:
            staged[:, lanes] = result.astype(staged.dtype)
        else:
            out_ref[:, lanes] = result
            new_level_ref[:, lanes] = level + jnp.log2(row_sum)

    def attend(picks):
        far_key_refs = far_refs[: len(far_refs) // 2]
        far_value_refs = far_refs[len(far_refs) // 2 :]
        count = len(picks) * sum(ref.shape[2] for ref in far_key_refs)

        def block(pieces, group):
            return jnp.concatenate([ref[p, group] for p in picks for ref in pieces], axis=0)

        def keys_and_values(group):
            return block(far_key_refs, group).T, with_ones(block(far_value_refs, group))

        def repeat(narrow):
            return jnp.concatenate([narrow] * (count // HEAD_SIZE), axis=1)

        def quick(group, head, scores, value, largest):
            lanes = head_of(group, head)
            level = level_of(group, head)
            weights = jnp.exp2(scores * FACTOR - repeat(level)).astype(jnp.bfloat16)
            both = dot(weights, value)
            row_sum = 1.0 + both[:, HEAD_SIZE:]
            store(lanes, own_ref[:, lanes] + both[:, :HEAD_SIZE], row_sum, level)
            return jnp.maximum(
                largest, jnp.max(row_sum.reshape(rows // 8, 8, HEAD_SIZE), axis=0)
            )

        def careful(group, head, scores, value):
            lanes = head_of(group, head)
            part = scores * FACTOR
            level = level_of(group, head)
            shift = jnp.maximum(jnp.max(part, axis=1, keepdims=True), level)
            weights = jnp.exp2(part - repeat(shift)).astype(jnp.bfloat16)
            both = dot(weights, value)
            share = jnp.exp2(level - shift)
            mixture = own_ref[:, lanes] * share + both[:, :HEAD_SIZE]
            store(lanes, mixture, share + both[:, HEAD_SIZE:], shift)

        def score(group, head, keys_across):
            return dot(query_ref[:, head_of(group, head)], keys_across)

        largest = jnp.zeros((8, HEAD_SIZE), jnp.float32)
        order = [(g, h) for g in range(KEY_VALUE_HEADS) for h in range(GROUP)]
        held = {0: keys_and_values(0)}
        scores = score(0, 0, held[0][0])
        for (group, head), later in zip(order, order[1:] + [None]):
            following = None
            if later is not None:
                if later[0] not in held:
                    held[later[0]] = keys_and_values(later[0])
                following = score(*later, held[later[0]][0])
            if head == 0 and not last:
                fetch(group, 1).wait()
                fetch(group, 0).wait()
            largest = quick(group, head, scores, held[group][1], largest)
            if head == GROUP - 1 and last:
                send(group).start()
            scores = following

        @pl.when(jnp.max(largest) > LARGE_SUM)
        def _():
            @pl.loop(0, KEY_VALUE_HEADS)
            def _(group):
                if last:
                    send(group).wait()
                keys_across, value = keys_and_values(group)
                for head in range(GROUP):
                    careful(group, head, score(group, head, keys_across), value)
                if last:
                    send(group).start()

    my_block = lax.axis_index("ctx")
    chosen = selected_ref[0, 0], selected_ref[0, 1]
    first = chosen[0] < my_block
    second = jnp.logical_and(chosen[1] < my_block, chosen[1] != chosen[0])
    valid = first.astype(jnp.int32) + second.astype(jnp.int32)

    @pl.when(valid == 2)
    def _():
        attend((0, 1))

    @pl.when(valid == 1)
    def _():
        attend((second.astype(jnp.int32),))

    @pl.when(valid == 0)
    def _():
        @pl.loop(0, KEY_VALUE_HEADS)
        def _(group):
            lanes = wide(group)
            if last:
                staged[:, lanes] = own_ref[:, lanes].astype(staged.dtype)
                send(group).start()
            else:
                fetch(group, 1).wait()
                fetch(group, 0).wait()
                out_ref[:, lanes] = own_ref[:, lanes]
                for head in range(GROUP):
                    new_level_ref[:, head_of(group, head)] = level_of(group, head)

    if last:

        @pl.loop(0, KEY_VALUE_HEADS)
        def _(group):
            send(group).wait()


def far_attention(selected, queries, own, level, far, last):
    rows = queries.shape[0]
    scores = QUERY_HEADS * rows * sum(piece.shape[2] for piece in far)
    in_vmem = pl.BlockSpec(memory_space=pltpu.VMEM)
    anywhere = pl.BlockSpec(memory_space=pl.ANY)
    if last:
        earlier = in_vmem
        out_shape = jax.ShapeDtypeStruct(queries.shape, jnp.bfloat16)
        out_specs = anywhere
        scratch = [
            pltpu.VMEM(queries.shape, jnp.bfloat16),
            pltpu.SemaphoreType.DMA((KEY_VALUE_HEADS,)),
        ]
    else:
        earlier = anywhere
        own = pltpu.with_memory_space_constraint(own, pltpu.HBM)
        level = pltpu.with_memory_space_constraint(level, pltpu.HBM)
        out_shape = [jax.ShapeDtypeStruct(queries.shape, jnp.float32)] * 2
        out_specs = [in_vmem] * 2
        scratch = [
            pltpu.VMEM(queries.shape, jnp.float32),
            pltpu.VMEM(level.shape, jnp.float32),
            pltpu.SemaphoreType.DMA((2, KEY_VALUE_HEADS)),
        ]
    return pl.pallas_call(
        functools.partial(far_kernel, last=last),
        out_shape=out_shape,
        in_specs=[
            pl.BlockSpec(memory_space=pltpu.SMEM),
            in_vmem,
            earlier,
            earlier,
            *[in_vmem] * len(far),
        ],
        out_specs=out_specs,
        scratch_shapes=scratch,
        compiler_params=pltpu.CompilerParams(vmem_limit_bytes=30 * MIB),
        cost_estimate=pl.CostEstimate(
            flops=4 * scores * HEAD_SIZE, bytes_accessed=10 * MIB, transcendentals=scores
        ),
        name="late_attention" if last else "early_attention",
    )(selected, queries, own, level, *far)


def local(queries, all_key_states, all_value_states, selected):
    devices = lax.axis_size("ctx")
    run = devices // 2
    rows = all_key_states.shape[0]
    piece_rows = rows // run
    upward = [(i, i + run) for i in range(run)]

    keys_over = lax.ppermute(all_key_states, "ctx", upward)
    values_next, keys_over = lax.optimization_barrier((all_value_states, keys_over))
    values_over = lax.ppermute(values_next, "ctx", upward)

    near = cut([all_key_states, all_value_states], run)
    queries, mine, near = lax.optimization_barrier((queries, selected, near))
    near = trade(near, devices)
    own, level = own_attention(queries, all_key_states, all_value_states)
    requests = jnp.clip(exchange_requests(mine, run, devices), 0, devices - 1)

    keys_over, own, level = lax.optimization_barrier((keys_over, own, level))
    keys_over = trade(cut([keys_over], run), devices)
    half = KEY_VALUE_HEADS * piece_rows
    far_keys = trade(pick_pieces(requests, near, keys_over, 0), devices)

    values_over = trade(cut([values_over], run), devices)
    far_values = trade(pick_pieces(requests, near, values_over, half), devices)

    shape = (2, KEY_VALUE_HEADS, piece_rows, HEAD_SIZE)
    order = [0, *delivery_order(run)]
    parts = []
    for steps in (order[: run // 2], order[run // 2 :]):
        both = []
        for pieces in (far_keys, far_values):
            pieces = [pieces[step].reshape(shape) for step in steps]
            both += [jnp.concatenate(pieces, axis=2)] if piece_rows % 16 != 0 else pieces
        parts.append(both)
    own, level = far_attention(selected, queries, own, level, parts[0], last=False)
    return far_attention(selected, queries, own, level, parts[1], last=True)


def solution(mesh):
    placed = P(("groups", "ctx"), None)
    return jax.shard_map(
        local, mesh=mesh, in_specs=(placed,) * 4, out_specs=placed, check_vma=False
    )
```

```python
import functools
import math

import jax
import jax.numpy as jnp
from jax import lax
from jax.experimental import pallas as pl
from jax.experimental.pallas import tpu as pltpu
from jax.sharding import PartitionSpec as P

QUERY_HEADS = 32
KEY_VALUE_HEADS = 4
HEAD_SIZE = 128
GROUP = QUERY_HEADS // KEY_VALUE_HEADS
SLOTS = 2 * KEY_VALUE_HEADS
COPIES = 2
MIB = 1024 * 1024


def pack_kernel(key_ref, value_ref, out_ref, staged, arrived, left):
    shares, piece_rows, _ = key_ref.shape
    half = KEY_VALUE_HEADS * piece_rows

    def take(slot):
        ref = key_ref if slot < KEY_VALUE_HEADS else value_ref
        head = slot % KEY_VALUE_HEADS
        lanes = pl.ds(head * HEAD_SIZE, HEAD_SIZE)
        rows = pl.ds(slot * piece_rows, piece_rows)
        return pltpu.make_async_copy(
            ref.at[:, :, lanes], staged.at[:, rows, :], arrived.at[slot]
        )

    def give(which, copy):
        rows = pl.ds(which * half, half)
        return pltpu.make_async_copy(
            staged.at[:, rows, :],
            out_ref.at[pl.ds(copy * shares, shares), rows, :],
            left.at[which, copy],
        )

    for slot in range(SLOTS):
        take(slot).start()
    for which in range(2):
        for head in range(KEY_VALUE_HEADS):
            take(which * KEY_VALUE_HEADS + head).wait()
        for copy in range(COPIES):
            give(which, copy).start()
    for which in range(2):
        for copy in range(COPIES):
            give(which, copy).wait()


def pack(keys, values, devices):
    shares = devices // COPIES
    piece_rows = keys.shape[0] // shares
    if piece_rows % 16 == 0:
        split = (shares, piece_rows, keys.shape[1])
        return pl.pallas_call(
            pack_kernel,
            out_shape=jax.ShapeDtypeStruct(
                (devices, SLOTS * piece_rows, HEAD_SIZE), jnp.bfloat16
            ),
            in_specs=[pl.BlockSpec(memory_space=pl.ANY)] * 2,
            out_specs=pl.BlockSpec(memory_space=pl.ANY),
            scratch_shapes=[
                pltpu.VMEM((shares, SLOTS * piece_rows, HEAD_SIZE), jnp.bfloat16),
                pltpu.SemaphoreType.DMA((SLOTS,)),
                pltpu.SemaphoreType.DMA((2, COPIES)),
            ],
            name="pack",
        )(keys.reshape(split), values.reshape(split))
    both = jnp.concatenate([keys, values], axis=1)
    both = both.reshape(shares, piece_rows, SLOTS, HEAD_SIZE).transpose(0, 2, 1, 3)
    both = both.reshape(shares, SLOTS * piece_rows, HEAD_SIZE)
    return jnp.concatenate([both] * COPIES, axis=0)


def partner(position, step):
    return position ^ step


def swap(array, step, devices):
    return lax.ppermute(array, "ctx", [(i, partner(i, step)) for i in range(devices)])


def exchange_requests(selected, shares, devices):
    requests = selected
    step = 1
    while step < shares:
        requests = jnp.concatenate([requests, swap(requests, step, devices)], axis=0)
        step *= 2
    return requests


def pick_kernel(requests_ref, held_ref, *out_refs, steps):
    for step, out_ref in zip(steps, out_refs):
        for pick in range(2):
            out_ref[pick] = held_ref[requests_ref[step, pick]]


def pick_pieces(requests, held, steps):
    rows = held.shape[1]
    return pl.pallas_call(
        functools.partial(pick_kernel, steps=steps),
        out_shape=[jax.ShapeDtypeStruct((2, rows, HEAD_SIZE), jnp.bfloat16)] * len(steps),
        in_specs=[
            pl.BlockSpec(memory_space=pltpu.SMEM),
            pl.BlockSpec(memory_space=pltpu.VMEM),
        ],
        out_specs=[pl.BlockSpec(memory_space=pltpu.VMEM)] * len(steps),
        compiler_params=pltpu.CompilerParams(vmem_limit_bytes=16 * MIB),
        name="pick_pieces",
    )(requests, held)


def delivery_order(shares):
    half, quarter = shares // 2, shares // 4
    return [
        *range(1, quarter),
        *range(half, half + quarter),
        *range(quarter, half),
        *range(half + quarter, shares),
    ]


def deliver(requests, held):
    devices = held.shape[0]
    order = delivery_order(devices // COPIES)
    early, late = order[: len(order) // 2], [*order[len(order) // 2 :], 0]
    moved = []
    for steps in (early, late):
        pieces = pick_pieces(requests, held, steps)
        moved += [p if s == 0 else swap(p, s, devices) for s, p in zip(steps, pieces)]
    return [moved[-1], *moved[:-1]]


FACTOR = math.log2(math.e) / math.sqrt(HEAD_SIZE)
PAIR = 2
SENT = 4
LARGE_SUM = 2.0**100


def head_lanes(head):
    return slice(head * HEAD_SIZE, (head + 1) * HEAD_SIZE)


def with_ones(value):
    return jnp.concatenate([value, jnp.ones_like(value)], axis=1)


def inverse_of(positive):
    return pl.reciprocal(positive, approx=True)


def dot(a, b):
    return jnp.dot(a, b, preferred_element_type=jnp.float32)


def stack_heads(wide):
    heads = wide.shape[1] // HEAD_SIZE
    return jnp.concatenate([wide[:, head_lanes(h)] for h in range(heads)], axis=0)


def own_kernel(query_ref, key_ref, value_ref, out_ref, level_ref):
    rows = query_ref.shape[0]
    row = lax.broadcasted_iota(jnp.int32, (rows, rows), 0)
    column = lax.broadcasted_iota(jnp.int32, (rows, rows), 1)
    causal = column <= row
    lane = lax.broadcasted_iota(jnp.int32, (rows, HEAD_SIZE), 1)
    keys_across = key_ref[...].T
    value = with_ones(value_ref[...])

    def score(first):
        lanes = slice(first * HEAD_SIZE, (first + PAIR) * HEAD_SIZE)
        return dot(stack_heads(query_ref[:, lanes]), keys_across)

    def finish(first, scores):
        weights, shifts = [], []
        for h in range(PAIR):
            part = jnp.where(causal, scores[h * rows : (h + 1) * rows], -1e30)
            shift = jnp.max(part, axis=1, keepdims=True) * FACTOR
            shifts.append(shift)
            weights.append(jnp.exp2(part * FACTOR - shift).astype(jnp.bfloat16))
        both = dot(jnp.concatenate(weights, axis=0), value)
        for h in range(PAIR):
            part = both[h * rows : (h + 1) * rows]
            row_sum = part[:, HEAD_SIZE:]
            out_ref[:, head_lanes(first + h)] = part[:, :HEAD_SIZE] / row_sum
            level = shifts[h] + jnp.log2(row_sum)
            level_ref[...] = jnp.where(lane == first + h, level, level_ref[...])

    level_ref[...] = jnp.zeros_like(level_ref)
    scores = score(0)
    for first in range(0, GROUP, PAIR):
        following = score(first + PAIR) if first + PAIR < GROUP else None
        finish(first, scores)
        scores = following


def own_attention(queries, keys, values):
    rows = queries.shape[0]
    width = GROUP * HEAD_SIZE
    scores = QUERY_HEADS * rows * rows
    return pl.pallas_call(
        own_kernel,
        out_shape=[
            pltpu.HBM(queries.shape, jnp.float32),
            pltpu.HBM((rows, KEY_VALUE_HEADS * HEAD_SIZE), jnp.float32),
        ],
        grid=(KEY_VALUE_HEADS,),
        in_specs=[
            pl.BlockSpec((rows, width), lambda g: (0, g)),
            pl.BlockSpec((rows, HEAD_SIZE), lambda g: (0, g)),
            pl.BlockSpec((rows, HEAD_SIZE), lambda g: (0, g)),
        ],
        out_specs=[
            pl.BlockSpec((rows, width), lambda g: (0, g)),
            pl.BlockSpec((rows, HEAD_SIZE), lambda g: (0, g)),
        ],
        compiler_params=pltpu.CompilerParams(vmem_limit_bytes=16 * MIB),
        cost_estimate=pl.CostEstimate(
            flops=4 * scores * HEAD_SIZE, bytes_accessed=7 * MIB, transcendentals=scores
        ),
        name="own_attention",
    )(queries, keys, values)


def far_kernel(selected_ref, query_ref, own_in, level_in, *refs, last):
    if last:
        *far_refs, out_ref, staged, sems = refs
        own_ref, level_ref = own_in, level_in
    else:
        *far_refs, out_ref, new_level_ref, own_ref, level_ref, sems = refs
    rows = query_ref.shape[0]
    width = GROUP * HEAD_SIZE

    def wide(group):
        start = group * width
        return pl.ds(start if isinstance(group, int) else pl.multiple_of(start, width), width)

    def narrow(group):
        start = group * HEAD_SIZE
        fixed = isinstance(group, int)
        return pl.ds(start if fixed else pl.multiple_of(start, HEAD_SIZE), HEAD_SIZE)

    def level_of(group, head):
        if last:
            return level_ref[:, head_of(group, head)]
        one = level_ref[:, narrow(group)][:, head : head + 1]
        return jnp.broadcast_to(one, (rows, HEAD_SIZE))

    def fetch(group, which):
        source, target = ((own_in, own_ref), (level_in, level_ref))[which]
        lanes = wide(group) if which == 0 else narrow(group)
        return pltpu.make_async_copy(
            source.at[:, lanes], target.at[:, lanes], sems.at[which, group]
        )

    def send(part):
        start = part * SENT * HEAD_SIZE
        fixed = isinstance(part, int)
        lanes = pl.ds(
            start if fixed else pl.multiple_of(start, SENT * HEAD_SIZE), SENT * HEAD_SIZE
        )
        return pltpu.make_async_copy(staged.at[:, lanes], out_ref.at[:, lanes], sems.at[part])

    if not last:
        for group in range(KEY_VALUE_HEADS):
            fetch(group, 1).start()
            fetch(group, 0).start()

    def head_of(group, head):
        start = (group * GROUP + head) * HEAD_SIZE
        fixed = isinstance(group, int)
        return pl.ds(start if fixed else pl.multiple_of(start, HEAD_SIZE), HEAD_SIZE)

    def store(lanes, mixture, row_sum, level):
        result = mixture * inverse_of(row_sum)
        if last:
            staged[:, lanes] = result.astype(staged.dtype)
        else:
            out_ref[:, lanes] = result
            new_level_ref[:, lanes] = level + jnp.log2(row_sum)

    def attend(picks):
        count = len(picks) * sum(ref.shape[2] for ref in far_refs)

        def block(slot):
            return jnp.concatenate([ref[p, slot] for p in picks for ref in far_refs], axis=0)

        def keys_and_values(group):
            return block(group).T, with_ones(block(group + KEY_VALUE_HEADS))

        def repeat(narrow):
            return jnp.concatenate([narrow] * (count // HEAD_SIZE), axis=1)

        def quick(group, head, scores, value, largest):
            lanes = head_of(group, head)
            level = level_of(group, head)
            weights = jnp.exp2(scores * FACTOR - repeat(level)).astype(jnp.bfloat16)
            both = dot(weights, value)
            row_sum = 1.0 + both[:, HEAD_SIZE:]
            store(lanes, own_ref[:, lanes] + both[:, :HEAD_SIZE], row_sum, level)
            return jnp.maximum(
                largest, jnp.max(row_sum.reshape(rows // 8, 8, HEAD_SIZE), axis=0)
            )

        def careful(group, head, scores, value):
            lanes = head_of(group, head)
            part = scores * FACTOR
            level = level_of(group, head)
            shift = jnp.maximum(jnp.max(part, axis=1, keepdims=True), level)
            weights = jnp.exp2(part - repeat(shift)).astype(jnp.bfloat16)
            both = dot(weights, value)
            share = jnp.exp2(level - shift)
            mixture = own_ref[:, lanes] * share + both[:, :HEAD_SIZE]
            store(lanes, mixture, share + both[:, HEAD_SIZE:], shift)

        def score(group, head, keys_across):
            return dot(query_ref[:, head_of(group, head)], keys_across)

        largest = jnp.zeros((8, HEAD_SIZE), jnp.float32)
        order = [(g, h) for g in range(KEY_VALUE_HEADS) for h in range(GROUP)]
        held = {0: keys_and_values(0)}
        scores = score(0, 0, held[0][0])
        for (group, head), later in zip(order, order[1:] + [None]):
            following = None
            if later is not None:
                if later[0] not in held:
                    held[later[0]] = keys_and_values(later[0])
                following = score(*later, held[later[0]][0])
            if head == 0 and not last:
                fetch(group, 1).wait()
                fetch(group, 0).wait()
            largest = quick(group, head, scores, held[group][1], largest)
            if (head + 1) % SENT == 0 and last:
                send((group * GROUP + head) // SENT).start()
            scores = following

        @pl.when(jnp.max(largest) > LARGE_SUM)
        def _():
            @pl.loop(0, KEY_VALUE_HEADS)
            def _(group):
                parts = [group * (GROUP // SENT) + part for part in range(GROUP // SENT)]
                if last:
                    for part in parts:
                        send(part).wait()
                keys_across, value = keys_and_values(group)
                for head in range(GROUP):
                    careful(group, head, score(group, head, keys_across), value)
                if last:
                    for part in parts:
                        send(part).start()

    my_block = lax.axis_index("ctx")
    chosen = selected_ref[0, 0], selected_ref[0, 1]
    first = chosen[0] < my_block
    second = jnp.logical_and(chosen[1] < my_block, chosen[1] != chosen[0])
    valid = first.astype(jnp.int32) + second.astype(jnp.int32)

    @pl.when(valid == 2)
    def _():
        attend((0, 1))

    @pl.when(valid == 1)
    def _():
        attend((second.astype(jnp.int32),))

    @pl.when(valid == 0)
    def _():
        @pl.loop(0, KEY_VALUE_HEADS)
        def _(group):
            lanes = wide(group)
            if last:
                staged[:, lanes] = own_ref[:, lanes].astype(staged.dtype)
                for part in range(GROUP // SENT):
                    send(group * (GROUP // SENT) + part).start()
            else:
                fetch(group, 1).wait()
                fetch(group, 0).wait()
                out_ref[:, lanes] = own_ref[:, lanes]
                for head in range(GROUP):
                    new_level_ref[:, head_of(group, head)] = level_of(group, head)

    if last:

        @pl.loop(0, QUERY_HEADS // SENT)
        def _(part):
            send(part).wait()


def far_attention(selected, queries, own, level, far, last):
    rows = queries.shape[0]
    scores = QUERY_HEADS * rows * 2 * sum(piece.shape[2] for piece in far)
    in_vmem = pl.BlockSpec(memory_space=pltpu.VMEM)
    anywhere = pl.BlockSpec(memory_space=pl.ANY)
    if last:
        earlier = in_vmem
        out_shape = jax.ShapeDtypeStruct(queries.shape, jnp.bfloat16)
        out_specs = anywhere
        scratch = [
            pltpu.VMEM(queries.shape, jnp.bfloat16),
            pltpu.SemaphoreType.DMA((QUERY_HEADS // SENT,)),
        ]
    else:
        earlier = anywhere
        own = pltpu.with_memory_space_constraint(own, pltpu.HBM)
        level = pltpu.with_memory_space_constraint(level, pltpu.HBM)
        out_shape = [jax.ShapeDtypeStruct(queries.shape, jnp.float32)] * 2
        out_specs = [in_vmem] * 2
        scratch = [
            pltpu.VMEM(queries.shape, jnp.float32),
            pltpu.VMEM(level.shape, jnp.float32),
            pltpu.SemaphoreType.DMA((2, KEY_VALUE_HEADS)),
        ]
    return pl.pallas_call(
        functools.partial(far_kernel, last=last),
        out_shape=out_shape,
        in_specs=[
            pl.BlockSpec(memory_space=pltpu.SMEM),
            in_vmem,
            earlier,
            earlier,
            *[in_vmem] * len(far),
        ],
        out_specs=out_specs,
        scratch_shapes=scratch,
        compiler_params=pltpu.CompilerParams(vmem_limit_bytes=30 * MIB),
        cost_estimate=pl.CostEstimate(
            flops=4 * scores * HEAD_SIZE, bytes_accessed=10 * MIB, transcendentals=scores
        ),
        name="late_attention" if last else "early_attention",
    )(selected, queries, own, level, *far)


def local(queries, all_key_states, all_value_states, selected):
    devices = lax.axis_size("ctx")
    rows = all_key_states.shape[0]
    piece_rows = rows * COPIES // devices
    packed = pack(all_key_states, all_value_states, devices)
    packed, queries = lax.optimization_barrier((packed, queries))
    held = lax.all_to_all(packed, "ctx", split_axis=0, concat_axis=0, tiled=True)
    own, level = own_attention(queries, all_key_states, all_value_states)
    mine, own, level = lax.optimization_barrier((selected, own, level))
    requests = exchange_requests(mine, devices // COPIES, devices)
    requests = jnp.clip(requests, 0, devices - 1)
    moved = deliver(requests, held)
    far = [m.reshape(2, SLOTS, piece_rows, HEAD_SIZE) for m in moved]
    early, late = far[: len(far) // 2], far[len(far) // 2 :]
    if piece_rows % 16 != 0:
        early, late = [jnp.concatenate(early, axis=2)], [jnp.concatenate(late, axis=2)]
    own, level = far_attention(selected, queries, own, level, early, last=False)
    return far_attention(selected, queries, own, level, late, last=True)


def solution(mesh):
    placed = P(("groups", "ctx"), None)
    return jax.shard_map(
        local, mesh=mesh, in_specs=(placed,) * 4, out_specs=placed, check_vma=False
    )
```

```python
import functools
import math

import jax
import jax.numpy as jnp
from jax import lax
from jax.experimental import pallas as pl
from jax.experimental.pallas import tpu as pltpu
from jax.sharding import PartitionSpec as P

QUERY_HEADS = 32
KEY_VALUE_HEADS = 4
HEAD_SIZE = 128
GROUP = QUERY_HEADS // KEY_VALUE_HEADS
SLOTS = 2 * KEY_VALUE_HEADS
COPIES = 2
MIB = 1024 * 1024


def pack(keys, values, devices):
    shares = devices // COPIES
    piece_rows = keys.shape[0] // shares
    both = jnp.concatenate([keys, values], axis=1)
    if piece_rows % 16 != 0:
        both = both.reshape(shares, piece_rows, SLOTS, HEAD_SIZE).transpose(0, 2, 1, 3)
        both = both.reshape(shares, SLOTS * piece_rows, HEAD_SIZE)
    else:
        both = both.reshape(shares, piece_rows, SLOTS * HEAD_SIZE)
    return jnp.broadcast_to(both[None], (COPIES, *both.shape)).reshape(devices, *both.shape[1:])


def partner(position, step):
    return position ^ step


def swap(array, step, devices):
    return lax.ppermute(array, "ctx", [(i, partner(i, step)) for i in range(devices)])


def exchange_requests(selected, shares, devices):
    requests = selected
    step = 1
    while step < shares:
        requests = jnp.concatenate([requests, swap(requests, step, devices)], axis=0)
        step *= 2
    return requests


def pick_kernel(requests_ref, held_ref, *out_refs):
    for step, out_ref in enumerate(out_refs):
        for pick in range(2):
            out_ref[pick] = held_ref[requests_ref[step, pick]]


def pick_pieces(requests, held):
    devices, rows, width = held.shape
    shares = devices // COPIES
    return pl.pallas_call(
        pick_kernel,
        out_shape=[jax.ShapeDtypeStruct((2, rows, width), jnp.bfloat16)] * shares,
        in_specs=[
            pl.BlockSpec(memory_space=pltpu.SMEM),
            pl.BlockSpec(memory_space=pltpu.VMEM),
        ],
        out_specs=[pl.BlockSpec(memory_space=pltpu.VMEM)] * shares,
        compiler_params=pltpu.CompilerParams(vmem_limit_bytes=16 * MIB),
        name="pick_pieces",
    )(requests, held)


def delivery_order(shares):
    half, quarter = shares // 2, shares // 4
    apart = zip(range(half, half + quarter), range(quarter, half))
    return [*range(1, quarter), *range(half + quarter, shares), *[s for pair in apart for s in pair]]


def deliver(pieces, devices):
    order = delivery_order(len(pieces))
    return [pieces[0]] + [swap(pieces[step], step, devices) for step in order]


FACTOR = math.log2(math.e) / math.sqrt(HEAD_SIZE)
PAIR = 2
SENT = 4
LARGE_SUM = 2.0**100


def head_lanes(head):
    return slice(head * HEAD_SIZE, (head + 1) * HEAD_SIZE)


def with_ones(value):
    return jnp.concatenate([value, jnp.ones_like(value)], axis=1)


def inverse_of(positive):
    return pl.reciprocal(positive, approx=True)


def dot(a, b):
    return jnp.dot(a, b, preferred_element_type=jnp.float32)


def stack_heads(wide):
    heads = wide.shape[1] // HEAD_SIZE
    return jnp.concatenate([wide[:, head_lanes(h)] for h in range(heads)], axis=0)


def own_kernel(query_ref, key_ref, value_ref, out_ref, level_ref):
    rows = query_ref.shape[0]
    row = lax.broadcasted_iota(jnp.int32, (rows, rows), 0)
    column = lax.broadcasted_iota(jnp.int32, (rows, rows), 1)
    causal = column <= row
    lane = lax.broadcasted_iota(jnp.int32, (rows, HEAD_SIZE), 1)
    keys_across = key_ref[...].T
    value = with_ones(value_ref[...])

    def score(first):
        lanes = slice(first * HEAD_SIZE, (first + PAIR) * HEAD_SIZE)
        return dot(stack_heads(query_ref[:, lanes]), keys_across)

    def finish(first, scores):
        weights, shifts = [], []
        for h in range(PAIR):
            part = jnp.where(causal, scores[h * rows : (h + 1) * rows], -1e30)
            shift = jnp.max(part, axis=1, keepdims=True) * FACTOR
            shifts.append(shift)
            weights.append(jnp.exp2(part * FACTOR - shift).astype(jnp.bfloat16))
        both = dot(jnp.concatenate(weights, axis=0), value)
        for h in range(PAIR):
            part = both[h * rows : (h + 1) * rows]
            row_sum = part[:, HEAD_SIZE:]
            out_ref[:, head_lanes(first + h)] = part[:, :HEAD_SIZE] / row_sum
            level = shifts[h] + jnp.log2(row_sum)
            level_ref[...] = jnp.where(lane == first + h, level, level_ref[...])

    level_ref[...] = jnp.zeros_like(level_ref)
    scores = score(0)
    for first in range(0, GROUP, PAIR):
        following = score(first + PAIR) if first + PAIR < GROUP else None
        finish(first, scores)
        scores = following


def own_attention(queries, keys, values):
    rows = queries.shape[0]
    width = GROUP * HEAD_SIZE
    scores = QUERY_HEADS * rows * rows
    return pl.pallas_call(
        own_kernel,
        out_shape=[
            pltpu.HBM(queries.shape, jnp.float32),
            pltpu.HBM((rows, KEY_VALUE_HEADS * HEAD_SIZE), jnp.float32),
        ],
        grid=(KEY_VALUE_HEADS,),
        in_specs=[
            pl.BlockSpec((rows, width), lambda g: (0, g)),
            pl.BlockSpec((rows, HEAD_SIZE), lambda g: (0, g)),
            pl.BlockSpec((rows, HEAD_SIZE), lambda g: (0, g)),
        ],
        out_specs=[
            pl.BlockSpec((rows, width), lambda g: (0, g)),
            pl.BlockSpec((rows, HEAD_SIZE), lambda g: (0, g)),
        ],
        compiler_params=pltpu.CompilerParams(vmem_limit_bytes=16 * MIB),
        cost_estimate=pl.CostEstimate(
            flops=4 * scores * HEAD_SIZE, bytes_accessed=7 * MIB, transcendentals=scores
        ),
        name="own_attention",
    )(queries, keys, values)


def far_kernel(selected_ref, query_ref, own_in, level_in, *refs, last):
    if last:
        *far_refs, out_ref, staged, sems = refs
        own_ref, level_ref = own_in, level_in
    else:
        *far_refs, out_ref, new_level_ref, own_ref, level_ref, sems = refs
    rows = query_ref.shape[0]
    width = GROUP * HEAD_SIZE

    def wide(group):
        start = group * width
        return pl.ds(start if isinstance(group, int) else pl.multiple_of(start, width), width)

    def narrow(group):
        start = group * HEAD_SIZE
        fixed = isinstance(group, int)
        return pl.ds(start if fixed else pl.multiple_of(start, HEAD_SIZE), HEAD_SIZE)

    def level_of(group, head):
        if last:
            return level_ref[:, head_of(group, head)]
        one = level_ref[:, narrow(group)][:, head : head + 1]
        return jnp.broadcast_to(one, (rows, HEAD_SIZE))

    def fetch(group, which):
        source, target = ((own_in, own_ref), (level_in, level_ref))[which]
        lanes = wide(group) if which == 0 else narrow(group)
        return pltpu.make_async_copy(
            source.at[:, lanes], target.at[:, lanes], sems.at[which, group]
        )

    def send(part):
        start = part * SENT * HEAD_SIZE
        fixed = isinstance(part, int)
        lanes = pl.ds(
            start if fixed else pl.multiple_of(start, SENT * HEAD_SIZE), SENT * HEAD_SIZE
        )
        return pltpu.make_async_copy(staged.at[:, lanes], out_ref.at[:, lanes], sems.at[part])

    if not last:
        for group in range(KEY_VALUE_HEADS):
            fetch(group, 1).start()
            fetch(group, 0).start()

    def head_of(group, head):
        start = (group * GROUP + head) * HEAD_SIZE
        fixed = isinstance(group, int)
        return pl.ds(start if fixed else pl.multiple_of(start, HEAD_SIZE), HEAD_SIZE)

    def store(lanes, mixture, row_sum, level):
        result = mixture * inverse_of(row_sum)
        if last:
            staged[:, lanes] = result.astype(staged.dtype)
        else:
            out_ref[:, lanes] = result
            new_level_ref[:, lanes] = level + jnp.log2(row_sum)

    def attend(picks):
        count = len(picks) * sum(ref.shape[1] for ref in far_refs)

        def block(slot):
            lanes = narrow(slot)
            return jnp.concatenate([ref[p, :, lanes] for p in picks for ref in far_refs], axis=0)

        def keys_and_values(group):
            return block(group).T, with_ones(block(group + KEY_VALUE_HEADS))

        def repeat(narrow):
            return jnp.concatenate([narrow] * (count // HEAD_SIZE), axis=1)

        def quick(group, head, scores, value, largest):
            lanes = head_of(group, head)
            level = level_of(group, head)
            weights = jnp.exp2(scores * FACTOR - repeat(level)).astype(jnp.bfloat16)
            both = dot(weights, value)
            row_sum = 1.0 + both[:, HEAD_SIZE:]
            store(lanes, own_ref[:, lanes] + both[:, :HEAD_SIZE], row_sum, level)
            return jnp.maximum(
                largest, jnp.max(row_sum.reshape(rows // 8, 8, HEAD_SIZE), axis=0)
            )

        def careful(group, head, scores, value):
            lanes = head_of(group, head)
            part = scores * FACTOR
            level = level_of(group, head)
            shift = jnp.maximum(jnp.max(part, axis=1, keepdims=True), level)
            weights = jnp.exp2(part - repeat(shift)).astype(jnp.bfloat16)
            both = dot(weights, value)
            share = jnp.exp2(level - shift)
            mixture = own_ref[:, lanes] * share + both[:, :HEAD_SIZE]
            store(lanes, mixture, share + both[:, HEAD_SIZE:], shift)

        def score(group, head, keys_across):
            return dot(query_ref[:, head_of(group, head)], keys_across)

        largest = jnp.zeros((8, HEAD_SIZE), jnp.float32)
        order = [(g, h) for g in range(KEY_VALUE_HEADS) for h in range(GROUP)]
        held = {0: keys_and_values(0)}
        scores = score(0, 0, held[0][0])
        for (group, head), later in zip(order, order[1:] + [None]):
            following = None
            if later is not None:
                if later[0] not in held:
                    held[later[0]] = keys_and_values(later[0])
                following = score(*later, held[later[0]][0])
            if head == 0 and not last:
                fetch(group, 1).wait()
                fetch(group, 0).wait()
            largest = quick(group, head, scores, held[group][1], largest)
            if (head + 1) % SENT == 0 and last:
                send((group * GROUP + head) // SENT).start()
            scores = following

        @pl.when(jnp.max(largest) > LARGE_SUM)
        def _():
            @pl.loop(0, KEY_VALUE_HEADS)
            def _(group):
                parts = [group * (GROUP // SENT) + part for part in range(GROUP // SENT)]
                if last:
                    for part in parts:
                        send(part).wait()
                keys_across, value = keys_and_values(group)
                for head in range(GROUP):
                    careful(group, head, score(group, head, keys_across), value)
                if last:
                    for part in parts:
                        send(part).start()

    my_block = lax.axis_index("ctx")
    chosen = selected_ref[0, 0], selected_ref[0, 1]
    first = chosen[0] < my_block
    second = jnp.logical_and(chosen[1] < my_block, chosen[1] != chosen[0])
    valid = first.astype(jnp.int32) + second.astype(jnp.int32)

    @pl.when(valid == 2)
    def _():
        attend((0, 1))

    @pl.when(valid == 1)
    def _():
        attend((second.astype(jnp.int32),))

    @pl.when(valid == 0)
    def _():
        @pl.loop(0, KEY_VALUE_HEADS)
        def _(group):
            lanes = wide(group)
            if last:
                staged[:, lanes] = own_ref[:, lanes].astype(staged.dtype)
                for part in range(GROUP // SENT):
                    send(group * (GROUP // SENT) + part).start()
            else:
                fetch(group, 1).wait()
                fetch(group, 0).wait()
                out_ref[:, lanes] = own_ref[:, lanes]
                for head in range(GROUP):
                    new_level_ref[:, head_of(group, head)] = level_of(group, head)

    if last:

        @pl.loop(0, QUERY_HEADS // SENT)
        def _(part):
            send(part).wait()


def far_attention(selected, queries, own, level, far, last):
    rows = queries.shape[0]
    scores = QUERY_HEADS * rows * 2 * sum(piece.shape[1] for piece in far)
    in_vmem = pl.BlockSpec(memory_space=pltpu.VMEM)
    anywhere = pl.BlockSpec(memory_space=pl.ANY)
    if last:
        earlier = in_vmem
        out_shape = jax.ShapeDtypeStruct(queries.shape, jnp.bfloat16)
        out_specs = anywhere
        scratch = [
            pltpu.VMEM(queries.shape, jnp.bfloat16),
            pltpu.SemaphoreType.DMA((QUERY_HEADS // SENT,)),
        ]
    else:
        earlier = anywhere
        own = pltpu.with_memory_space_constraint(own, pltpu.HBM)
        level = pltpu.with_memory_space_constraint(level, pltpu.HBM)
        out_shape = [jax.ShapeDtypeStruct(queries.shape, jnp.float32)] * 2
        out_specs = [in_vmem] * 2
        scratch = [
            pltpu.VMEM(queries.shape, jnp.float32),
            pltpu.VMEM(level.shape, jnp.float32),
            pltpu.SemaphoreType.DMA((2, KEY_VALUE_HEADS)),
        ]
    return pl.pallas_call(
        functools.partial(far_kernel, last=last),
        out_shape=out_shape,
        in_specs=[
            pl.BlockSpec(memory_space=pltpu.SMEM),
            in_vmem,
            earlier,
            earlier,
            *[in_vmem] * len(far),
        ],
        out_specs=out_specs,
        scratch_shapes=scratch,
        compiler_params=pltpu.CompilerParams(vmem_limit_bytes=30 * MIB),
        cost_estimate=pl.CostEstimate(
            flops=4 * scores * HEAD_SIZE, bytes_accessed=10 * MIB, transcendentals=scores
        ),
        name="late_attention" if last else "early_attention",
    )(selected, queries, own, level, *far)


def join(pieces, piece_rows):
    pieces = [p.reshape(2, SLOTS, piece_rows, HEAD_SIZE).transpose(0, 2, 1, 3) for p in pieces]
    return jnp.concatenate(pieces, axis=1).reshape(2, -1, SLOTS * HEAD_SIZE)


def local(queries, all_key_states, all_value_states, selected):
    devices = lax.axis_size("ctx")
    rows = all_key_states.shape[0]
    piece_rows = rows * COPIES // devices
    packed = pack(all_key_states, all_value_states, devices)
    packed, queries = lax.optimization_barrier((packed, queries))
    held = lax.all_to_all(packed, "ctx", split_axis=0, concat_axis=0, tiled=True)
    own, level = own_attention(queries, all_key_states, all_value_states)
    mine, own, level = lax.optimization_barrier((selected, own, level))
    requests = exchange_requests(mine, devices // COPIES, devices)
    requests = jnp.clip(requests, 0, devices - 1)
    moved = deliver(pick_pieces(requests, held), devices)
    early, late = moved[: len(moved) // 2], moved[len(moved) // 2 :]
    if piece_rows % 16 != 0:
        early, late = [join(early, piece_rows)], [join(late, piece_rows)]
    own, level = far_attention(selected, queries, own, level, early, last=False)
    return far_attention(selected, queries, own, level, late, last=True)


def solution(mesh):
    placed = P(("groups", "ctx"), None)
    return jax.shard_map(
        local, mesh=mesh, in_specs=(placed,) * 4, out_specs=placed, check_vma=False
    )
```

```python
import functools
import math

import jax
import jax.numpy as jnp
from jax import lax
from jax.experimental import pallas as pl
from jax.experimental.pallas import tpu as pltpu
from jax.sharding import PartitionSpec as P

QUERY_HEADS = 32
KEY_VALUE_HEADS = 4
HEAD_SIZE = 128
GROUP = QUERY_HEADS // KEY_VALUE_HEADS
SLOTS = 2 * KEY_VALUE_HEADS
COPIES = 2
MIB = 1024 * 1024


def pack_kernel(key_ref, value_ref, out_ref, staged, arrived, left):
    shares, piece_rows, _ = key_ref.shape
    half = KEY_VALUE_HEADS * piece_rows

    def take(slot):
        ref = key_ref if slot < KEY_VALUE_HEADS else value_ref
        head = slot % KEY_VALUE_HEADS
        lanes = pl.ds(head * HEAD_SIZE, HEAD_SIZE)
        rows = pl.ds(slot * piece_rows, piece_rows)
        return pltpu.make_async_copy(
            ref.at[:, :, lanes], staged.at[:, rows, :], arrived.at[slot]
        )

    def give(which, copy):
        rows = pl.ds(which * half, half)
        return pltpu.make_async_copy(
            staged.at[:, rows, :],
            out_ref.at[pl.ds(copy * shares, shares), rows, :],
            left.at[which, copy],
        )

    for slot in range(SLOTS):
        take(slot).start()
    for which in range(2):
        for head in range(KEY_VALUE_HEADS):
            take(which * KEY_VALUE_HEADS + head).wait()
        for copy in range(COPIES):
            give(which, copy).start()
    for which in range(2):
        for copy in range(COPIES):
            give(which, copy).wait()


def pack(keys, values, devices):
    shares = devices // COPIES
    piece_rows = keys.shape[0] // shares
    if piece_rows % 16 == 0:
        split = (shares, piece_rows, keys.shape[1])
        return pl.pallas_call(
            pack_kernel,
            out_shape=jax.ShapeDtypeStruct(
                (devices, SLOTS * piece_rows, HEAD_SIZE), jnp.bfloat16
            ),
            in_specs=[pl.BlockSpec(memory_space=pl.ANY)] * 2,
            out_specs=pl.BlockSpec(memory_space=pl.ANY),
            scratch_shapes=[
                pltpu.VMEM((shares, SLOTS * piece_rows, HEAD_SIZE), jnp.bfloat16),
                pltpu.SemaphoreType.DMA((SLOTS,)),
                pltpu.SemaphoreType.DMA((2, COPIES)),
            ],
            name="pack",
        )(keys.reshape(split), values.reshape(split))
    both = jnp.concatenate([keys, values], axis=1)
    both = both.reshape(shares, piece_rows, SLOTS, HEAD_SIZE).transpose(0, 2, 1, 3)
    both = both.reshape(shares, SLOTS * piece_rows, HEAD_SIZE)
    return jnp.concatenate([both] * COPIES, axis=0)


def partner(position, step):
    return position ^ step


def swap(array, step, devices):
    return lax.ppermute(array, "ctx", [(i, partner(i, step)) for i in range(devices)])


def exchange_requests(selected, shares, devices):
    requests = selected
    step = 1
    while step < shares:
        requests = jnp.concatenate([requests, swap(requests, step, devices)], axis=0)
        step *= 2
    return requests


def scalar_of(values, row, column):
    rows = lax.broadcasted_iota(jnp.int32, values.shape, 0)
    columns = lax.broadcasted_iota(jnp.int32, values.shape, 1)
    here = jnp.logical_and(rows == row, columns == column)
    return jnp.max(jnp.where(here, values.astype(jnp.float32), 0.0)).astype(jnp.int32)


def pick_kernel(requests_ref, held_ref, *out_refs):
    requests = requests_ref[...]
    for step, out_ref in enumerate(out_refs):
        for pick in range(2):
            out_ref[pick] = held_ref[scalar_of(requests, step, pick)]


def pick_pieces(requests, held):
    devices, rows, _ = held.shape
    shares = devices // COPIES
    return pl.pallas_call(
        pick_kernel,
        out_shape=[jax.ShapeDtypeStruct((2, rows, HEAD_SIZE), jnp.bfloat16)] * shares,
        in_specs=[pl.BlockSpec(memory_space=pltpu.VMEM)] * 2,
        out_specs=[pl.BlockSpec(memory_space=pltpu.VMEM)] * shares,
        compiler_params=pltpu.CompilerParams(vmem_limit_bytes=16 * MIB),
        name="pick_pieces",
    )(requests, held)


def delivery_order(shares):
    half, quarter = shares // 2, shares // 4
    apart = zip(range(half, half + quarter), range(quarter, half))
    return [*range(1, quarter), *[s for pair in apart for s in pair], *range(half + quarter, shares)]


def deliver(pieces, devices):
    order = delivery_order(len(pieces))
    return [pieces[0]] + [swap(pieces[step], step, devices) for step in order]


FACTOR = math.log2(math.e) / math.sqrt(HEAD_SIZE)
PAIR = 2
SENT = 4
LARGE_SUM = 2.0**100


def head_lanes(head):
    return slice(head * HEAD_SIZE, (head + 1) * HEAD_SIZE)


def with_ones(value):
    return jnp.concatenate([value, jnp.ones_like(value)], axis=1)


def inverse_of(positive):
    return pl.reciprocal(positive, approx=True)


def dot(a, b):
    return jnp.dot(a, b, preferred_element_type=jnp.float32)


def stack_heads(wide):
    heads = wide.shape[1] // HEAD_SIZE
    return jnp.concatenate([wide[:, head_lanes(h)] for h in range(heads)], axis=0)


def own_kernel(query_ref, key_ref, value_ref, out_ref, level_ref):
    rows = query_ref.shape[0]
    row = lax.broadcasted_iota(jnp.int32, (rows, rows), 0)
    column = lax.broadcasted_iota(jnp.int32, (rows, rows), 1)
    causal = column <= row
    lane = lax.broadcasted_iota(jnp.int32, (rows, HEAD_SIZE), 1)
    keys_across = key_ref[...].T
    value = with_ones(value_ref[...])

    def score(first):
        lanes = slice(first * HEAD_SIZE, (first + PAIR) * HEAD_SIZE)
        return dot(stack_heads(query_ref[:, lanes]), keys_across)

    def finish(first, scores):
        weights, shifts = [], []
        for h in range(PAIR):
            part = jnp.where(causal, scores[h * rows : (h + 1) * rows], -1e30)
            shift = jnp.max(part, axis=1, keepdims=True) * FACTOR
            shifts.append(shift)
            weights.append(jnp.exp2(part * FACTOR - shift).astype(jnp.bfloat16))
        both = dot(jnp.concatenate(weights, axis=0), value)
        for h in range(PAIR):
            part = both[h * rows : (h + 1) * rows]
            row_sum = part[:, HEAD_SIZE:]
            out_ref[:, head_lanes(first + h)] = part[:, :HEAD_SIZE] / row_sum
            level = shifts[h] + jnp.log2(row_sum)
            level_ref[...] = jnp.where(lane == first + h, level, level_ref[...])

    level_ref[...] = jnp.zeros_like(level_ref)
    scores = score(0)
    for first in range(0, GROUP, PAIR):
        following = score(first + PAIR) if first + PAIR < GROUP else None
        finish(first, scores)
        scores = following


def own_attention(queries, keys, values):
    rows = queries.shape[0]
    width = GROUP * HEAD_SIZE
    scores = QUERY_HEADS * rows * rows
    return pl.pallas_call(
        own_kernel,
        out_shape=[
            pltpu.HBM(queries.shape, jnp.float32),
            pltpu.HBM((rows, KEY_VALUE_HEADS * HEAD_SIZE), jnp.float32),
        ],
        grid=(KEY_VALUE_HEADS,),
        in_specs=[
            pl.BlockSpec((rows, width), lambda g: (0, g)),
            pl.BlockSpec((rows, HEAD_SIZE), lambda g: (0, g)),
            pl.BlockSpec((rows, HEAD_SIZE), lambda g: (0, g)),
        ],
        out_specs=[
            pl.BlockSpec((rows, width), lambda g: (0, g)),
            pl.BlockSpec((rows, HEAD_SIZE), lambda g: (0, g)),
        ],
        compiler_params=pltpu.CompilerParams(vmem_limit_bytes=16 * MIB),
        cost_estimate=pl.CostEstimate(
            flops=4 * scores * HEAD_SIZE, bytes_accessed=7 * MIB, transcendentals=scores
        ),
        name="own_attention",
    )(queries, keys, values)


def far_kernel(selected_ref, query_ref, own_in, level_in, *refs, last):
    if last:
        *far_refs, out_ref, staged, sems = refs
        own_ref, level_ref = own_in, level_in
    else:
        *far_refs, out_ref, new_level_ref, own_ref, level_ref, sems = refs
    rows = query_ref.shape[0]
    width = GROUP * HEAD_SIZE

    def wide(group):
        start = group * width
        return pl.ds(start if isinstance(group, int) else pl.multiple_of(start, width), width)

    def narrow(group):
        start = group * HEAD_SIZE
        fixed = isinstance(group, int)
        return pl.ds(start if fixed else pl.multiple_of(start, HEAD_SIZE), HEAD_SIZE)

    def level_of(group, head):
        if last:
            return level_ref[:, head_of(group, head)]
        one = level_ref[:, narrow(group)][:, head : head + 1]
        return jnp.broadcast_to(one, (rows, HEAD_SIZE))

    def fetch(group, which):
        source, target = ((own_in, own_ref), (level_in, level_ref))[which]
        lanes = wide(group) if which == 0 else narrow(group)
        return pltpu.make_async_copy(
            source.at[:, lanes], target.at[:, lanes], sems.at[which, group]
        )

    def send(part):
        start = part * SENT * HEAD_SIZE
        fixed = isinstance(part, int)
        lanes = pl.ds(
            start if fixed else pl.multiple_of(start, SENT * HEAD_SIZE), SENT * HEAD_SIZE
        )
        return pltpu.make_async_copy(staged.at[:, lanes], out_ref.at[:, lanes], sems.at[part])

    if not last:
        for group in range(KEY_VALUE_HEADS):
            fetch(group, 1).start()
            fetch(group, 0).start()

    def head_of(group, head):
        start = (group * GROUP + head) * HEAD_SIZE
        fixed = isinstance(group, int)
        return pl.ds(start if fixed else pl.multiple_of(start, HEAD_SIZE), HEAD_SIZE)

    def store(lanes, mixture, row_sum, level):
        result = mixture * inverse_of(row_sum)
        if last:
            staged[:, lanes] = result.astype(staged.dtype)
        else:
            out_ref[:, lanes] = result
            new_level_ref[:, lanes] = level + jnp.log2(row_sum)

    def attend(picks):
        count = len(picks) * sum(ref.shape[2] for ref in far_refs)

        def block(slot):
            return jnp.concatenate([ref[p, slot] for p in picks for ref in far_refs], axis=0)

        def keys_and_values(group):
            return block(group).T, with_ones(block(group + KEY_VALUE_HEADS))

        def repeat(narrow):
            return jnp.concatenate([narrow] * (count // HEAD_SIZE), axis=1)

        def quick(group, head, scores, value, largest):
            lanes = head_of(group, head)
            level = level_of(group, head)
            weights = jnp.exp2(scores * FACTOR - repeat(level)).astype(jnp.bfloat16)
            both = dot(weights, value)
            row_sum = 1.0 + both[:, HEAD_SIZE:]
            store(lanes, own_ref[:, lanes] + both[:, :HEAD_SIZE], row_sum, level)
            return jnp.maximum(
                largest, jnp.max(row_sum.reshape(rows // 8, 8, HEAD_SIZE), axis=0)
            )

        def careful(group, head, scores, value):
            lanes = head_of(group, head)
            part = scores * FACTOR
            level = level_of(group, head)
            shift = jnp.maximum(jnp.max(part, axis=1, keepdims=True), level)
            weights = jnp.exp2(part - repeat(shift)).astype(jnp.bfloat16)
            both = dot(weights, value)
            share = jnp.exp2(level - shift)
            mixture = own_ref[:, lanes] * share + both[:, :HEAD_SIZE]
            store(lanes, mixture, share + both[:, HEAD_SIZE:], shift)

        def score(group, head, keys_across):
            return dot(query_ref[:, head_of(group, head)], keys_across)

        largest = jnp.zeros((8, HEAD_SIZE), jnp.float32)
        order = [(g, h) for g in range(KEY_VALUE_HEADS) for h in range(GROUP)]
        held = {0: keys_and_values(0)}
        scores = score(0, 0, held[0][0])
        for (group, head), later in zip(order, order[1:] + [None]):
            following = None
            if later is not None:
                if later[0] not in held:
                    held[later[0]] = keys_and_values(later[0])
                following = score(*later, held[later[0]][0])
            if head == 0 and not last:
                fetch(group, 1).wait()
                fetch(group, 0).wait()
            largest = quick(group, head, scores, held[group][1], largest)
            if (head + 1) % SENT == 0 and last:
                send((group * GROUP + head) // SENT).start()
            scores = following

        @pl.when(jnp.max(largest) > LARGE_SUM)
        def _():
            @pl.loop(0, KEY_VALUE_HEADS)
            def _(group):
                parts = [group * (GROUP // SENT) + part for part in range(GROUP // SENT)]
                if last:
                    for part in parts:
                        send(part).wait()
                keys_across, value = keys_and_values(group)
                for head in range(GROUP):
                    careful(group, head, score(group, head, keys_across), value)
                if last:
                    for part in parts:
                        send(part).start()

    my_block = lax.axis_index("ctx")
    selected = selected_ref[...]
    chosen = scalar_of(selected, 0, 0), scalar_of(selected, 0, 1)
    first = chosen[0] < my_block
    second = jnp.logical_and(chosen[1] < my_block, chosen[1] != chosen[0])
    valid = first.astype(jnp.int32) + second.astype(jnp.int32)

    @pl.when(valid == 2)
    def _():
        attend((0, 1))

    @pl.when(valid == 1)
    def _():
        attend((second.astype(jnp.int32),))

    @pl.when(valid == 0)
    def _():
        @pl.loop(0, KEY_VALUE_HEADS)
        def _(group):
            lanes = wide(group)
            if last:
                staged[:, lanes] = own_ref[:, lanes].astype(staged.dtype)
                for part in range(GROUP // SENT):
                    send(group * (GROUP // SENT) + part).start()
            else:
                fetch(group, 1).wait()
                fetch(group, 0).wait()
                out_ref[:, lanes] = own_ref[:, lanes]
                for head in range(GROUP):
                    new_level_ref[:, head_of(group, head)] = level_of(group, head)

    if last:

        @pl.loop(0, QUERY_HEADS // SENT)
        def _(part):
            send(part).wait()


def far_attention(selected, queries, own, level, far, last):
    rows = queries.shape[0]
    scores = QUERY_HEADS * rows * 2 * sum(piece.shape[2] for piece in far)
    in_vmem = pl.BlockSpec(memory_space=pltpu.VMEM)
    anywhere = pl.BlockSpec(memory_space=pl.ANY)
    if last:
        earlier = in_vmem
        out_shape = jax.ShapeDtypeStruct(queries.shape, jnp.bfloat16)
        out_specs = anywhere
        scratch = [
            pltpu.VMEM(queries.shape, jnp.bfloat16),
            pltpu.SemaphoreType.DMA((QUERY_HEADS // SENT,)),
        ]
    else:
        earlier = anywhere
        own = pltpu.with_memory_space_constraint(own, pltpu.HBM)
        level = pltpu.with_memory_space_constraint(level, pltpu.HBM)
        out_shape = [jax.ShapeDtypeStruct(queries.shape, jnp.float32)] * 2
        out_specs = [in_vmem] * 2
        scratch = [
            pltpu.VMEM(queries.shape, jnp.float32),
            pltpu.VMEM(level.shape, jnp.float32),
            pltpu.SemaphoreType.DMA((2, KEY_VALUE_HEADS)),
        ]
    return pl.pallas_call(
        functools.partial(far_kernel, last=last),
        out_shape=out_shape,
        in_specs=[
            in_vmem,
            in_vmem,
            earlier,
            earlier,
            *[in_vmem] * len(far),
        ],
        out_specs=out_specs,
        scratch_shapes=scratch,
        compiler_params=pltpu.CompilerParams(vmem_limit_bytes=30 * MIB),
        cost_estimate=pl.CostEstimate(
            flops=4 * scores * HEAD_SIZE, bytes_accessed=10 * MIB, transcendentals=scores
        ),
        name="late_attention" if last else "early_attention",
    )(selected, queries, own, level, *far)


def local(queries, all_key_states, all_value_states, selected):
    devices = lax.axis_size("ctx")
    rows = all_key_states.shape[0]
    piece_rows = rows * COPIES // devices
    packed = pack(all_key_states, all_value_states, devices)
    packed, queries = lax.optimization_barrier((packed, queries))
    held = lax.all_to_all(packed, "ctx", split_axis=0, concat_axis=0, tiled=True)
    own, level = own_attention(queries, all_key_states, all_value_states)
    mine, own, level = lax.optimization_barrier((selected, own, level))
    requests = exchange_requests(mine, devices // COPIES, devices)
    requests = jnp.clip(requests, 0, devices - 1)
    moved = deliver(pick_pieces(requests, held), devices)
    far = [m.reshape(2, SLOTS, piece_rows, HEAD_SIZE) for m in moved]
    early, late = far[: len(far) // 2], far[len(far) // 2 :]
    if piece_rows % 16 != 0:
        early, late = [jnp.concatenate(early, axis=2)], [jnp.concatenate(late, axis=2)]
    own, level = far_attention(selected, queries, own, level, early, last=False)
    return far_attention(selected, queries, own, level, late, last=True)


def solution(mesh):
    placed = P(("groups", "ctx"), None)
    return jax.shard_map(
        local, mesh=mesh, in_specs=(placed,) * 4, out_specs=placed, check_vma=False
    )
```

```python
import functools
import math

import jax
import jax.numpy as jnp
from jax import lax
from jax.experimental import pallas as pl
from jax.experimental.pallas import tpu as pltpu
from jax.sharding import PartitionSpec as P

QUERY_HEADS = 32
KEY_VALUE_HEADS = 4
HEAD_SIZE = 128
GROUP = QUERY_HEADS // KEY_VALUE_HEADS
SLOTS = 2 * KEY_VALUE_HEADS
COPIES = 2
MIB = 1024 * 1024


def pack_kernel(key_ref, value_ref, out_ref, staged, arrived, left):
    shares, piece_rows, _ = key_ref.shape
    half = KEY_VALUE_HEADS * piece_rows

    def take(slot):
        ref = key_ref if slot < KEY_VALUE_HEADS else value_ref
        head = slot % KEY_VALUE_HEADS
        lanes = pl.ds(head * HEAD_SIZE, HEAD_SIZE)
        rows = pl.ds(slot * piece_rows, piece_rows)
        return pltpu.make_async_copy(
            ref.at[:, :, lanes], staged.at[:, rows, :], arrived.at[slot]
        )

    def give(which, copy):
        rows = pl.ds(which * half, half)
        return pltpu.make_async_copy(
            staged.at[:, rows, :],
            out_ref.at[pl.ds(copy * shares, shares), rows, :],
            left.at[which, copy],
        )

    for slot in range(SLOTS):
        take(slot).start()
    for which in range(2):
        for head in range(KEY_VALUE_HEADS):
            take(which * KEY_VALUE_HEADS + head).wait()
        for copy in range(COPIES):
            give(which, copy).start()
    for which in range(2):
        for copy in range(COPIES):
            give(which, copy).wait()


def pack(keys, values, devices):
    shares = devices // COPIES
    piece_rows = keys.shape[0] // shares
    if piece_rows % 16 == 0:
        split = (shares, piece_rows, keys.shape[1])
        return pl.pallas_call(
            pack_kernel,
            out_shape=jax.ShapeDtypeStruct(
                (devices, SLOTS * piece_rows, HEAD_SIZE), jnp.bfloat16
            ),
            in_specs=[pl.BlockSpec(memory_space=pl.ANY)] * 2,
            out_specs=pl.BlockSpec(memory_space=pl.ANY),
            scratch_shapes=[
                pltpu.VMEM((shares, SLOTS * piece_rows, HEAD_SIZE), jnp.bfloat16),
                pltpu.SemaphoreType.DMA((SLOTS,)),
                pltpu.SemaphoreType.DMA((2, COPIES)),
            ],
            name="pack",
        )(keys.reshape(split), values.reshape(split))
    both = jnp.concatenate([keys, values], axis=1)
    both = both.reshape(shares, piece_rows, SLOTS, HEAD_SIZE).transpose(0, 2, 1, 3)
    both = both.reshape(shares, SLOTS * piece_rows, HEAD_SIZE)
    return jnp.concatenate([both] * COPIES, axis=0)


def partner(position, step):
    return position ^ step


def swap(array, step, devices):
    return lax.ppermute(array, "ctx", [(i, partner(i, step)) for i in range(devices)])


def exchange_requests(selected, shares, devices):
    requests = selected
    step = 1
    while step < shares:
        requests = jnp.concatenate([requests, swap(requests, step, devices)], axis=0)
        step *= 2
    return requests


def scalar_of(values, row, column):
    rows = lax.broadcasted_iota(jnp.int32, values.shape, 0)
    columns = lax.broadcasted_iota(jnp.int32, values.shape, 1)
    here = jnp.logical_and(rows == row, columns == column)
    return jnp.max(jnp.where(here, values.astype(jnp.float32), 0.0)).astype(jnp.int32)


def pick_kernel(requests_ref, held_ref, *out_refs):
    requests = requests_ref[...]
    for step, out_ref in enumerate(out_refs):
        for pick in range(2):
            out_ref[pick] = held_ref[scalar_of(requests, step, pick)]


def pick_pieces(requests, held):
    devices, rows, _ = held.shape
    shares = devices // COPIES
    return pl.pallas_call(
        pick_kernel,
        out_shape=[jax.ShapeDtypeStruct((2, rows, HEAD_SIZE), jnp.bfloat16)] * shares,
        in_specs=[pl.BlockSpec(memory_space=pltpu.VMEM)] * 2,
        out_specs=[pl.BlockSpec(memory_space=pltpu.VMEM)] * shares,
        compiler_params=pltpu.CompilerParams(vmem_limit_bytes=16 * MIB),
        name="pick_pieces",
    )(requests, held)


def delivery_order(shares):
    half, quarter = shares // 2, shares // 4
    apart = zip(range(half, half + quarter), range(quarter, half))
    return [*range(1, quarter), *[s for pair in apart for s in pair], *range(half + quarter, shares)]


def deliver(pieces, devices):
    order = delivery_order(len(pieces))
    return [pieces[0]] + [swap(pieces[step], step, devices) for step in order]


FACTOR = math.log2(math.e) / math.sqrt(HEAD_SIZE)
PAIR = 2
SENT = 4
LARGE_SUM = 2.0**100


def head_lanes(head):
    return slice(head * HEAD_SIZE, (head + 1) * HEAD_SIZE)


def with_ones(value):
    return jnp.concatenate([value, jnp.ones_like(value)], axis=1)


def inverse_of(positive):
    return pl.reciprocal(positive, approx=True)


def dot(a, b):
    return jnp.dot(a, b, preferred_element_type=jnp.float32)


def stack_heads(wide):
    heads = wide.shape[1] // HEAD_SIZE
    return jnp.concatenate([wide[:, head_lanes(h)] for h in range(heads)], axis=0)


def own_kernel(query_ref, key_ref, value_ref, out_ref, level_ref):
    rows = query_ref.shape[0]
    row = lax.broadcasted_iota(jnp.int32, (rows, rows), 0)
    column = lax.broadcasted_iota(jnp.int32, (rows, rows), 1)
    causal = column <= row
    lane = lax.broadcasted_iota(jnp.int32, (rows, HEAD_SIZE), 1)
    keys_across = key_ref[...].T
    value = with_ones(value_ref[...])

    def score(first):
        lanes = slice(first * HEAD_SIZE, (first + PAIR) * HEAD_SIZE)
        return dot(stack_heads(query_ref[:, lanes]), keys_across)

    def finish(first, scores):
        weights, shifts = [], []
        for h in range(PAIR):
            part = jnp.where(causal, scores[h * rows : (h + 1) * rows], -1e30)
            shift = jnp.max(part, axis=1, keepdims=True) * FACTOR
            shifts.append(shift)
            weights.append(jnp.exp2(part * FACTOR - shift).astype(jnp.bfloat16))
        both = dot(jnp.concatenate(weights, axis=0), value)
        for h in range(PAIR):
            part = both[h * rows : (h + 1) * rows]
            row_sum = part[:, HEAD_SIZE:]
            out_ref[:, head_lanes(first + h)] = part[:, :HEAD_SIZE] / row_sum
            level = shifts[h] + jnp.log2(row_sum)
            level_ref[...] = jnp.where(lane == first + h, level, level_ref[...])

    level_ref[...] = jnp.zeros_like(level_ref)
    scores = score(0)
    for first in range(0, GROUP, PAIR):
        following = score(first + PAIR) if first + PAIR < GROUP else None
        finish(first, scores)
        scores = following


def own_attention(queries, keys, values):
    rows = queries.shape[0]
    width = GROUP * HEAD_SIZE
    scores = QUERY_HEADS * rows * rows
    return pl.pallas_call(
        own_kernel,
        out_shape=[
            pltpu.HBM(queries.shape, jnp.float32),
            pltpu.HBM((rows, KEY_VALUE_HEADS * HEAD_SIZE), jnp.float32),
        ],
        grid=(KEY_VALUE_HEADS,),
        in_specs=[
            pl.BlockSpec((rows, width), lambda g: (0, g)),
            pl.BlockSpec((rows, HEAD_SIZE), lambda g: (0, g)),
            pl.BlockSpec((rows, HEAD_SIZE), lambda g: (0, g)),
        ],
        out_specs=[
            pl.BlockSpec((rows, width), lambda g: (0, g)),
            pl.BlockSpec((rows, HEAD_SIZE), lambda g: (0, g)),
        ],
        compiler_params=pltpu.CompilerParams(vmem_limit_bytes=16 * MIB),
        cost_estimate=pl.CostEstimate(
            flops=4 * scores * HEAD_SIZE, bytes_accessed=7 * MIB, transcendentals=scores
        ),
        name="own_attention",
    )(queries, keys, values)


def far_kernel(selected_ref, query_ref, own_in, level_in, *refs, last):
    if last:
        *far_refs, out_ref, staged, sems = refs
        own_ref, level_ref = own_in, level_in
    else:
        *far_refs, out_ref, new_level_ref, own_ref, level_ref, sems = refs
    rows = query_ref.shape[0]
    width = GROUP * HEAD_SIZE

    def wide(group):
        start = group * width
        return pl.ds(start if isinstance(group, int) else pl.multiple_of(start, width), width)

    def narrow(group):
        start = group * HEAD_SIZE
        fixed = isinstance(group, int)
        return pl.ds(start if fixed else pl.multiple_of(start, HEAD_SIZE), HEAD_SIZE)

    def level_of(group, head):
        if last:
            return level_ref[:, head_of(group, head)]
        one = level_ref[:, narrow(group)][:, head : head + 1]
        return jnp.broadcast_to(one, (rows, HEAD_SIZE))

    def fetch(group, which):
        source, target = ((own_in, own_ref), (level_in, level_ref))[which]
        lanes = wide(group) if which == 0 else narrow(group)
        return pltpu.make_async_copy(
            source.at[:, lanes], target.at[:, lanes], sems.at[which, group]
        )

    def send(part):
        start = part * SENT * HEAD_SIZE
        fixed = isinstance(part, int)
        lanes = pl.ds(
            start if fixed else pl.multiple_of(start, SENT * HEAD_SIZE), SENT * HEAD_SIZE
        )
        return pltpu.make_async_copy(staged.at[:, lanes], out_ref.at[:, lanes], sems.at[part])

    if not last:
        for group in range(KEY_VALUE_HEADS):
            fetch(group, 1).start()
            fetch(group, 0).start()

    def head_of(group, head):
        start = (group * GROUP + head) * HEAD_SIZE
        fixed = isinstance(group, int)
        return pl.ds(start if fixed else pl.multiple_of(start, HEAD_SIZE), HEAD_SIZE)

    def store(lanes, mixture, row_sum, level):
        result = mixture * inverse_of(row_sum)
        if last:
            staged[:, lanes] = result.astype(staged.dtype)
        else:
            out_ref[:, lanes] = result
            new_level_ref[:, lanes] = level + jnp.log2(row_sum)

    def attend(picks):
        count = len(picks) * sum(ref.shape[2] for ref in far_refs)

        def block(slot):
            return jnp.concatenate([ref[p, slot] for p in picks for ref in far_refs], axis=0)

        def keys_and_values(group):
            return block(group).T, with_ones(block(group + KEY_VALUE_HEADS))

        def repeat(narrow):
            return jnp.concatenate([narrow] * (count // HEAD_SIZE), axis=1)

        def quick(group, head, scores, value, largest):
            lanes = [head_of(group, head + h) for h in range(PAIR)]
            levels = [level_of(group, head + h) for h in range(PAIR)]
            weights = [
                jnp.exp2(scores[h * rows : (h + 1) * rows] * FACTOR - repeat(levels[h]))
                for h in range(PAIR)
            ]
            both = dot(jnp.concatenate(weights, axis=0).astype(jnp.bfloat16), value)
            for h in range(PAIR):
                part = both[h * rows : (h + 1) * rows]
                row_sum = 1.0 + part[:, HEAD_SIZE:]
                store(lanes[h], own_ref[:, lanes[h]] + part[:, :HEAD_SIZE], row_sum, levels[h])
                largest = jnp.maximum(
                    largest, jnp.max(row_sum.reshape(rows // 8, 8, HEAD_SIZE), axis=0)
                )
            return largest

        def careful(group, head, scores, value):
            lanes = head_of(group, head)
            part = scores * FACTOR
            level = level_of(group, head)
            shift = jnp.maximum(jnp.max(part, axis=1, keepdims=True), level)
            weights = jnp.exp2(part - repeat(shift)).astype(jnp.bfloat16)
            both = dot(weights, value)
            share = jnp.exp2(level - shift)
            mixture = own_ref[:, lanes] * share + both[:, :HEAD_SIZE]
            store(lanes, mixture, share + both[:, HEAD_SIZE:], shift)

        def score(group, head, keys_across, heads=1):
            query = [query_ref[:, head_of(group, head + h)] for h in range(heads)]
            return dot(jnp.concatenate(query, axis=0), keys_across)

        largest = jnp.zeros((8, HEAD_SIZE), jnp.float32)
        order = [(g, h) for g in range(KEY_VALUE_HEADS) for h in range(0, GROUP, PAIR)]
        held = {0: keys_and_values(0)}
        scores = score(0, 0, held[0][0], PAIR)
        for (group, head), later in zip(order, order[1:] + [None]):
            following = None
            if later is not None:
                if later[0] not in held:
                    held[later[0]] = keys_and_values(later[0])
                following = score(*later, held[later[0]][0], PAIR)
            if head == 0 and not last:
                fetch(group, 1).wait()
                fetch(group, 0).wait()
            largest = quick(group, head, scores, held[group][1], largest)
            if (head + PAIR) % SENT == 0 and last:
                send((group * GROUP + head) // SENT).start()
            scores = following

        @pl.when(jnp.max(largest) > LARGE_SUM)
        def _():
            @pl.loop(0, KEY_VALUE_HEADS)
            def _(group):
                parts = [group * (GROUP // SENT) + part for part in range(GROUP // SENT)]
                if last:
                    for part in parts:
                        send(part).wait()
                keys_across, value = keys_and_values(group)
                for head in range(GROUP):
                    careful(group, head, score(group, head, keys_across), value)
                if last:
                    for part in parts:
                        send(part).start()

    my_block = lax.axis_index("ctx")
    selected = selected_ref[...]
    chosen = scalar_of(selected, 0, 0), scalar_of(selected, 0, 1)
    first = chosen[0] < my_block
    second = jnp.logical_and(chosen[1] < my_block, chosen[1] != chosen[0])
    valid = first.astype(jnp.int32) + second.astype(jnp.int32)

    @pl.when(valid == 2)
    def _():
        attend((0, 1))

    @pl.when(valid == 1)
    def _():
        attend((second.astype(jnp.int32),))

    @pl.when(valid == 0)
    def _():
        @pl.loop(0, KEY_VALUE_HEADS)
        def _(group):
            lanes = wide(group)
            if last:
                staged[:, lanes] = own_ref[:, lanes].astype(staged.dtype)
                for part in range(GROUP // SENT):
                    send(group * (GROUP // SENT) + part).start()
            else:
                fetch(group, 1).wait()
                fetch(group, 0).wait()
                out_ref[:, lanes] = own_ref[:, lanes]
                for head in range(GROUP):
                    new_level_ref[:, head_of(group, head)] = level_of(group, head)

    if last:

        @pl.loop(0, QUERY_HEADS // SENT)
        def _(part):
            send(part).wait()


def far_attention(selected, queries, own, level, far, last):
    rows = queries.shape[0]
    scores = QUERY_HEADS * rows * 2 * sum(piece.shape[2] for piece in far)
    in_vmem = pl.BlockSpec(memory_space=pltpu.VMEM)
    anywhere = pl.BlockSpec(memory_space=pl.ANY)
    if last:
        earlier = in_vmem
        out_shape = jax.ShapeDtypeStruct(queries.shape, jnp.bfloat16)
        out_specs = anywhere
        scratch = [
            pltpu.VMEM(queries.shape, jnp.bfloat16),
            pltpu.SemaphoreType.DMA((QUERY_HEADS // SENT,)),
        ]
    else:
        earlier = anywhere
        own = pltpu.with_memory_space_constraint(own, pltpu.HBM)
        level = pltpu.with_memory_space_constraint(level, pltpu.HBM)
        out_shape = [jax.ShapeDtypeStruct(queries.shape, jnp.float32)] * 2
        out_specs = [in_vmem] * 2
        scratch = [
            pltpu.VMEM(queries.shape, jnp.float32),
            pltpu.VMEM(level.shape, jnp.float32),
            pltpu.SemaphoreType.DMA((2, KEY_VALUE_HEADS)),
        ]
    return pl.pallas_call(
        functools.partial(far_kernel, last=last),
        out_shape=out_shape,
        in_specs=[
            in_vmem,
            in_vmem,
            earlier,
            earlier,
            *[in_vmem] * len(far),
        ],
        out_specs=out_specs,
        scratch_shapes=scratch,
        compiler_params=pltpu.CompilerParams(vmem_limit_bytes=30 * MIB),
        cost_estimate=pl.CostEstimate(
            flops=4 * scores * HEAD_SIZE, bytes_accessed=10 * MIB, transcendentals=scores
        ),
        name="late_attention" if last else "early_attention",
    )(selected, queries, own, level, *far)


def local(queries, all_key_states, all_value_states, selected):
    devices = lax.axis_size("ctx")
    rows = all_key_states.shape[0]
    piece_rows = rows * COPIES // devices
    packed = pack(all_key_states, all_value_states, devices)
    packed, queries = lax.optimization_barrier((packed, queries))
    held = lax.all_to_all(packed, "ctx", split_axis=0, concat_axis=0, tiled=True)
    own, level = own_attention(queries, all_key_states, all_value_states)
    mine, own, level = lax.optimization_barrier((selected, own, level))
    requests = exchange_requests(mine, devices // COPIES, devices)
    requests = jnp.clip(requests, 0, devices - 1)
    moved = deliver(pick_pieces(requests, held), devices)
    far = [m.reshape(2, SLOTS, piece_rows, HEAD_SIZE) for m in moved]
    early, late = far[: len(far) // 2], far[len(far) // 2 :]
    if piece_rows % 16 != 0:
        early, late = [jnp.concatenate(early, axis=2)], [jnp.concatenate(late, axis=2)]
    own, level = far_attention(selected, queries, own, level, early, last=False)
    return far_attention(selected, queries, own, level, late, last=True)


def solution(mesh):
    placed = P(("groups", "ctx"), None)
    return jax.shard_map(
        local, mesh=mesh, in_specs=(placed,) * 4, out_specs=placed, check_vma=False
    )
```

```python
import functools
import math

import jax
import jax.numpy as jnp
from jax import lax
from jax.experimental import pallas as pl
from jax.experimental.pallas import tpu as pltpu
from jax.sharding import PartitionSpec as P

QUERY_HEADS = 32
KEY_VALUE_HEADS = 4
HEAD_SIZE = 128
GROUP = QUERY_HEADS // KEY_VALUE_HEADS
SLOTS = 2 * KEY_VALUE_HEADS
COPIES = 2
MIB = 1024 * 1024


def mixed_order(devices):
    shares = devices // COPIES
    return [copy * shares + share for share in range(shares) for copy in range(COPIES)]


def place_of(block, devices):
    shares = devices // COPIES
    return block % shares * COPIES + block // shares


def pack_kernel(key_ref, value_ref, out_ref, staged, arrived, left):
    shares, piece_rows, _ = key_ref.shape
    half = KEY_VALUE_HEADS * piece_rows

    def take(slot):
        ref = key_ref if slot < KEY_VALUE_HEADS else value_ref
        head = slot % KEY_VALUE_HEADS
        lanes = pl.ds(head * HEAD_SIZE, HEAD_SIZE)
        rows = pl.ds(slot * piece_rows, piece_rows)
        return pltpu.make_async_copy(
            ref.at[:, :, lanes], staged.at[:, rows, :], arrived.at[slot]
        )

    def give(which, copy):
        rows = pl.ds(which * half, half)
        return pltpu.make_async_copy(
            staged.at[:, rows, :], out_ref.at[:, copy, rows, :], left.at[which, copy]
        )

    for slot in range(SLOTS):
        take(slot).start()
    for which in range(2):
        for head in range(KEY_VALUE_HEADS):
            take(which * KEY_VALUE_HEADS + head).wait()
        for copy in range(COPIES):
            give(which, copy).start()
    for which in range(2):
        for copy in range(COPIES):
            give(which, copy).wait()


def pack(keys, values, devices):
    shares = devices // COPIES
    piece_rows = keys.shape[0] // shares
    if piece_rows % 16 == 0:
        split = (shares, piece_rows, keys.shape[1])
        return pl.pallas_call(
            pack_kernel,
            out_shape=jax.ShapeDtypeStruct(
                (shares, COPIES, SLOTS * piece_rows, HEAD_SIZE), jnp.bfloat16
            ),
            in_specs=[pl.BlockSpec(memory_space=pl.ANY)] * 2,
            out_specs=pl.BlockSpec(memory_space=pl.ANY),
            scratch_shapes=[
                pltpu.VMEM((shares, SLOTS * piece_rows, HEAD_SIZE), jnp.bfloat16),
                pltpu.SemaphoreType.DMA((SLOTS,)),
                pltpu.SemaphoreType.DMA((2, COPIES)),
            ],
            name="pack",
        )(keys.reshape(split), values.reshape(split)).reshape(
            devices, SLOTS * piece_rows, HEAD_SIZE
        )
    both = jnp.concatenate([keys, values], axis=1)
    both = both.reshape(shares, piece_rows, SLOTS, HEAD_SIZE).transpose(0, 2, 1, 3)
    both = both.reshape(shares, SLOTS * piece_rows, HEAD_SIZE)
    return jnp.repeat(both, COPIES, axis=0)


def partner(position, step):
    return position ^ step


def swap(array, step, devices):
    return lax.ppermute(array, "ctx", [(i, partner(i, step)) for i in range(devices)])


def exchange_requests(selected, shares, devices):
    requests = selected
    step = 1
    while step < shares:
        requests = jnp.concatenate([requests, swap(requests, step, devices)], axis=0)
        step *= 2
    return requests


def scalar_of(values, row, column):
    rows = lax.broadcasted_iota(jnp.int32, values.shape, 0)
    columns = lax.broadcasted_iota(jnp.int32, values.shape, 1)
    here = jnp.logical_and(rows == row, columns == column)
    return jnp.max(jnp.where(here, values.astype(jnp.float32), 0.0)).astype(jnp.int32)


def pick_kernel(requests_ref, held_ref, *out_refs):
    requests = requests_ref[...]
    for step, out_ref in enumerate(out_refs):
        for pick in range(2):
            out_ref[pick] = held_ref[scalar_of(requests, step, pick)]


def pick_pieces(requests, held):
    devices, rows, _ = held.shape
    shares = devices // COPIES
    return pl.pallas_call(
        pick_kernel,
        out_shape=[jax.ShapeDtypeStruct((2, rows, HEAD_SIZE), jnp.bfloat16)] * shares,
        in_specs=[pl.BlockSpec(memory_space=pltpu.VMEM)] * 2,
        out_specs=[pl.BlockSpec(memory_space=pltpu.VMEM)] * shares,
        compiler_params=pltpu.CompilerParams(vmem_limit_bytes=16 * MIB),
        name="pick_pieces",
    )(requests, held)


def delivery_order(shares):
    half, quarter = shares // 2, shares // 4
    apart = zip(range(half, half + quarter), range(quarter, half))
    return [*range(1, quarter), *[s for pair in apart for s in pair], *range(half + quarter, shares)]


def deliver(pieces, devices):
    order = delivery_order(len(pieces))
    return [pieces[0]] + [swap(pieces[step], step, devices) for step in order]


FACTOR = math.log2(math.e) / math.sqrt(HEAD_SIZE)
PAIR = 2
SENT = 4
LARGE_SUM = 2.0**100


def head_lanes(head):
    return slice(head * HEAD_SIZE, (head + 1) * HEAD_SIZE)


def with_ones(value):
    return jnp.concatenate([value, jnp.ones_like(value)], axis=1)


def inverse_of(positive):
    return pl.reciprocal(positive, approx=True)


def dot(a, b):
    return jnp.dot(a, b, preferred_element_type=jnp.float32)


def stack_heads(wide):
    heads = wide.shape[1] // HEAD_SIZE
    return jnp.concatenate([wide[:, head_lanes(h)] for h in range(heads)], axis=0)


def own_kernel(query_ref, key_ref, value_ref, out_ref, level_ref):
    rows = query_ref.shape[0]
    row = lax.broadcasted_iota(jnp.int32, (rows, rows), 0)
    column = lax.broadcasted_iota(jnp.int32, (rows, rows), 1)
    causal = column <= row
    lane = lax.broadcasted_iota(jnp.int32, (rows, HEAD_SIZE), 1)
    keys_across = key_ref[...].T
    value = with_ones(value_ref[...])

    def score(first):
        lanes = slice(first * HEAD_SIZE, (first + PAIR) * HEAD_SIZE)
        return dot(stack_heads(query_ref[:, lanes]), keys_across)

    def finish(first, scores):
        weights, shifts = [], []
        for h in range(PAIR):
            part = jnp.where(causal, scores[h * rows : (h + 1) * rows], -1e30)
            shift = jnp.max(part, axis=1, keepdims=True) * FACTOR
            shifts.append(shift)
            weights.append(jnp.exp2(part * FACTOR - shift).astype(jnp.bfloat16))
        both = dot(jnp.concatenate(weights, axis=0), value)
        for h in range(PAIR):
            part = both[h * rows : (h + 1) * rows]
            row_sum = part[:, HEAD_SIZE:]
            out_ref[:, head_lanes(first + h)] = part[:, :HEAD_SIZE] / row_sum
            level = shifts[h] + jnp.log2(row_sum)
            level_ref[...] = jnp.where(lane == first + h, level, level_ref[...])

    level_ref[...] = jnp.zeros_like(level_ref)
    scores = score(0)
    for first in range(0, GROUP, PAIR):
        following = score(first + PAIR) if first + PAIR < GROUP else None
        finish(first, scores)
        scores = following


def own_attention(queries, keys, values):
    rows = queries.shape[0]
    width = GROUP * HEAD_SIZE
    scores = QUERY_HEADS * rows * rows
    return pl.pallas_call(
        own_kernel,
        out_shape=[
            pltpu.HBM(queries.shape, jnp.float32),
            pltpu.HBM((rows, KEY_VALUE_HEADS * HEAD_SIZE), jnp.float32),
        ],
        grid=(KEY_VALUE_HEADS,),
        in_specs=[
            pl.BlockSpec((rows, width), lambda g: (0, g)),
            pl.BlockSpec((rows, HEAD_SIZE), lambda g: (0, g)),
            pl.BlockSpec((rows, HEAD_SIZE), lambda g: (0, g)),
        ],
        out_specs=[
            pl.BlockSpec((rows, width), lambda g: (0, g)),
            pl.BlockSpec((rows, HEAD_SIZE), lambda g: (0, g)),
        ],
        compiler_params=pltpu.CompilerParams(vmem_limit_bytes=16 * MIB),
        cost_estimate=pl.CostEstimate(
            flops=4 * scores * HEAD_SIZE, bytes_accessed=7 * MIB, transcendentals=scores
        ),
        name="own_attention",
    )(queries, keys, values)


def far_kernel(selected_ref, query_ref, own_in, level_in, *refs, last):
    if last:
        *far_refs, out_ref, staged, sems = refs
        own_ref, level_ref = own_in, level_in
    else:
        *far_refs, out_ref, new_level_ref, own_ref, level_ref, sems = refs
    rows = query_ref.shape[0]
    width = GROUP * HEAD_SIZE

    def wide(group):
        start = group * width
        return pl.ds(start if isinstance(group, int) else pl.multiple_of(start, width), width)

    def narrow(group):
        start = group * HEAD_SIZE
        fixed = isinstance(group, int)
        return pl.ds(start if fixed else pl.multiple_of(start, HEAD_SIZE), HEAD_SIZE)

    def level_of(group, head):
        if last:
            return level_ref[:, head_of(group, head)]
        one = level_ref[:, narrow(group)][:, head : head + 1]
        return jnp.broadcast_to(one, (rows, HEAD_SIZE))

    def fetch(group, which):
        source, target = ((own_in, own_ref), (level_in, level_ref))[which]
        lanes = wide(group) if which == 0 else narrow(group)
        return pltpu.make_async_copy(
            source.at[:, lanes], target.at[:, lanes], sems.at[which, group]
        )

    def send(part):
        start = part * SENT * HEAD_SIZE
        fixed = isinstance(part, int)
        lanes = pl.ds(
            start if fixed else pl.multiple_of(start, SENT * HEAD_SIZE), SENT * HEAD_SIZE
        )
        return pltpu.make_async_copy(staged.at[:, lanes], out_ref.at[:, lanes], sems.at[part])

    if not last:
        for group in range(KEY_VALUE_HEADS):
            fetch(group, 1).start()
            fetch(group, 0).start()

    def head_of(group, head):
        start = (group * GROUP + head) * HEAD_SIZE
        fixed = isinstance(group, int)
        return pl.ds(start if fixed else pl.multiple_of(start, HEAD_SIZE), HEAD_SIZE)

    def store(lanes, mixture, row_sum, level):
        result = mixture * inverse_of(row_sum)
        if last:
            staged[:, lanes] = result.astype(staged.dtype)
        else:
            out_ref[:, lanes] = result
            new_level_ref[:, lanes] = level + jnp.log2(row_sum)

    def attend(picks):
        count = len(picks) * sum(ref.shape[2] for ref in far_refs)

        def block(slot):
            return jnp.concatenate([ref[p, slot] for p in picks for ref in far_refs], axis=0)

        def keys_and_values(group):
            return block(group).T, with_ones(block(group + KEY_VALUE_HEADS))

        def repeat(narrow):
            return jnp.concatenate([narrow] * (count // HEAD_SIZE), axis=1)

        def quick(group, head, scores, value, largest):
            lanes = head_of(group, head)
            level = level_of(group, head)
            weights = jnp.exp2(scores * FACTOR - repeat(level)).astype(jnp.bfloat16)
            both = dot(weights, value)
            row_sum = 1.0 + both[:, HEAD_SIZE:]
            store(lanes, own_ref[:, lanes] + both[:, :HEAD_SIZE], row_sum, level)
            return jnp.maximum(
                largest, jnp.max(row_sum.reshape(rows // 8, 8, HEAD_SIZE), axis=0)
            )

        def careful(group, head, scores, value):
            lanes = head_of(group, head)
            part = scores * FACTOR
            level = level_of(group, head)
            shift = jnp.maximum(jnp.max(part, axis=1, keepdims=True), level)
            weights = jnp.exp2(part - repeat(shift)).astype(jnp.bfloat16)
            both = dot(weights, value)
            share = jnp.exp2(level - shift)
            mixture = own_ref[:, lanes] * share + both[:, :HEAD_SIZE]
            store(lanes, mixture, share + both[:, HEAD_SIZE:], shift)

        def score(group, head, keys_across):
            return dot(query_ref[:, head_of(group, head)], keys_across)

        largest = jnp.zeros((8, HEAD_SIZE), jnp.float32)
        order = [(g, h) for g in range(KEY_VALUE_HEADS) for h in range(GROUP)]
        held = {0: keys_and_values(0)}
        scores = score(0, 0, held[0][0])
        for (group, head), later in zip(order, order[1:] + [None]):
            following = None
            if later is not None:
                if later[0] not in held:
                    held[later[0]] = keys_and_values(later[0])
                following = score(*later, held[later[0]][0])
            if head == 0 and not last:
                fetch(group, 1).wait()
                fetch(group, 0).wait()
            largest = quick(group, head, scores, held[group][1], largest)
            if (head + 1) % SENT == 0 and last:
                send((group * GROUP + head) // SENT).start()
            scores = following

        @pl.when(jnp.max(largest) > LARGE_SUM)
        def _():
            @pl.loop(0, KEY_VALUE_HEADS)
            def _(group):
                parts = [group * (GROUP // SENT) + part for part in range(GROUP // SENT)]
                if last:
                    for part in parts:
                        send(part).wait()
                keys_across, value = keys_and_values(group)
                for head in range(GROUP):
                    careful(group, head, score(group, head, keys_across), value)
                if last:
                    for part in parts:
                        send(part).start()

    my_block = lax.axis_index("ctx")
    selected = selected_ref[...]
    chosen = scalar_of(selected, 0, 0), scalar_of(selected, 0, 1)
    first = chosen[0] < my_block
    second = jnp.logical_and(chosen[1] < my_block, chosen[1] != chosen[0])
    valid = first.astype(jnp.int32) + second.astype(jnp.int32)

    @pl.when(valid == 2)
    def _():
        attend((0, 1))

    @pl.when(valid == 1)
    def _():
        attend((second.astype(jnp.int32),))

    @pl.when(valid == 0)
    def _():
        @pl.loop(0, KEY_VALUE_HEADS)
        def _(group):
            lanes = wide(group)
            if last:
                staged[:, lanes] = own_ref[:, lanes].astype(staged.dtype)
                for part in range(GROUP // SENT):
                    send(group * (GROUP // SENT) + part).start()
            else:
                fetch(group, 1).wait()
                fetch(group, 0).wait()
                out_ref[:, lanes] = own_ref[:, lanes]
                for head in range(GROUP):
                    new_level_ref[:, head_of(group, head)] = level_of(group, head)

    if last:

        @pl.loop(0, QUERY_HEADS // SENT)
        def _(part):
            send(part).wait()


def far_attention(selected, queries, own, level, far, last):
    rows = queries.shape[0]
    scores = QUERY_HEADS * rows * 2 * sum(piece.shape[2] for piece in far)
    in_vmem = pl.BlockSpec(memory_space=pltpu.VMEM)
    anywhere = pl.BlockSpec(memory_space=pl.ANY)
    if last:
        earlier = in_vmem
        out_shape = jax.ShapeDtypeStruct(queries.shape, jnp.bfloat16)
        out_specs = anywhere
        scratch = [
            pltpu.VMEM(queries.shape, jnp.bfloat16),
            pltpu.SemaphoreType.DMA((QUERY_HEADS // SENT,)),
        ]
    else:
        earlier = anywhere
        own = pltpu.with_memory_space_constraint(own, pltpu.HBM)
        level = pltpu.with_memory_space_constraint(level, pltpu.HBM)
        out_shape = [jax.ShapeDtypeStruct(queries.shape, jnp.float32)] * 2
        out_specs = [in_vmem] * 2
        scratch = [
            pltpu.VMEM(queries.shape, jnp.float32),
            pltpu.VMEM(level.shape, jnp.float32),
            pltpu.SemaphoreType.DMA((2, KEY_VALUE_HEADS)),
        ]
    return pl.pallas_call(
        functools.partial(far_kernel, last=last),
        out_shape=out_shape,
        in_specs=[
            in_vmem,
            in_vmem,
            earlier,
            earlier,
            *[in_vmem] * len(far),
        ],
        out_specs=out_specs,
        scratch_shapes=scratch,
        compiler_params=pltpu.CompilerParams(vmem_limit_bytes=30 * MIB),
        cost_estimate=pl.CostEstimate(
            flops=4 * scores * HEAD_SIZE, bytes_accessed=10 * MIB, transcendentals=scores
        ),
        name="late_attention" if last else "early_attention",
    )(selected, queries, own, level, *far)


def local(queries, all_key_states, all_value_states, selected):
    devices = lax.axis_size("ctx")
    rows = all_key_states.shape[0]
    piece_rows = rows * COPIES // devices
    packed = pack(all_key_states, all_value_states, devices)
    packed, queries = lax.optimization_barrier((packed, queries))
    held = lax.all_to_all(
        packed,
        "ctx",
        split_axis=0,
        concat_axis=0,
        axis_index_groups=[mixed_order(devices)],
        tiled=True,
    )
    own, level = own_attention(queries, all_key_states, all_value_states)
    mine, own, level = lax.optimization_barrier((selected, own, level))
    requests = exchange_requests(mine, devices // COPIES, devices)
    requests = place_of(jnp.clip(requests, 0, devices - 1), devices)
    moved = deliver(pick_pieces(requests, held), devices)
    far = [m.reshape(2, SLOTS, piece_rows, HEAD_SIZE) for m in moved]
    early, late = far[: len(far) // 2], far[len(far) // 2 :]
    if piece_rows % 16 != 0:
        early, late = [jnp.concatenate(early, axis=2)], [jnp.concatenate(late, axis=2)]
    own, level = far_attention(selected, queries, own, level, early, last=False)
    return far_attention(selected, queries, own, level, late, last=True)


def solution(mesh):
    placed = P(("groups", "ctx"), None)
    return jax.shard_map(
        local, mesh=mesh, in_specs=(placed,) * 4, out_specs=placed, check_vma=False
    )
```

```python
import functools
import math

import jax
import jax.numpy as jnp
from jax import lax
from jax.experimental import pallas as pl
from jax.experimental.pallas import tpu as pltpu
from jax.sharding import PartitionSpec as P

QUERY_HEADS = 32
KEY_VALUE_HEADS = 4
HEAD_SIZE = 128
GROUP = QUERY_HEADS // KEY_VALUE_HEADS
SLOTS = 2 * KEY_VALUE_HEADS
COPIES = 2
MIB = 1024 * 1024


def mixed_order(devices):
    shares = devices // COPIES
    return [
        copy * shares + share + core
        for share in range(0, shares, 2)
        for copy in range(COPIES)
        for core in range(2)
    ]


def place_of(block, devices):
    shares = devices // COPIES
    share, copy = block % shares, block // shares
    return share // 2 * (2 * COPIES) + copy * 2 + share % 2


def pack_kernel(key_ref, value_ref, out_ref, staged, arrived, left):
    piece_rows = key_ref.shape[2]
    half = KEY_VALUE_HEADS * piece_rows

    def take(slot):
        ref = key_ref if slot < KEY_VALUE_HEADS else value_ref
        head = slot % KEY_VALUE_HEADS
        lanes = pl.ds(head * HEAD_SIZE, HEAD_SIZE)
        rows = pl.ds(slot * piece_rows, piece_rows)
        return pltpu.make_async_copy(
            ref.at[:, :, :, lanes], staged.at[:, :, rows, :], arrived.at[slot]
        )

    def give(which, copy):
        rows = pl.ds(which * half, half)
        return pltpu.make_async_copy(
            staged.at[:, :, rows, :], out_ref.at[:, copy, :, rows, :], left.at[which, copy]
        )

    for slot in range(SLOTS):
        take(slot).start()
    for which in range(2):
        for head in range(KEY_VALUE_HEADS):
            take(which * KEY_VALUE_HEADS + head).wait()
        for copy in range(COPIES):
            give(which, copy).start()
    for which in range(2):
        for copy in range(COPIES):
            give(which, copy).wait()


def pack(keys, values, devices):
    shares = devices // COPIES
    piece_rows = keys.shape[0] // shares
    if piece_rows % 16 == 0:
        split = (shares // 2, 2, piece_rows, keys.shape[1])
        return pl.pallas_call(
            pack_kernel,
            out_shape=jax.ShapeDtypeStruct(
                (shares // 2, COPIES, 2, SLOTS * piece_rows, HEAD_SIZE), jnp.bfloat16
            ),
            in_specs=[pl.BlockSpec(memory_space=pl.ANY)] * 2,
            out_specs=pl.BlockSpec(memory_space=pl.ANY),
            scratch_shapes=[
                pltpu.VMEM((shares // 2, 2, SLOTS * piece_rows, HEAD_SIZE), jnp.bfloat16),
                pltpu.SemaphoreType.DMA((SLOTS,)),
                pltpu.SemaphoreType.DMA((2, COPIES)),
            ],
            name="pack",
        )(keys.reshape(split), values.reshape(split)).reshape(
            devices, SLOTS * piece_rows, HEAD_SIZE
        )
    both = jnp.concatenate([keys, values], axis=1)
    both = both.reshape(shares, piece_rows, SLOTS, HEAD_SIZE).transpose(0, 2, 1, 3)
    both = both.reshape(shares // 2, 2, SLOTS * piece_rows, HEAD_SIZE)
    return jnp.repeat(both, COPIES, axis=0).reshape(devices, SLOTS * piece_rows, HEAD_SIZE)


def partner(position, step):
    return position ^ step


def swap(array, step, devices):
    return lax.ppermute(array, "ctx", [(i, partner(i, step)) for i in range(devices)])


def exchange_requests(selected, shares, devices):
    requests = selected
    step = 1
    while step < shares:
        requests = jnp.concatenate([requests, swap(requests, step, devices)], axis=0)
        step *= 2
    return requests


def scalar_of(values, row, column):
    rows = lax.broadcasted_iota(jnp.int32, values.shape, 0)
    columns = lax.broadcasted_iota(jnp.int32, values.shape, 1)
    here = jnp.logical_and(rows == row, columns == column)
    return jnp.max(jnp.where(here, values.astype(jnp.float32), 0.0)).astype(jnp.int32)


def pick_kernel(requests_ref, held_ref, *out_refs):
    requests = requests_ref[...]
    for step, out_ref in enumerate(out_refs):
        for pick in range(2):
            out_ref[pick] = held_ref[scalar_of(requests, step, pick)]


def pick_pieces(requests, held):
    devices, rows, _ = held.shape
    shares = devices // COPIES
    return pl.pallas_call(
        pick_kernel,
        out_shape=[jax.ShapeDtypeStruct((2, rows, HEAD_SIZE), jnp.bfloat16)] * shares,
        in_specs=[pl.BlockSpec(memory_space=pltpu.VMEM)] * 2,
        out_specs=[pl.BlockSpec(memory_space=pltpu.VMEM)] * shares,
        compiler_params=pltpu.CompilerParams(vmem_limit_bytes=16 * MIB),
        name="pick_pieces",
    )(requests, held)


def delivery_order(shares):
    half, quarter = shares // 2, shares // 4
    apart = zip(range(half, half + quarter), range(quarter, half))
    return [*range(1, quarter), *[s for pair in apart for s in pair], *range(half + quarter, shares)]


def deliver(pieces, devices):
    order = delivery_order(len(pieces))
    return [pieces[0]] + [swap(pieces[step], step, devices) for step in order]


FACTOR = math.log2(math.e) / math.sqrt(HEAD_SIZE)
PAIR = 2
SENT = 4
LARGE_SUM = 2.0**100


def head_lanes(head):
    return slice(head * HEAD_SIZE, (head + 1) * HEAD_SIZE)


def with_ones(value):
    return jnp.concatenate([value, jnp.ones_like(value)], axis=1)


def inverse_of(positive):
    return pl.reciprocal(positive, approx=True)


def dot(a, b):
    return jnp.dot(a, b, preferred_element_type=jnp.float32)


def stack_heads(wide):
    heads = wide.shape[1] // HEAD_SIZE
    return jnp.concatenate([wide[:, head_lanes(h)] for h in range(heads)], axis=0)


def own_kernel(query_ref, key_ref, value_ref, out_ref, level_ref):
    rows = query_ref.shape[0]
    row = lax.broadcasted_iota(jnp.int32, (rows, rows), 0)
    column = lax.broadcasted_iota(jnp.int32, (rows, rows), 1)
    causal = column <= row
    lane = lax.broadcasted_iota(jnp.int32, (rows, HEAD_SIZE), 1)
    keys_across = key_ref[...].T
    value = with_ones(value_ref[...])

    def score(first):
        lanes = slice(first * HEAD_SIZE, (first + PAIR) * HEAD_SIZE)
        return dot(stack_heads(query_ref[:, lanes]), keys_across)

    def finish(first, scores):
        weights, shifts = [], []
        for h in range(PAIR):
            part = jnp.where(causal, scores[h * rows : (h + 1) * rows], -1e30)
            shift = jnp.max(part, axis=1, keepdims=True) * FACTOR
            shifts.append(shift)
            weights.append(jnp.exp2(part * FACTOR - shift).astype(jnp.bfloat16))
        both = dot(jnp.concatenate(weights, axis=0), value)
        for h in range(PAIR):
            part = both[h * rows : (h + 1) * rows]
            row_sum = part[:, HEAD_SIZE:]
            out_ref[:, head_lanes(first + h)] = part[:, :HEAD_SIZE] / row_sum
            level = shifts[h] + jnp.log2(row_sum)
            level_ref[...] = jnp.where(lane == first + h, level, level_ref[...])

    level_ref[...] = jnp.zeros_like(level_ref)
    scores = score(0)
    for first in range(0, GROUP, PAIR):
        following = score(first + PAIR) if first + PAIR < GROUP else None
        finish(first, scores)
        scores = following


def own_attention(queries, keys, values):
    rows = queries.shape[0]
    width = GROUP * HEAD_SIZE
    scores = QUERY_HEADS * rows * rows
    return pl.pallas_call(
        own_kernel,
        out_shape=[
            pltpu.HBM(queries.shape, jnp.float32),
            pltpu.HBM((rows, KEY_VALUE_HEADS * HEAD_SIZE), jnp.float32),
        ],
        grid=(KEY_VALUE_HEADS,),
        in_specs=[
            pl.BlockSpec((rows, width), lambda g: (0, g)),
            pl.BlockSpec((rows, HEAD_SIZE), lambda g: (0, g)),
            pl.BlockSpec((rows, HEAD_SIZE), lambda g: (0, g)),
        ],
        out_specs=[
            pl.BlockSpec((rows, width), lambda g: (0, g)),
            pl.BlockSpec((rows, HEAD_SIZE), lambda g: (0, g)),
        ],
        compiler_params=pltpu.CompilerParams(vmem_limit_bytes=16 * MIB),
        cost_estimate=pl.CostEstimate(
            flops=4 * scores * HEAD_SIZE, bytes_accessed=7 * MIB, transcendentals=scores
        ),
        name="own_attention",
    )(queries, keys, values)


def far_kernel(selected_ref, query_ref, own_in, level_in, *refs, last):
    if last:
        *far_refs, out_ref, staged, sems = refs
        own_ref, level_ref = own_in, level_in
    else:
        *far_refs, out_ref, new_level_ref, own_ref, level_ref, sems = refs
    rows = query_ref.shape[0]
    width = GROUP * HEAD_SIZE

    def wide(group):
        start = group * width
        return pl.ds(start if isinstance(group, int) else pl.multiple_of(start, width), width)

    def narrow(group):
        start = group * HEAD_SIZE
        fixed = isinstance(group, int)
        return pl.ds(start if fixed else pl.multiple_of(start, HEAD_SIZE), HEAD_SIZE)

    def level_of(group, head):
        if last:
            return level_ref[:, head_of(group, head)]
        one = level_ref[:, narrow(group)][:, head : head + 1]
        return jnp.broadcast_to(one, (rows, HEAD_SIZE))

    def fetch(group, which):
        source, target = ((own_in, own_ref), (level_in, level_ref))[which]
        lanes = wide(group) if which == 0 else narrow(group)
        return pltpu.make_async_copy(
            source.at[:, lanes], target.at[:, lanes], sems.at[which, group]
        )

    def send(part):
        start = part * SENT * HEAD_SIZE
        fixed = isinstance(part, int)
        lanes = pl.ds(
            start if fixed else pl.multiple_of(start, SENT * HEAD_SIZE), SENT * HEAD_SIZE
        )
        return pltpu.make_async_copy(staged.at[:, lanes], out_ref.at[:, lanes], sems.at[part])

    if not last:
        for group in range(KEY_VALUE_HEADS):
            fetch(group, 1).start()
            fetch(group, 0).start()

    def head_of(group, head):
        start = (group * GROUP + head) * HEAD_SIZE
        fixed = isinstance(group, int)
        return pl.ds(start if fixed else pl.multiple_of(start, HEAD_SIZE), HEAD_SIZE)

    def store(lanes, mixture, row_sum, level):
        result = mixture * inverse_of(row_sum)
        if last:
            staged[:, lanes] = result.astype(staged.dtype)
        else:
            out_ref[:, lanes] = result
            new_level_ref[:, lanes] = level + jnp.log2(row_sum)

    def attend(picks):
        count = len(picks) * sum(ref.shape[2] for ref in far_refs)

        def block(slot):
            return jnp.concatenate([ref[p, slot] for p in picks for ref in far_refs], axis=0)

        def keys_and_values(group):
            return block(group).T, with_ones(block(group + KEY_VALUE_HEADS))

        def repeat(narrow):
            return jnp.concatenate([narrow] * (count // HEAD_SIZE), axis=1)

        def quick(group, head, scores, value, largest):
            lanes = head_of(group, head)
            level = level_of(group, head)
            weights = jnp.exp2(scores * FACTOR - repeat(level)).astype(jnp.bfloat16)
            both = dot(weights, value)
            row_sum = 1.0 + both[:, HEAD_SIZE:]
            store(lanes, own_ref[:, lanes] + both[:, :HEAD_SIZE], row_sum, level)
            return jnp.maximum(
                largest, jnp.max(row_sum.reshape(rows // 8, 8, HEAD_SIZE), axis=0)
            )

        def careful(group, head, scores, value):
            lanes = head_of(group, head)
            part = scores * FACTOR
            level = level_of(group, head)
            shift = jnp.maximum(jnp.max(part, axis=1, keepdims=True), level)
            weights = jnp.exp2(part - repeat(shift)).astype(jnp.bfloat16)
            both = dot(weights, value)
            share = jnp.exp2(level - shift)
            mixture = own_ref[:, lanes] * share + both[:, :HEAD_SIZE]
            store(lanes, mixture, share + both[:, HEAD_SIZE:], shift)

        def score(group, head, keys_across):
            return dot(query_ref[:, head_of(group, head)], keys_across)

        largest = jnp.zeros((8, HEAD_SIZE), jnp.float32)
        order = [(g, h) for g in range(KEY_VALUE_HEADS) for h in range(GROUP)]
        held = {0: keys_and_values(0)}
        scores = score(0, 0, held[0][0])
        for (group, head), later in zip(order, order[1:] + [None]):
            following = None
            if later is not None:
                if later[0] not in held:
                    held[later[0]] = keys_and_values(later[0])
                following = score(*later, held[later[0]][0])
            if head == 0 and not last:
                fetch(group, 1).wait()
                fetch(group, 0).wait()
            largest = quick(group, head, scores, held[group][1], largest)
            if (head + 1) % SENT == 0 and last:
                send((group * GROUP + head) // SENT).start()
            scores = following

        @pl.when(jnp.max(largest) > LARGE_SUM)
        def _():
            @pl.loop(0, KEY_VALUE_HEADS)
            def _(group):
                parts = [group * (GROUP // SENT) + part for part in range(GROUP // SENT)]
                if last:
                    for part in parts:
                        send(part).wait()
                keys_across, value = keys_and_values(group)
                for head in range(GROUP):
                    careful(group, head, score(group, head, keys_across), value)
                if last:
                    for part in parts:
                        send(part).start()

    my_block = lax.axis_index("ctx")
    selected = selected_ref[...]
    chosen = scalar_of(selected, 0, 0), scalar_of(selected, 0, 1)
    first = chosen[0] < my_block
    second = jnp.logical_and(chosen[1] < my_block, chosen[1] != chosen[0])
    valid = first.astype(jnp.int32) + second.astype(jnp.int32)

    @pl.when(valid == 2)
    def _():
        attend((0, 1))

    @pl.when(valid == 1)
    def _():
        attend((second.astype(jnp.int32),))

    @pl.when(valid == 0)
    def _():
        @pl.loop(0, KEY_VALUE_HEADS)
        def _(group):
            lanes = wide(group)
            if last:
                staged[:, lanes] = own_ref[:, lanes].astype(staged.dtype)
                for part in range(GROUP // SENT):
                    send(group * (GROUP // SENT) + part).start()
            else:
                fetch(group, 1).wait()
                fetch(group, 0).wait()
                out_ref[:, lanes] = own_ref[:, lanes]
                for head in range(GROUP):
                    new_level_ref[:, head_of(group, head)] = level_of(group, head)

    if last:

        @pl.loop(0, QUERY_HEADS // SENT)
        def _(part):
            send(part).wait()


def far_attention(selected, queries, own, level, far, last):
    rows = queries.shape[0]
    scores = QUERY_HEADS * rows * 2 * sum(piece.shape[2] for piece in far)
    in_vmem = pl.BlockSpec(memory_space=pltpu.VMEM)
    anywhere = pl.BlockSpec(memory_space=pl.ANY)
    if last:
        earlier = in_vmem
        out_shape = jax.ShapeDtypeStruct(queries.shape, jnp.bfloat16)
        out_specs = anywhere
        scratch = [
            pltpu.VMEM(queries.shape, jnp.bfloat16),
            pltpu.SemaphoreType.DMA((QUERY_HEADS // SENT,)),
        ]
    else:
        earlier = anywhere
        own = pltpu.with_memory_space_constraint(own, pltpu.HBM)
        level = pltpu.with_memory_space_constraint(level, pltpu.HBM)
        out_shape = [jax.ShapeDtypeStruct(queries.shape, jnp.float32)] * 2
        out_specs = [in_vmem] * 2
        scratch = [
            pltpu.VMEM(queries.shape, jnp.float32),
            pltpu.VMEM(level.shape, jnp.float32),
            pltpu.SemaphoreType.DMA((2, KEY_VALUE_HEADS)),
        ]
    return pl.pallas_call(
        functools.partial(far_kernel, last=last),
        out_shape=out_shape,
        in_specs=[
            in_vmem,
            in_vmem,
            earlier,
            earlier,
            *[in_vmem] * len(far),
        ],
        out_specs=out_specs,
        scratch_shapes=scratch,
        compiler_params=pltpu.CompilerParams(vmem_limit_bytes=30 * MIB),
        cost_estimate=pl.CostEstimate(
            flops=4 * scores * HEAD_SIZE, bytes_accessed=10 * MIB, transcendentals=scores
        ),
        name="late_attention" if last else "early_attention",
    )(selected, queries, own, level, *far)


def local(queries, all_key_states, all_value_states, selected):
    devices = lax.axis_size("ctx")
    rows = all_key_states.shape[0]
    piece_rows = rows * COPIES // devices
    packed = pack(all_key_states, all_value_states, devices)
    packed, queries = lax.optimization_barrier((packed, queries))
    held = lax.all_to_all(
        packed,
        "ctx",
        split_axis=0,
        concat_axis=0,
        axis_index_groups=[mixed_order(devices)],
        tiled=True,
    )
    own, level = own_attention(queries, all_key_states, all_value_states)
    mine, own, level = lax.optimization_barrier((selected, own, level))
    requests = exchange_requests(mine, devices // COPIES, devices)
    requests = place_of(jnp.clip(requests, 0, devices - 1), devices)
    moved = deliver(pick_pieces(requests, held), devices)
    far = [m.reshape(2, SLOTS, piece_rows, HEAD_SIZE) for m in moved]
    early, late = far[: len(far) // 2], far[len(far) // 2 :]
    if piece_rows % 16 != 0:
        early, late = [jnp.concatenate(early, axis=2)], [jnp.concatenate(late, axis=2)]
    own, level = far_attention(selected, queries, own, level, early, last=False)
    return far_attention(selected, queries, own, level, late, last=True)


def solution(mesh):
    placed = P(("groups", "ctx"), None)
    return jax.shard_map(
        local, mesh=mesh, in_specs=(placed,) * 4, out_specs=placed, check_vma=False
    )
```

```python
import functools
import math

import jax
import jax.numpy as jnp
from jax import lax
from jax.experimental import pallas as pl
from jax.experimental.pallas import tpu as pltpu
from jax.sharding import PartitionSpec as P

QUERY_HEADS = 32
KEY_VALUE_HEADS = 4
HEAD_SIZE = 128
GROUP = QUERY_HEADS // KEY_VALUE_HEADS
SLOTS = 2 * KEY_VALUE_HEADS
COPIES = 2
MIB = 1024 * 1024


def pack_kernel(key_ref, value_ref, out_ref, staged, arrived, left):
    shares, piece_rows, _ = key_ref.shape
    half = KEY_VALUE_HEADS * piece_rows

    def take(slot):
        ref = key_ref if slot < KEY_VALUE_HEADS else value_ref
        head = slot % KEY_VALUE_HEADS
        lanes = pl.ds(head * HEAD_SIZE, HEAD_SIZE)
        rows = pl.ds(slot * piece_rows, piece_rows)
        return pltpu.make_async_copy(
            ref.at[:, :, lanes], staged.at[:, rows, :], arrived.at[slot]
        )

    def give(which, copy):
        rows = pl.ds(which * half, half)
        return pltpu.make_async_copy(
            staged.at[:, rows, :],
            out_ref.at[pl.ds(copy * shares, shares), rows, :],
            left.at[which, copy],
        )

    for slot in range(SLOTS):
        take(slot).start()
    for which in range(2):
        for head in range(KEY_VALUE_HEADS):
            take(which * KEY_VALUE_HEADS + head).wait()
        for copy in range(COPIES):
            give(which, copy).start()
    for which in range(2):
        for copy in range(COPIES):
            give(which, copy).wait()


def pack(keys, values, devices):
    shares = devices // COPIES
    piece_rows = keys.shape[0] // shares
    if piece_rows % 16 == 0:
        split = (shares, piece_rows, keys.shape[1])
        return pl.pallas_call(
            pack_kernel,
            out_shape=jax.ShapeDtypeStruct(
                (devices, SLOTS * piece_rows, HEAD_SIZE), jnp.bfloat16
            ),
            in_specs=[pl.BlockSpec(memory_space=pl.ANY)] * 2,
            out_specs=pl.BlockSpec(memory_space=pl.ANY),
            scratch_shapes=[
                pltpu.VMEM((shares, SLOTS * piece_rows, HEAD_SIZE), jnp.bfloat16),
                pltpu.SemaphoreType.DMA((SLOTS,)),
                pltpu.SemaphoreType.DMA((2, COPIES)),
            ],
            name="pack",
        )(keys.reshape(split), values.reshape(split))
    both = jnp.concatenate([keys, values], axis=1)
    both = both.reshape(shares, piece_rows, SLOTS, HEAD_SIZE).transpose(0, 2, 1, 3)
    both = both.reshape(shares, SLOTS * piece_rows, HEAD_SIZE)
    return jnp.concatenate([both] * COPIES, axis=0)


def partner(position, step):
    return position ^ step


def swap(array, step, devices):
    return lax.ppermute(array, "ctx", [(i, partner(i, step)) for i in range(devices)])


def exchange_requests(selected, shares, devices):
    requests = selected
    step = 1
    while step < shares:
        requests = jnp.concatenate([requests, swap(requests, step, devices)], axis=0)
        step *= 2
    return requests


def scalar_of(values, row, column):
    rows = lax.broadcasted_iota(jnp.int32, values.shape, 0)
    columns = lax.broadcasted_iota(jnp.int32, values.shape, 1)
    here = jnp.logical_and(rows == row, columns == column)
    return jnp.max(jnp.where(here, values.astype(jnp.float32), 0.0)).astype(jnp.int32)


def pick_kernel(requests_ref, held_ref, *out_refs):
    requests = requests_ref[...]
    for step, out_ref in enumerate(out_refs):
        for pick in range(2):
            out_ref[pick] = held_ref[scalar_of(requests, step, pick)]


def pick_pieces(requests, held):
    devices, rows, _ = held.shape
    shares = devices // COPIES
    return pl.pallas_call(
        pick_kernel,
        out_shape=[jax.ShapeDtypeStruct((2, rows, HEAD_SIZE), jnp.bfloat16)] * shares,
        in_specs=[pl.BlockSpec(memory_space=pltpu.VMEM)] * 2,
        out_specs=[pl.BlockSpec(memory_space=pltpu.VMEM)] * shares,
        compiler_params=pltpu.CompilerParams(vmem_limit_bytes=16 * MIB),
        name="pick_pieces",
    )(requests, held)


def delivery_order(shares):
    half, quarter = shares // 2, shares // 4
    apart = zip(range(half, half + quarter), range(quarter, half))
    return [*range(1, quarter), *[s for pair in apart for s in pair], *range(half + quarter, shares)]


def deliver(pieces, devices):
    order = delivery_order(len(pieces))
    return [pieces[0]] + [swap(pieces[step], step, devices) for step in order]


FACTOR = math.log2(math.e) / math.sqrt(HEAD_SIZE)
PAIR = 2
SENT = 4
LARGE_SUM = 2.0**100


def head_lanes(head):
    return slice(head * HEAD_SIZE, (head + 1) * HEAD_SIZE)


def with_ones(value):
    return jnp.concatenate([value, jnp.ones_like(value)], axis=1)


def inverse_of(positive):
    return pl.reciprocal(positive, approx=True)


def dot(a, b):
    return jnp.dot(a, b, preferred_element_type=jnp.float32)


def stack_heads(wide):
    heads = wide.shape[1] // HEAD_SIZE
    return jnp.concatenate([wide[:, head_lanes(h)] for h in range(heads)], axis=0)


def own_kernel(query_ref, key_ref, value_ref, out_ref, level_ref):
    rows = query_ref.shape[0]
    row = lax.broadcasted_iota(jnp.int32, (rows, rows), 0)
    column = lax.broadcasted_iota(jnp.int32, (rows, rows), 1)
    causal = column <= row
    lane = lax.broadcasted_iota(jnp.int32, (rows, HEAD_SIZE), 1)
    keys_across = key_ref[...].T
    value = with_ones(value_ref[...])

    def score(first):
        lanes = slice(first * HEAD_SIZE, (first + PAIR) * HEAD_SIZE)
        return dot(stack_heads(query_ref[:, lanes]), keys_across)

    def finish(first, scores):
        weights, shifts = [], []
        for h in range(PAIR):
            part = jnp.where(causal, scores[h * rows : (h + 1) * rows], -1e30)
            shift = jnp.max(part, axis=1, keepdims=True) * FACTOR
            shifts.append(shift)
            weights.append(jnp.exp2(part * FACTOR - shift).astype(jnp.bfloat16))
        both = dot(jnp.concatenate(weights, axis=0), value)
        for h in range(PAIR):
            part = both[h * rows : (h + 1) * rows]
            row_sum = part[:, HEAD_SIZE:]
            out_ref[:, head_lanes(first + h)] = part[:, :HEAD_SIZE] / row_sum
            level = shifts[h] + jnp.log2(row_sum)
            level_ref[...] = jnp.where(lane == first + h, level, level_ref[...])

    level_ref[...] = jnp.zeros_like(level_ref)
    scores = score(0)
    for first in range(0, GROUP, PAIR):
        following = score(first + PAIR) if first + PAIR < GROUP else None
        finish(first, scores)
        scores = following


def own_attention(queries, keys, values):
    rows = queries.shape[0]
    width = GROUP * HEAD_SIZE
    scores = QUERY_HEADS * rows * rows
    return pl.pallas_call(
        own_kernel,
        out_shape=[
            pltpu.HBM(queries.shape, jnp.float32),
            pltpu.HBM((rows, KEY_VALUE_HEADS * HEAD_SIZE), jnp.float32),
        ],
        grid=(KEY_VALUE_HEADS,),
        in_specs=[
            pl.BlockSpec((rows, width), lambda g: (0, g)),
            pl.BlockSpec((rows, HEAD_SIZE), lambda g: (0, g)),
            pl.BlockSpec((rows, HEAD_SIZE), lambda g: (0, g)),
        ],
        out_specs=[
            pl.BlockSpec((rows, width), lambda g: (0, g)),
            pl.BlockSpec((rows, HEAD_SIZE), lambda g: (0, g)),
        ],
        compiler_params=pltpu.CompilerParams(vmem_limit_bytes=16 * MIB),
        cost_estimate=pl.CostEstimate(
            flops=4 * scores * HEAD_SIZE, bytes_accessed=7 * MIB, transcendentals=scores
        ),
        name="own_attention",
    )(queries, keys, values)


def far_kernel(selected_ref, query_ref, own_in, level_in, *refs, last):
    if last:
        *far_refs, out_ref, staged, sems = refs
        own_ref, level_ref = own_in, level_in
    else:
        *far_refs, out_ref, new_level_ref, own_ref, level_ref, sems = refs
    rows = query_ref.shape[0]
    width = GROUP * HEAD_SIZE

    def wide(group):
        start = group * width
        return pl.ds(start if isinstance(group, int) else pl.multiple_of(start, width), width)

    def narrow(group):
        start = group * HEAD_SIZE
        fixed = isinstance(group, int)
        return pl.ds(start if fixed else pl.multiple_of(start, HEAD_SIZE), HEAD_SIZE)

    def level_of(group, head):
        if last:
            return level_ref[:, head_of(group, head)]
        one = level_ref[:, narrow(group)][:, head : head + 1]
        return jnp.broadcast_to(one, (rows, HEAD_SIZE))

    def fetch(group, which):
        source, target = ((own_in, own_ref), (level_in, level_ref))[which]
        lanes = wide(group) if which == 0 else narrow(group)
        return pltpu.make_async_copy(
            source.at[:, lanes], target.at[:, lanes], sems.at[which, group]
        )

    def send(part):
        start = part * SENT * HEAD_SIZE
        fixed = isinstance(part, int)
        lanes = pl.ds(
            start if fixed else pl.multiple_of(start, SENT * HEAD_SIZE), SENT * HEAD_SIZE
        )
        return pltpu.make_async_copy(staged.at[:, lanes], out_ref.at[:, lanes], sems.at[part])

    if not last:
        for group in range(KEY_VALUE_HEADS):
            fetch(group, 1).start()
            fetch(group, 0).start()

    def head_of(group, head):
        start = (group * GROUP + head) * HEAD_SIZE
        fixed = isinstance(group, int)
        return pl.ds(start if fixed else pl.multiple_of(start, HEAD_SIZE), HEAD_SIZE)

    def store(lanes, mixture, row_sum, level):
        result = mixture * inverse_of(row_sum)
        if last:
            staged[:, lanes] = result.astype(staged.dtype)
        else:
            out_ref[:, lanes] = result
            new_level_ref[:, lanes] = level + jnp.log2(row_sum)

    def attend(picks):
        count = len(picks) * sum(ref.shape[2] for ref in far_refs)

        def block(slot):
            return jnp.concatenate([ref[p, slot] for p in picks for ref in far_refs], axis=0)

        def keys_and_values(group):
            return block(group).T, with_ones(block(group + KEY_VALUE_HEADS))

        def repeat(narrow):
            return jnp.concatenate([narrow] * (count // HEAD_SIZE), axis=1)

        def weigh(group, head, scores):
            level = level_of(group, head)
            return jnp.exp2(scores * FACTOR - repeat(level)).astype(jnp.bfloat16)

        def mix(group, head, weights, value, largest):
            lanes = head_of(group, head)
            both = dot(weights, value)
            row_sum = 1.0 + both[:, HEAD_SIZE:]
            mixture = own_ref[:, lanes] + both[:, :HEAD_SIZE]
            store(lanes, mixture, row_sum, level_of(group, head))
            return jnp.maximum(
                largest, jnp.max(row_sum.reshape(rows // 8, 8, HEAD_SIZE), axis=0)
            )

        def careful(group, head, scores, value):
            lanes = head_of(group, head)
            part = scores * FACTOR
            level = level_of(group, head)
            shift = jnp.maximum(jnp.max(part, axis=1, keepdims=True), level)
            weights = jnp.exp2(part - repeat(shift)).astype(jnp.bfloat16)
            both = dot(weights, value)
            share = jnp.exp2(level - shift)
            mixture = own_ref[:, lanes] * share + both[:, :HEAD_SIZE]
            store(lanes, mixture, share + both[:, HEAD_SIZE:], shift)

        def score(group, head, keys_across):
            return dot(query_ref[:, head_of(group, head)], keys_across)

        largest = jnp.zeros((8, HEAD_SIZE), jnp.float32)
        order = [(g, h) for g in range(KEY_VALUE_HEADS) for h in range(GROUP)]
        held, scores, weights = {}, {}, {}
        for turn in range(len(order) + 2):
            if turn < len(order):
                group, head = order[turn]
                if group not in held:
                    held[group] = keys_and_values(group)
                scores[turn] = score(group, head, held[group][0])
            if 1 <= turn <= len(order):
                group, head = order[turn - 1]
                if head == 0 and not last:
                    fetch(group, 1).wait()
                    fetch(group, 0).wait()
                weights[turn - 1] = weigh(group, head, scores.pop(turn - 1))
            if turn >= 2:
                group, head = order[turn - 2]
                largest = mix(group, head, weights.pop(turn - 2), held[group][1], largest)
                if (head + 1) % SENT == 0 and last:
                    send((group * GROUP + head) // SENT).start()

        @pl.when(jnp.max(largest) > LARGE_SUM)
        def _():
            @pl.loop(0, KEY_VALUE_HEADS)
            def _(group):
                parts = [group * (GROUP // SENT) + part for part in range(GROUP // SENT)]
                if last:
                    for part in parts:
                        send(part).wait()
                keys_across, value = keys_and_values(group)
                for head in range(GROUP):
                    careful(group, head, score(group, head, keys_across), value)
                if last:
                    for part in parts:
                        send(part).start()

    my_block = lax.axis_index("ctx")
    selected = selected_ref[...]
    chosen = scalar_of(selected, 0, 0), scalar_of(selected, 0, 1)
    first = chosen[0] < my_block
    second = jnp.logical_and(chosen[1] < my_block, chosen[1] != chosen[0])
    valid = first.astype(jnp.int32) + second.astype(jnp.int32)

    @pl.when(valid == 2)
    def _():
        attend((0, 1))

    @pl.when(valid == 1)
    def _():
        attend((second.astype(jnp.int32),))

    @pl.when(valid == 0)
    def _():
        @pl.loop(0, KEY_VALUE_HEADS)
        def _(group):
            lanes = wide(group)
            if last:
                staged[:, lanes] = own_ref[:, lanes].astype(staged.dtype)
                for part in range(GROUP // SENT):
                    send(group * (GROUP // SENT) + part).start()
            else:
                fetch(group, 1).wait()
                fetch(group, 0).wait()
                out_ref[:, lanes] = own_ref[:, lanes]
                for head in range(GROUP):
                    new_level_ref[:, head_of(group, head)] = level_of(group, head)

    if last:

        @pl.loop(0, QUERY_HEADS // SENT)
        def _(part):
            send(part).wait()


def far_attention(selected, queries, own, level, far, last):
    rows = queries.shape[0]
    scores = QUERY_HEADS * rows * 2 * sum(piece.shape[2] for piece in far)
    in_vmem = pl.BlockSpec(memory_space=pltpu.VMEM)
    anywhere = pl.BlockSpec(memory_space=pl.ANY)
    if last:
        earlier = in_vmem
        out_shape = jax.ShapeDtypeStruct(queries.shape, jnp.bfloat16)
        out_specs = anywhere
        scratch = [
            pltpu.VMEM(queries.shape, jnp.bfloat16),
            pltpu.SemaphoreType.DMA((QUERY_HEADS // SENT,)),
        ]
    else:
        earlier = anywhere
        own = pltpu.with_memory_space_constraint(own, pltpu.HBM)
        level = pltpu.with_memory_space_constraint(level, pltpu.HBM)
        out_shape = [jax.ShapeDtypeStruct(queries.shape, jnp.float32)] * 2
        out_specs = [in_vmem] * 2
        scratch = [
            pltpu.VMEM(queries.shape, jnp.float32),
            pltpu.VMEM(level.shape, jnp.float32),
            pltpu.SemaphoreType.DMA((2, KEY_VALUE_HEADS)),
        ]
    return pl.pallas_call(
        functools.partial(far_kernel, last=last),
        out_shape=out_shape,
        in_specs=[
            in_vmem,
            in_vmem,
            earlier,
            earlier,
            *[in_vmem] * len(far),
        ],
        out_specs=out_specs,
        scratch_shapes=scratch,
        compiler_params=pltpu.CompilerParams(vmem_limit_bytes=30 * MIB),
        cost_estimate=pl.CostEstimate(
            flops=4 * scores * HEAD_SIZE, bytes_accessed=10 * MIB, transcendentals=scores
        ),
        name="late_attention" if last else "early_attention",
    )(selected, queries, own, level, *far)


def local(queries, all_key_states, all_value_states, selected):
    devices = lax.axis_size("ctx")
    rows = all_key_states.shape[0]
    piece_rows = rows * COPIES // devices
    packed = pack(all_key_states, all_value_states, devices)
    packed, queries = lax.optimization_barrier((packed, queries))
    held = lax.all_to_all(packed, "ctx", split_axis=0, concat_axis=0, tiled=True)
    own, level = own_attention(queries, all_key_states, all_value_states)
    mine, own, level = lax.optimization_barrier((selected, own, level))
    requests = exchange_requests(mine, devices // COPIES, devices)
    requests = jnp.clip(requests, 0, devices - 1)
    moved = deliver(pick_pieces(requests, held), devices)
    far = [m.reshape(2, SLOTS, piece_rows, HEAD_SIZE) for m in moved]
    early, late = far[: len(far) // 2], far[len(far) // 2 :]
    if piece_rows % 16 != 0:
        early, late = [jnp.concatenate(early, axis=2)], [jnp.concatenate(late, axis=2)]
    own, level = far_attention(selected, queries, own, level, early, last=False)
    return far_attention(selected, queries, own, level, late, last=True)


def solution(mesh):
    placed = P(("groups", "ctx"), None)
    return jax.shard_map(
        local, mesh=mesh, in_specs=(placed,) * 4, out_specs=placed, check_vma=False
    )
```

```python
import functools
import math

import jax
import jax.numpy as jnp
from jax import lax
from jax.experimental import pallas as pl
from jax.experimental.pallas import tpu as pltpu
from jax.sharding import PartitionSpec as P

QUERY_HEADS = 32
KEY_VALUE_HEADS = 4
HEAD_SIZE = 128
GROUP = QUERY_HEADS // KEY_VALUE_HEADS
SLOTS = 2 * KEY_VALUE_HEADS
COPIES = 2
MIB = 1024 * 1024


def pack_kernel(key_ref, value_ref, out_ref, staged, arrived, left):
    shares, piece_rows, _ = key_ref.shape
    half = KEY_VALUE_HEADS * piece_rows

    def take(slot):
        ref = key_ref if slot < KEY_VALUE_HEADS else value_ref
        head = slot % KEY_VALUE_HEADS
        lanes = pl.ds(head * HEAD_SIZE, HEAD_SIZE)
        rows = pl.ds(slot * piece_rows, piece_rows)
        return pltpu.make_async_copy(
            ref.at[:, :, lanes], staged.at[:, rows, :], arrived.at[slot]
        )

    def give(which, copy):
        rows = pl.ds(which * half, half)
        return pltpu.make_async_copy(
            staged.at[:, rows, :],
            out_ref.at[pl.ds(copy * shares, shares), rows, :],
            left.at[which, copy],
        )

    for slot in range(SLOTS):
        take(slot).start()
    for which in range(2):
        for head in range(KEY_VALUE_HEADS):
            take(which * KEY_VALUE_HEADS + head).wait()
        for copy in range(COPIES):
            give(which, copy).start()
    for which in range(2):
        for copy in range(COPIES):
            give(which, copy).wait()


def pack(keys, values, devices):
    shares = devices // COPIES
    piece_rows = keys.shape[0] // shares
    if piece_rows % 16 == 0:
        split = (shares, piece_rows, keys.shape[1])
        return pl.pallas_call(
            pack_kernel,
            out_shape=jax.ShapeDtypeStruct(
                (devices, SLOTS * piece_rows, HEAD_SIZE), jnp.bfloat16
            ),
            in_specs=[pl.BlockSpec(memory_space=pl.ANY)] * 2,
            out_specs=pl.BlockSpec(memory_space=pl.ANY),
            scratch_shapes=[
                pltpu.VMEM((shares, SLOTS * piece_rows, HEAD_SIZE), jnp.bfloat16),
                pltpu.SemaphoreType.DMA((SLOTS,)),
                pltpu.SemaphoreType.DMA((2, COPIES)),
            ],
            name="pack",
        )(keys.reshape(split), values.reshape(split))
    both = jnp.concatenate([keys, values], axis=1)
    both = both.reshape(shares, piece_rows, SLOTS, HEAD_SIZE).transpose(0, 2, 1, 3)
    both = both.reshape(shares, SLOTS * piece_rows, HEAD_SIZE)
    return jnp.concatenate([both] * COPIES, axis=0)


def partner(position, step):
    return position ^ step


def swap(array, step, devices):
    return lax.ppermute(array, "ctx", [(i, partner(i, step)) for i in range(devices)])


def exchange_requests(selected, shares, devices):
    requests = selected
    step = 1
    while step < shares:
        requests = jnp.concatenate([requests, swap(requests, step, devices)], axis=0)
        step *= 2
    return requests


def scalar_of(values, row, column):
    rows = lax.broadcasted_iota(jnp.int32, values.shape, 0)
    columns = lax.broadcasted_iota(jnp.int32, values.shape, 1)
    here = jnp.logical_and(rows == row, columns == column)
    return jnp.max(jnp.where(here, values.astype(jnp.float32), 0.0)).astype(jnp.int32)


def pick_kernel(requests_ref, held_ref, *out_refs):
    requests = requests_ref[...]
    for step, out_ref in enumerate(out_refs):
        for pick in range(2):
            out_ref[pick] = held_ref[scalar_of(requests, step, pick)]


def pick_pieces(requests, held):
    devices, rows, _ = held.shape
    shares = devices // COPIES
    return pl.pallas_call(
        pick_kernel,
        out_shape=[jax.ShapeDtypeStruct((2, rows, HEAD_SIZE), jnp.bfloat16)] * shares,
        in_specs=[pl.BlockSpec(memory_space=pltpu.VMEM)] * 2,
        out_specs=[pl.BlockSpec(memory_space=pltpu.VMEM)] * shares,
        compiler_params=pltpu.CompilerParams(vmem_limit_bytes=16 * MIB),
        name="pick_pieces",
    )(requests, held)


def delivery_order(shares):
    half, quarter = shares // 2, shares // 4
    apart = zip(range(half, half + quarter), range(quarter, half))
    return [*range(1, quarter), *[s for pair in apart for s in pair], *range(half + quarter, shares)]


def deliver(pieces, devices):
    order = delivery_order(len(pieces))
    return [pieces[0]] + [swap(pieces[step], step, devices) for step in order]


FACTOR = math.log2(math.e) / math.sqrt(HEAD_SIZE)
PAIR = 2
SENT = 2
LARGE_SUM = 2.0**100


def head_lanes(head):
    return slice(head * HEAD_SIZE, (head + 1) * HEAD_SIZE)


def with_ones(value):
    return jnp.concatenate([value, jnp.ones_like(value)], axis=1)


def inverse_of(positive):
    return pl.reciprocal(positive, approx=True)


def dot(a, b):
    return jnp.dot(a, b, preferred_element_type=jnp.float32)


def stack_heads(wide):
    heads = wide.shape[1] // HEAD_SIZE
    return jnp.concatenate([wide[:, head_lanes(h)] for h in range(heads)], axis=0)


def own_kernel(query_ref, key_ref, value_ref, out_ref, level_ref):
    rows = query_ref.shape[0]
    row = lax.broadcasted_iota(jnp.int32, (rows, rows), 0)
    column = lax.broadcasted_iota(jnp.int32, (rows, rows), 1)
    causal = column <= row
    lane = lax.broadcasted_iota(jnp.int32, (rows, HEAD_SIZE), 1)
    keys_across = key_ref[...].T
    value = with_ones(value_ref[...])

    def score(first):
        lanes = slice(first * HEAD_SIZE, (first + PAIR) * HEAD_SIZE)
        return dot(stack_heads(query_ref[:, lanes]), keys_across)

    def finish(first, scores):
        weights, shifts = [], []
        for h in range(PAIR):
            part = jnp.where(causal, scores[h * rows : (h + 1) * rows], -1e30)
            shift = jnp.max(part, axis=1, keepdims=True) * FACTOR
            shifts.append(shift)
            weights.append(jnp.exp2(part * FACTOR - shift).astype(jnp.bfloat16))
        both = dot(jnp.concatenate(weights, axis=0), value)
        for h in range(PAIR):
            part = both[h * rows : (h + 1) * rows]
            row_sum = part[:, HEAD_SIZE:]
            out_ref[:, head_lanes(first + h)] = part[:, :HEAD_SIZE] / row_sum
            level = shifts[h] + jnp.log2(row_sum)
            level_ref[...] = jnp.where(lane == first + h, level, level_ref[...])

    level_ref[...] = jnp.zeros_like(level_ref)
    scores = score(0)
    for first in range(0, GROUP, PAIR):
        following = score(first + PAIR) if first + PAIR < GROUP else None
        finish(first, scores)
        scores = following


def own_attention(queries, keys, values):
    rows = queries.shape[0]
    width = GROUP * HEAD_SIZE
    scores = QUERY_HEADS * rows * rows
    return pl.pallas_call(
        own_kernel,
        out_shape=[
            pltpu.HBM(queries.shape, jnp.float32),
            pltpu.HBM((rows, KEY_VALUE_HEADS * HEAD_SIZE), jnp.float32),
        ],
        grid=(KEY_VALUE_HEADS,),
        in_specs=[
            pl.BlockSpec((rows, width), lambda g: (0, g)),
            pl.BlockSpec((rows, HEAD_SIZE), lambda g: (0, g)),
            pl.BlockSpec((rows, HEAD_SIZE), lambda g: (0, g)),
        ],
        out_specs=[
            pl.BlockSpec((rows, width), lambda g: (0, g)),
            pl.BlockSpec((rows, HEAD_SIZE), lambda g: (0, g)),
        ],
        compiler_params=pltpu.CompilerParams(vmem_limit_bytes=16 * MIB),
        cost_estimate=pl.CostEstimate(
            flops=4 * scores * HEAD_SIZE, bytes_accessed=7 * MIB, transcendentals=scores
        ),
        name="own_attention",
    )(queries, keys, values)


def far_kernel(selected_ref, query_ref, own_in, level_in, *refs, last):
    if last:
        *far_refs, out_ref, staged, sems = refs
        own_ref, level_ref = own_in, level_in
    else:
        *far_refs, out_ref, new_level_ref, own_ref, level_ref, sems = refs
    rows = query_ref.shape[0]
    width = GROUP * HEAD_SIZE

    def wide(group):
        start = group * width
        return pl.ds(start if isinstance(group, int) else pl.multiple_of(start, width), width)

    def narrow(group):
        start = group * HEAD_SIZE
        fixed = isinstance(group, int)
        return pl.ds(start if fixed else pl.multiple_of(start, HEAD_SIZE), HEAD_SIZE)

    def level_of(group, head):
        if last:
            return level_ref[:, head_of(group, head)]
        one = level_ref[:, narrow(group)][:, head : head + 1]
        return jnp.broadcast_to(one, (rows, HEAD_SIZE))

    def fetch(group, which):
        source, target = ((own_in, own_ref), (level_in, level_ref))[which]
        lanes = wide(group) if which == 0 else narrow(group)
        return pltpu.make_async_copy(
            source.at[:, lanes], target.at[:, lanes], sems.at[which, group]
        )

    def send(part):
        start = part * SENT * HEAD_SIZE
        fixed = isinstance(part, int)
        lanes = pl.ds(
            start if fixed else pl.multiple_of(start, SENT * HEAD_SIZE), SENT * HEAD_SIZE
        )
        return pltpu.make_async_copy(staged.at[:, lanes], out_ref.at[:, lanes], sems.at[part])

    if not last:
        for group in range(KEY_VALUE_HEADS):
            fetch(group, 1).start()
            fetch(group, 0).start()

    def head_of(group, head):
        start = (group * GROUP + head) * HEAD_SIZE
        fixed = isinstance(group, int)
        return pl.ds(start if fixed else pl.multiple_of(start, HEAD_SIZE), HEAD_SIZE)

    def store(lanes, mixture, row_sum, level):
        result = mixture * inverse_of(row_sum)
        if last:
            staged[:, lanes] = result.astype(staged.dtype)
        else:
            out_ref[:, lanes] = result
            new_level_ref[:, lanes] = level + jnp.log2(row_sum)

    def attend(picks):
        count = len(picks) * sum(ref.shape[2] for ref in far_refs)

        def block(slot):
            return jnp.concatenate([ref[p, slot] for p in picks for ref in far_refs], axis=0)

        def keys_and_values(group):
            return block(group).T, with_ones(block(group + KEY_VALUE_HEADS))

        def repeat(narrow):
            return jnp.concatenate([narrow] * (count // HEAD_SIZE), axis=1)

        def weigh(group, head, scores):
            level = level_of(group, head)
            return jnp.exp2(scores * FACTOR - repeat(level)).astype(jnp.bfloat16)

        def mix(group, head, weights, value, largest):
            lanes = head_of(group, head)
            both = dot(weights, value)
            row_sum = 1.0 + both[:, HEAD_SIZE:]
            mixture = own_ref[:, lanes] + both[:, :HEAD_SIZE]
            store(lanes, mixture, row_sum, level_of(group, head))
            return jnp.maximum(
                largest, jnp.max(row_sum.reshape(rows // 8, 8, HEAD_SIZE), axis=0)
            )

        def careful(group, head, scores, value):
            lanes = head_of(group, head)
            part = scores * FACTOR
            level = level_of(group, head)
            shift = jnp.maximum(jnp.max(part, axis=1, keepdims=True), level)
            weights = jnp.exp2(part - repeat(shift)).astype(jnp.bfloat16)
            both = dot(weights, value)
            share = jnp.exp2(level - shift)
            mixture = own_ref[:, lanes] * share + both[:, :HEAD_SIZE]
            store(lanes, mixture, share + both[:, HEAD_SIZE:], shift)

        def score(group, head, keys_across):
            return dot(query_ref[:, head_of(group, head)], keys_across)

        largest = jnp.zeros((8, HEAD_SIZE), jnp.float32)
        order = [(g, h) for g in range(KEY_VALUE_HEADS) for h in range(GROUP)]
        held, scores, weights = {}, {}, {}
        for turn in range(len(order) + 2):
            if turn < len(order):
                group, head = order[turn]
                soon = order[min(turn + GROUP // 2, len(order) - 1)][0]
                for needed in (group, soon):
                    if needed not in held:
                        held[needed] = keys_and_values(needed)
                scores[turn] = score(group, head, held[group][0])
            if 1 <= turn <= len(order):
                group, head = order[turn - 1]
                if head == 0 and not last:
                    fetch(group, 1).wait()
                    fetch(group, 0).wait()
                weights[turn - 1] = weigh(group, head, scores.pop(turn - 1))
            if turn >= 2:
                group, head = order[turn - 2]
                largest = mix(group, head, weights.pop(turn - 2), held[group][1], largest)
                if (head + 1) % SENT == 0 and last:
                    send((group * GROUP + head) // SENT).start()

        @pl.when(jnp.max(largest) > LARGE_SUM)
        def _():
            @pl.loop(0, KEY_VALUE_HEADS)
            def _(group):
                parts = [group * (GROUP // SENT) + part for part in range(GROUP // SENT)]
                if last:
                    for part in parts:
                        send(part).wait()
                keys_across, value = keys_and_values(group)
                for head in range(GROUP):
                    careful(group, head, score(group, head, keys_across), value)
                if last:
                    for part in parts:
                        send(part).start()

    my_block = lax.axis_index("ctx")
    selected = selected_ref[...]
    chosen = scalar_of(selected, 0, 0), scalar_of(selected, 0, 1)
    first = chosen[0] < my_block
    second = jnp.logical_and(chosen[1] < my_block, chosen[1] != chosen[0])
    valid = first.astype(jnp.int32) + second.astype(jnp.int32)

    @pl.when(valid == 2)
    def _():
        attend((0, 1))

    @pl.when(valid == 1)
    def _():
        attend((second.astype(jnp.int32),))

    @pl.when(valid == 0)
    def _():
        @pl.loop(0, KEY_VALUE_HEADS)
        def _(group):
            lanes = wide(group)
            if last:
                staged[:, lanes] = own_ref[:, lanes].astype(staged.dtype)
                for part in range(GROUP // SENT):
                    send(group * (GROUP // SENT) + part).start()
            else:
                fetch(group, 1).wait()
                fetch(group, 0).wait()
                out_ref[:, lanes] = own_ref[:, lanes]
                for head in range(GROUP):
                    new_level_ref[:, head_of(group, head)] = level_of(group, head)

    if last:

        @pl.loop(0, QUERY_HEADS // SENT)
        def _(part):
            send(part).wait()


def far_attention(selected, queries, own, level, far, last):
    rows = queries.shape[0]
    scores = QUERY_HEADS * rows * 2 * sum(piece.shape[2] for piece in far)
    in_vmem = pl.BlockSpec(memory_space=pltpu.VMEM)
    anywhere = pl.BlockSpec(memory_space=pl.ANY)
    if last:
        earlier = in_vmem
        out_shape = jax.ShapeDtypeStruct(queries.shape, jnp.bfloat16)
        out_specs = anywhere
        scratch = [
            pltpu.VMEM(queries.shape, jnp.bfloat16),
            pltpu.SemaphoreType.DMA((QUERY_HEADS // SENT,)),
        ]
    else:
        earlier = anywhere
        own = pltpu.with_memory_space_constraint(own, pltpu.HBM)
        level = pltpu.with_memory_space_constraint(level, pltpu.HBM)
        out_shape = [jax.ShapeDtypeStruct(queries.shape, jnp.float32)] * 2
        out_specs = [in_vmem] * 2
        scratch = [
            pltpu.VMEM(queries.shape, jnp.float32),
            pltpu.VMEM(level.shape, jnp.float32),
            pltpu.SemaphoreType.DMA((2, KEY_VALUE_HEADS)),
        ]
    return pl.pallas_call(
        functools.partial(far_kernel, last=last),
        out_shape=out_shape,
        in_specs=[
            in_vmem,
            in_vmem,
            earlier,
            earlier,
            *[in_vmem] * len(far),
        ],
        out_specs=out_specs,
        scratch_shapes=scratch,
        compiler_params=pltpu.CompilerParams(vmem_limit_bytes=30 * MIB),
        cost_estimate=pl.CostEstimate(
            flops=4 * scores * HEAD_SIZE, bytes_accessed=10 * MIB, transcendentals=scores
        ),
        name="late_attention" if last else "early_attention",
    )(selected, queries, own, level, *far)


def local(queries, all_key_states, all_value_states, selected):
    devices = lax.axis_size("ctx")
    rows = all_key_states.shape[0]
    piece_rows = rows * COPIES // devices
    packed = pack(all_key_states, all_value_states, devices)
    packed, queries = lax.optimization_barrier((packed, queries))
    held = lax.all_to_all(packed, "ctx", split_axis=0, concat_axis=0, tiled=True)
    own, level = own_attention(queries, all_key_states, all_value_states)
    mine, own, level = lax.optimization_barrier((selected, own, level))
    requests = exchange_requests(mine, devices // COPIES, devices)
    requests = jnp.clip(requests, 0, devices - 1)
    moved = deliver(pick_pieces(requests, held), devices)
    far = [m.reshape(2, SLOTS, piece_rows, HEAD_SIZE) for m in moved]
    early, late = far[: len(far) // 2], far[len(far) // 2 :]
    if piece_rows % 16 != 0:
        early, late = [jnp.concatenate(early, axis=2)], [jnp.concatenate(late, axis=2)]
    own, level = far_attention(selected, queries, own, level, early, last=False)
    return far_attention(selected, queries, own, level, late, last=True)


def solution(mesh):
    placed = P(("groups", "ctx"), None)
    return jax.shard_map(
        local, mesh=mesh, in_specs=(placed,) * 4, out_specs=placed, check_vma=False
    )
```

```python
import functools
import math

import jax
import jax.numpy as jnp
from jax import lax
from jax.experimental import pallas as pl
from jax.experimental.pallas import tpu as pltpu
from jax.sharding import PartitionSpec as P

QUERY_HEADS = 32
KEY_VALUE_HEADS = 4
HEAD_SIZE = 128
GROUP = QUERY_HEADS // KEY_VALUE_HEADS
SLOTS = 2 * KEY_VALUE_HEADS
COPIES = 2
MIB = 1024 * 1024


def pack_kernel(key_ref, value_ref, out_ref, staged, arrived, left):
    shares, piece_rows, _ = key_ref.shape

    def take(slot):
        ref = key_ref if slot < KEY_VALUE_HEADS else value_ref
        head = slot % KEY_VALUE_HEADS
        lanes = pl.ds(head * HEAD_SIZE, HEAD_SIZE)
        rows = pl.ds(slot * piece_rows, piece_rows)
        return pltpu.make_async_copy(
            ref.at[:, :, lanes], staged.at[:, rows, :], arrived.at[slot]
        )

    def give(which, copy):
        rows = pl.ds(which * piece_rows, piece_rows)
        return pltpu.make_async_copy(
            staged.at[:, rows, :],
            out_ref.at[pl.ds(copy * shares, shares), rows, :],
            left.at[which, copy],
        )

    for slot in range(SLOTS):
        take(slot).start()
    for slot in range(SLOTS):
        take(slot).wait()
        for copy in range(COPIES):
            give(slot, copy).start()
    for which in range(SLOTS):
        for copy in range(COPIES):
            give(which, copy).wait()


def pack(keys, values, devices):
    shares = devices // COPIES
    piece_rows = keys.shape[0] // shares
    if piece_rows % 16 == 0:
        split = (shares, piece_rows, keys.shape[1])
        return pl.pallas_call(
            pack_kernel,
            out_shape=jax.ShapeDtypeStruct(
                (devices, SLOTS * piece_rows, HEAD_SIZE), jnp.bfloat16
            ),
            in_specs=[pl.BlockSpec(memory_space=pl.ANY)] * 2,
            out_specs=pl.BlockSpec(memory_space=pl.ANY),
            scratch_shapes=[
                pltpu.VMEM((shares, SLOTS * piece_rows, HEAD_SIZE), jnp.bfloat16),
                pltpu.SemaphoreType.DMA((SLOTS,)),
                pltpu.SemaphoreType.DMA((SLOTS, COPIES)),
            ],
            name="pack",
        )(keys.reshape(split), values.reshape(split))
    both = jnp.concatenate([keys, values], axis=1)
    both = both.reshape(shares, piece_rows, SLOTS, HEAD_SIZE).transpose(0, 2, 1, 3)
    both = both.reshape(shares, SLOTS * piece_rows, HEAD_SIZE)
    return jnp.concatenate([both] * COPIES, axis=0)


def partner(position, step):
    return position ^ step


def swap(array, step, devices):
    return lax.ppermute(array, "ctx", [(i, partner(i, step)) for i in range(devices)])


def exchange_requests(selected, shares, devices):
    requests = selected
    step = 1
    while step < shares:
        requests = jnp.concatenate([requests, swap(requests, step, devices)], axis=0)
        step *= 2
    return requests


def scalar_of(values, row, column):
    rows = lax.broadcasted_iota(jnp.int32, values.shape, 0)
    columns = lax.broadcasted_iota(jnp.int32, values.shape, 1)
    here = jnp.logical_and(rows == row, columns == column)
    return jnp.max(jnp.where(here, values.astype(jnp.float32), 0.0)).astype(jnp.int32)


def pick_kernel(requests_ref, held_ref, *out_refs):
    requests = requests_ref[...]
    for step, out_ref in enumerate(out_refs):
        for pick in range(2):
            out_ref[pick] = held_ref[scalar_of(requests, step, pick)]


def pick_pieces(requests, held):
    devices, rows, _ = held.shape
    shares = devices // COPIES
    return pl.pallas_call(
        pick_kernel,
        out_shape=[jax.ShapeDtypeStruct((2, rows, HEAD_SIZE), jnp.bfloat16)] * shares,
        in_specs=[pl.BlockSpec(memory_space=pltpu.VMEM)] * 2,
        out_specs=[pl.BlockSpec(memory_space=pltpu.VMEM)] * shares,
        compiler_params=pltpu.CompilerParams(vmem_limit_bytes=16 * MIB),
        name="pick_pieces",
    )(requests, held)


def delivery_order(shares):
    half, quarter = shares // 2, shares // 4
    apart = zip(range(half, half + quarter), range(quarter, half))
    return [*range(1, quarter), *[s for pair in apart for s in pair], *range(half + quarter, shares)]


def deliver(pieces, devices):
    order = delivery_order(len(pieces))
    return [pieces[0]] + [swap(pieces[step], step, devices) for step in order]


FACTOR = math.log2(math.e) / math.sqrt(HEAD_SIZE)
PAIR = 2
SENT = 2
LARGE_SUM = 2.0**100


def head_lanes(head):
    return slice(head * HEAD_SIZE, (head + 1) * HEAD_SIZE)


def with_ones(value):
    return jnp.concatenate([value, jnp.ones_like(value)], axis=1)


def inverse_of(positive):
    return pl.reciprocal(positive, approx=True)


def dot(a, b):
    return jnp.dot(a, b, preferred_element_type=jnp.float32)


def stack_heads(wide):
    heads = wide.shape[1] // HEAD_SIZE
    return jnp.concatenate([wide[:, head_lanes(h)] for h in range(heads)], axis=0)


def own_kernel(query_ref, key_ref, value_ref, out_ref, level_ref):
    rows = query_ref.shape[0]
    row = lax.broadcasted_iota(jnp.int32, (rows, rows), 0)
    column = lax.broadcasted_iota(jnp.int32, (rows, rows), 1)
    causal = column <= row
    lane = lax.broadcasted_iota(jnp.int32, (rows, HEAD_SIZE), 1)
    keys_across = key_ref[...].T
    value = with_ones(value_ref[...])

    def score(first):
        lanes = slice(first * HEAD_SIZE, (first + PAIR) * HEAD_SIZE)
        return dot(stack_heads(query_ref[:, lanes]), keys_across)

    def finish(first, scores):
        weights, shifts = [], []
        for h in range(PAIR):
            part = jnp.where(causal, scores[h * rows : (h + 1) * rows], -1e30)
            shift = jnp.max(part, axis=1, keepdims=True) * FACTOR
            shifts.append(shift)
            weights.append(jnp.exp2(part * FACTOR - shift).astype(jnp.bfloat16))
        both = dot(jnp.concatenate(weights, axis=0), value)
        for h in range(PAIR):
            part = both[h * rows : (h + 1) * rows]
            row_sum = part[:, HEAD_SIZE:]
            out_ref[:, head_lanes(first + h)] = part[:, :HEAD_SIZE] / row_sum
            level = shifts[h] + jnp.log2(row_sum)
            level_ref[...] = jnp.where(lane == first + h, level, level_ref[...])

    level_ref[...] = jnp.zeros_like(level_ref)
    scores = score(0)
    for first in range(0, GROUP, PAIR):
        following = score(first + PAIR) if first + PAIR < GROUP else None
        finish(first, scores)
        scores = following


def own_attention(queries, keys, values):
    rows = queries.shape[0]
    width = GROUP * HEAD_SIZE
    scores = QUERY_HEADS * rows * rows
    return pl.pallas_call(
        own_kernel,
        out_shape=[
            pltpu.HBM(queries.shape, jnp.float32),
            pltpu.HBM((rows, KEY_VALUE_HEADS * HEAD_SIZE), jnp.float32),
        ],
        grid=(KEY_VALUE_HEADS,),
        in_specs=[
            pl.BlockSpec((rows, width), lambda g: (0, g)),
            pl.BlockSpec((rows, HEAD_SIZE), lambda g: (0, g)),
            pl.BlockSpec((rows, HEAD_SIZE), lambda g: (0, g)),
        ],
        out_specs=[
            pl.BlockSpec((rows, width), lambda g: (0, g)),
            pl.BlockSpec((rows, HEAD_SIZE), lambda g: (0, g)),
        ],
        compiler_params=pltpu.CompilerParams(vmem_limit_bytes=16 * MIB),
        cost_estimate=pl.CostEstimate(
            flops=4 * scores * HEAD_SIZE, bytes_accessed=7 * MIB, transcendentals=scores
        ),
        name="own_attention",
    )(queries, keys, values)


def far_kernel(selected_ref, query_ref, own_in, level_in, *refs, last):
    if last:
        *far_refs, out_ref, staged, sems = refs
        own_ref, level_ref = own_in, level_in
    else:
        *far_refs, out_ref, new_level_ref, own_ref, level_ref, sems = refs
    rows = query_ref.shape[0]
    width = GROUP * HEAD_SIZE

    def wide(group):
        start = group * width
        return pl.ds(start if isinstance(group, int) else pl.multiple_of(start, width), width)

    def narrow(group):
        start = group * HEAD_SIZE
        fixed = isinstance(group, int)
        return pl.ds(start if fixed else pl.multiple_of(start, HEAD_SIZE), HEAD_SIZE)

    def level_of(group, head):
        if last:
            return level_ref[:, head_of(group, head)]
        one = level_ref[:, narrow(group)][:, head : head + 1]
        return jnp.broadcast_to(one, (rows, HEAD_SIZE))

    def fetch(group, which):
        source, target = ((own_in, own_ref), (level_in, level_ref))[which]
        lanes = wide(group) if which == 0 else narrow(group)
        return pltpu.make_async_copy(
            source.at[:, lanes], target.at[:, lanes], sems.at[which, group]
        )

    def send(part):
        start = part * SENT * HEAD_SIZE
        fixed = isinstance(part, int)
        lanes = pl.ds(
            start if fixed else pl.multiple_of(start, SENT * HEAD_SIZE), SENT * HEAD_SIZE
        )
        return pltpu.make_async_copy(staged.at[:, lanes], out_ref.at[:, lanes], sems.at[part])

    if not last:
        for group in range(KEY_VALUE_HEADS):
            fetch(group, 1).start()
            fetch(group, 0).start()

    def head_of(group, head):
        start = (group * GROUP + head) * HEAD_SIZE
        fixed = isinstance(group, int)
        return pl.ds(start if fixed else pl.multiple_of(start, HEAD_SIZE), HEAD_SIZE)

    def store(lanes, mixture, row_sum, level):
        result = mixture * inverse_of(row_sum)
        if last:
            staged[:, lanes] = result.astype(staged.dtype)
        else:
            out_ref[:, lanes] = result
            new_level_ref[:, lanes] = level + jnp.log2(row_sum)

    def attend(picks):
        count = len(picks) * sum(ref.shape[2] for ref in far_refs)

        def block(slot):
            return jnp.concatenate([ref[p, slot] for p in picks for ref in far_refs], axis=0)

        def keys_and_values(group):
            return block(group).T, with_ones(block(group + KEY_VALUE_HEADS))

        def repeat(narrow):
            return jnp.concatenate([narrow] * (count // HEAD_SIZE), axis=1)

        def weigh(group, head, scores):
            level = level_of(group, head)
            return jnp.exp2(scores * FACTOR - repeat(level)).astype(jnp.bfloat16)

        def mix(group, head, weights, value, largest):
            lanes = head_of(group, head)
            both = dot(weights, value)
            row_sum = 1.0 + both[:, HEAD_SIZE:]
            mixture = own_ref[:, lanes] + both[:, :HEAD_SIZE]
            store(lanes, mixture, row_sum, level_of(group, head))
            return jnp.maximum(
                largest, jnp.max(row_sum.reshape(rows // 8, 8, HEAD_SIZE), axis=0)
            )

        def careful(group, head, scores, value):
            lanes = head_of(group, head)
            part = scores * FACTOR
            level = level_of(group, head)
            shift = jnp.maximum(jnp.max(part, axis=1, keepdims=True), level)
            weights = jnp.exp2(part - repeat(shift)).astype(jnp.bfloat16)
            both = dot(weights, value)
            share = jnp.exp2(level - shift)
            mixture = own_ref[:, lanes] * share + both[:, :HEAD_SIZE]
            store(lanes, mixture, share + both[:, HEAD_SIZE:], shift)

        def score(group, head, keys_across):
            return dot(query_ref[:, head_of(group, head)], keys_across)

        largest = jnp.zeros((8, HEAD_SIZE), jnp.float32)
        order = [(g, h) for g in range(KEY_VALUE_HEADS) for h in range(GROUP)]
        held, scores, weights = {}, {}, {}
        for turn in range(len(order) + 2):
            if turn < len(order):
                group, head = order[turn]
                soon = order[min(turn + GROUP // 2, len(order) - 1)][0]
                for needed in (group, soon):
                    if needed not in held:
                        held[needed] = keys_and_values(needed)
                scores[turn] = score(group, head, held[group][0])
            if 1 <= turn <= len(order):
                group, head = order[turn - 1]
                if head == 0 and not last:
                    fetch(group, 1).wait()
                    fetch(group, 0).wait()
                weights[turn - 1] = weigh(group, head, scores.pop(turn - 1))
            if turn >= 2:
                group, head = order[turn - 2]
                largest = mix(group, head, weights.pop(turn - 2), held[group][1], largest)
                if (head + 1) % SENT == 0 and last:
                    send((group * GROUP + head) // SENT).start()

        @pl.when(jnp.max(largest) > LARGE_SUM)
        def _():
            @pl.loop(0, KEY_VALUE_HEADS)
            def _(group):
                parts = [group * (GROUP // SENT) + part for part in range(GROUP // SENT)]
                if last:
                    for part in parts:
                        send(part).wait()
                keys_across, value = keys_and_values(group)
                for head in range(GROUP):
                    careful(group, head, score(group, head, keys_across), value)
                if last:
                    for part in parts:
                        send(part).start()

    my_block = lax.axis_index("ctx")
    selected = selected_ref[...]
    chosen = scalar_of(selected, 0, 0), scalar_of(selected, 0, 1)
    first = chosen[0] < my_block
    second = jnp.logical_and(chosen[1] < my_block, chosen[1] != chosen[0])
    valid = first.astype(jnp.int32) + second.astype(jnp.int32)

    @pl.when(valid == 2)
    def _():
        attend((0, 1))

    @pl.when(valid == 1)
    def _():
        attend((second.astype(jnp.int32),))

    @pl.when(valid == 0)
    def _():
        @pl.loop(0, KEY_VALUE_HEADS)
        def _(group):
            lanes = wide(group)
            if last:
                staged[:, lanes] = own_ref[:, lanes].astype(staged.dtype)
                for part in range(GROUP // SENT):
                    send(group * (GROUP // SENT) + part).start()
            else:
                fetch(group, 1).wait()
                fetch(group, 0).wait()
                out_ref[:, lanes] = own_ref[:, lanes]
                for head in range(GROUP):
                    new_level_ref[:, head_of(group, head)] = level_of(group, head)

    if last:

        @pl.loop(0, QUERY_HEADS // SENT)
        def _(part):
            send(part).wait()


def far_attention(selected, queries, own, level, far, last):
    rows = queries.shape[0]
    scores = QUERY_HEADS * rows * 2 * sum(piece.shape[2] for piece in far)
    in_vmem = pl.BlockSpec(memory_space=pltpu.VMEM)
    anywhere = pl.BlockSpec(memory_space=pl.ANY)
    if last:
        earlier = in_vmem
        out_shape = jax.ShapeDtypeStruct(queries.shape, jnp.bfloat16)
        out_specs = anywhere
        scratch = [
            pltpu.VMEM(queries.shape, jnp.bfloat16),
            pltpu.SemaphoreType.DMA((QUERY_HEADS // SENT,)),
        ]
    else:
        earlier = anywhere
        own = pltpu.with_memory_space_constraint(own, pltpu.HBM)
        level = pltpu.with_memory_space_constraint(level, pltpu.HBM)
        out_shape = [jax.ShapeDtypeStruct(queries.shape, jnp.float32)] * 2
        out_specs = [in_vmem] * 2
        scratch = [
            pltpu.VMEM(queries.shape, jnp.float32),
            pltpu.VMEM(level.shape, jnp.float32),
            pltpu.SemaphoreType.DMA((2, KEY_VALUE_HEADS)),
        ]
    return pl.pallas_call(
        functools.partial(far_kernel, last=last),
        out_shape=out_shape,
        in_specs=[
            in_vmem,
            in_vmem,
            earlier,
            earlier,
            *[in_vmem] * len(far),
        ],
        out_specs=out_specs,
        scratch_shapes=scratch,
        compiler_params=pltpu.CompilerParams(vmem_limit_bytes=30 * MIB),
        cost_estimate=pl.CostEstimate(
            flops=4 * scores * HEAD_SIZE, bytes_accessed=10 * MIB, transcendentals=scores
        ),
        name="late_attention" if last else "early_attention",
    )(selected, queries, own, level, *far)


def local(queries, all_key_states, all_value_states, selected):
    devices = lax.axis_size("ctx")
    rows = all_key_states.shape[0]
    piece_rows = rows * COPIES // devices
    packed = pack(all_key_states, all_value_states, devices)
    packed, queries = lax.optimization_barrier((packed, queries))
    held = lax.all_to_all(packed, "ctx", split_axis=0, concat_axis=0, tiled=True)
    own, level = own_attention(queries, all_key_states, all_value_states)
    mine, own, level = lax.optimization_barrier((selected, own, level))
    requests = exchange_requests(mine, devices // COPIES, devices)
    requests = jnp.clip(requests, 0, devices - 1)
    moved = deliver(pick_pieces(requests, held), devices)
    far = [m.reshape(2, SLOTS, piece_rows, HEAD_SIZE) for m in moved]
    early, late = far[: len(far) // 2], far[len(far) // 2 :]
    if piece_rows % 16 != 0:
        early, late = [jnp.concatenate(early, axis=2)], [jnp.concatenate(late, axis=2)]
    own, level = far_attention(selected, queries, own, level, early, last=False)
    return far_attention(selected, queries, own, level, late, last=True)


def solution(mesh):
    placed = P(("groups", "ctx"), None)
    return jax.shard_map(
        local, mesh=mesh, in_specs=(placed,) * 4, out_specs=placed, check_vma=False
    )
```
